32 devices in a mesh: tensor: 4 (over y, x), dp: 2 (over core), seq: 4 (over z).
Axes of the slice: x: 2, y: 2, z: 4, core: 2. Of those that a mesh axis runs over, the one named last changes fastest.
Arguments:
- tokens: bfloat16 [4, 2048, 1792], P('dp', 'seq'), may hold values from -6 to 6
- lengths: int32 [4], P('dp'), may hold values from 1024 to 2048, as said below
- attn_gain: float32 [1792], replicated, may hold values from 0.25 to 1.75
- w_query: bfloat16 [1792, 256], P(None, 'tensor'), may hold values from -0.125 to 0.125
- w_key: bfloat16 [1792, 256], P(None, 'tensor'), may hold values from -0.125 to 0.125
- w_value: bfloat16 [1792, 1792], P(None, 'tensor'), may hold values from -0.125 to 0.125
- w_output: bfloat16 [1792, 1792], P('tensor'), may hold values from -2 to 2
- mlp_gain: float32 [1792], replicated, may hold values from 0.25 to 1.75
- w_gate: bfloat16 [1792, 4864], P(None, 'tensor'), may hold values from -0.125 to 0.125
- w_up: bfloat16 [1792, 4864], P(None, 'tensor'), may hold values from -0.125 to 0.125
- w_down: bfloat16 [4864, 1792], P('tensor'), may hold values from -0.078125 to 0.078125
- cotangent: bfloat16 [4, 2048, 1792], P('dp', 'seq'), may hold values from -6 to 6
Outputs:
- block_out: bfloat16 [4, 2048, 1792], P('dp', 'seq')
- grad_tokens: float32 [4, 2048, 1792], P('dp', 'seq')
- grad_attn_gain: float32 [1792], P(('dp', 'seq'))
- grad_query: float32 [1792, 256], P(('dp', 'seq'), 'tensor')
- grad_key: float32 [1792, 256], P(('dp', 'seq'), 'tensor')
- grad_value: float32 [1792, 1792], P(('dp', 'seq'), 'tensor')
- grad_output: float32 [1792, 1792], P('tensor', ('dp', 'seq'))
- grad_mlp_gain: float32 [1792], P(('dp', 'seq'))
- grad_gate: float32 [1792, 4864], P(('dp', 'seq'), 'tensor')
- grad_up: float32 [1792, 4864], P(('dp', 'seq'), 'tensor')
- grad_down: float32 [4864, 1792], P('tensor', ('dp', 'seq'))
The draws below stay inside these ranges and needn't reach their ends.
Inputs may be any that keep to these rules, and one draw needn't show every extreme that they name: `lengths`: among the 2 consecutive sequences that one index of dp holds, at least one has length 2048.
All inputs are finite; a program needn't handle non-finite values.
Results may differ from the reference program's by a relative error of at most 0.024.
Values may be sent and summed in bfloat16 or wider, within the bound.
A program may use at most 192 MiB of HBM per device.

```python
import math
from functools import partial
import jax
import jax.numpy as jnp
import numpy as np
from jax import lax

D = 1792
H = 16
F = 16
FF = 4864
FEAT = 153
B_DEV = 2
BLOCK = 512
MINLEN = 1024
LMAX = 2048
SEQS = 4
N_TENSOR = 4
N_SEQ = 4


def draw_lengths(key, part):
    key = jax.random.fold_in(key, 7)
    key_lengths, key_slot = jax.random.split(key)
    lengths_raw = jax.random.randint(key_lengths, (SEQS // B_DEV, B_DEV), MINLEN, LMAX + 1)
    chosen_slot = jax.random.randint(key_slot, (SEQS // B_DEV, 1), 0, B_DEV)
    slot_index = jnp.arange(B_DEV)[None, :]
    filled = jnp.where(slot_index == chosen_slot, LMAX, lengths_raw)
    return filled.reshape(SEQS).astype(jnp.int32)


def spiked(array, own_key, source, target, parts, factor):
    owner, partner = [(jnp.arange(array.shape[position]) // (array.shape[position] // parts)).reshape([-1 if axis == position else 1 for axis in range(array.ndim)]) for position in (source, target)]
    chosen = jax.random.permutation(own_key, parts)[partner]
    strong = (owner == chosen) | (owner == (partner + parts // 2) % parts)
    return jnp.where(strong, factor * array, array)


def block_scale(rng, dims, pieces, least, top_value):
    def one(dim, blocks):
        heights = jax.random.uniform(jax.random.fold_in(jax.random.fold_in(rng, 6), dim), (blocks,), jnp.float32, least / len(pieces), top_value / len(pieces))
        return jnp.repeat(jnp.exp(heights), dims[dim] // blocks).reshape((-1,) + (1,) * (len(dims) - dim - 1))

    loudness = one(*pieces[0])
    for cut in pieces[1:]:
        loudness = loudness * one(*cut)
    return loudness


def noise(key, shape, scale, limit, pieces=(), held_as=jnp.bfloat16):
    level = block_scale(key, shape, pieces, -0.22, 0.18) if pieces else 1.0
    values = jax.random.normal(key, shape, jnp.float32) * scale * level
    return jnp.minimum(jnp.maximum(values, -limit), limit).astype(held_as)


def gaussian_with(key, dims, spread, reach, cuts, heavy, kind=jnp.bfloat16):
    array = spread * jax.random.normal(key, dims, jnp.float32)
    if cuts:
        array = array * block_scale(key, dims, cuts, -0.22, 0.18)
    return jnp.clip(spiked(array, jax.random.fold_in(key, 3), *heavy), -reach, reach).astype(kind)


def setup_inputs(seed: int = 0) -> dict:
    seeds = jax.random.split(jax.random.key(seed), 13)
    return {
        "tokens": noise(seeds[0], (SEQS, LMAX, D), 1.0, 6.0, ((0, 2), (1, 4))),
        "lengths": draw_lengths(jax.random.fold_in(seeds[12], 71), 0),
        "attn_gain": jnp.clip(1.0 + 0.15 * jax.random.normal(seeds[2], (D,), jnp.float32), 0.25, 1.75),
        "w_query": noise(seeds[3], (D, H * F), D ** -0.5, 0.125, ((1, 4),)),
        "w_key": noise(seeds[4], (D, H * F), D ** -0.5, 0.125, ((1, 4),)),
        "w_value": noise(seeds[5], (D, D), D ** -0.5, 0.125, ((1, 4),)),
        "w_output": noise(seeds[6], (D, D), (max(D // 256, 1)) ** -0.5, 2.0, ((0, 4),)),
        "mlp_gain": jnp.clip(1.0 + 0.15 * jax.random.normal(seeds[7], (D,), jnp.float32), 0.25, 1.75),
        "w_gate": noise(seeds[8], (D, FF), D ** -0.5, 0.125, ((1, 4),)),
        "w_up": noise(seeds[9], (D, FF), D ** -0.5, 0.125, ((1, 4),)),
        "w_down": noise(seeds[10], (FF, D), FF ** -0.5, 0.078125, ((0, 4),)),
        "cotangent": gaussian_with(seeds[11], (SEQS, LMAX, D), 1.0, 6.0, ((0, 2), (1, 4)), (0, 2, 2, 2.0)),
    }


@jax.custom_vjp
def low(v):
    return lax.optimization_barrier(v.astype(jnp.bfloat16)).astype(jnp.float32)

@jax.custom_vjp
def low_back(v):
    return v

def low_keep(v):
    return (low(v), None)

def low_pass(kept, grad):
    return (grad,)

def back_keep(v):
    return (v, None)

def back_low(kept, grad):
    return (low(grad),)
low.defvjp(low_keep, low_pass)
low_back.defvjp(back_keep, back_low)
HIGHEST_PREC = lax.Precision.HIGHEST

def matmul_high(left_side, right_side):
    return jnp.dot(left_side, right_side, precision=HIGHEST_PREC, preferred_element_type=jnp.float32)

def rms_apply(row_data, gain_vec):
    return row_data * lax.rsqrt(lax.optimization_barrier(jnp.mean(row_data * row_data, axis=-1, keepdims=True)) + 1e-06) * gain_vec

def feature_map(values):
    upper_i, upper_j = np.triu_indices(F)
    pair_scale = np.where(upper_i == upper_j, 1.0 / math.sqrt(2.0 * F), 1.0 / math.sqrt(F)).astype(np.float32)
    constant = jnp.ones(values.shape[:-1] + (1,), values.dtype)
    pair_terms = values[..., upper_i] * values[..., upper_j] * pair_scale
    return jnp.concatenate([constant, values / F ** 0.25, pair_terms], axis=-1)

def attend_block(carried, block_data):
    kv_state, normer = carried
    queries, key_rows, value_rows = block_data
    scores = jnp.einsum('thf,uhf->htu', queries, key_rows, precision=HIGHEST_PREC) / math.sqrt(F)
    block_len = queries.shape[0]
    causal = (jnp.arange(block_len)[:, None] >= jnp.arange(block_len)[None, :]).astype(queries.dtype)
    weights = (1.0 + scores + 0.5 * scores * scores) * causal
    phi_query = feature_map(queries)
    phi_key = feature_map(key_rows)
    numerator = jnp.einsum('htu,uhe->the', weights, value_rows, precision=HIGHEST_PREC)
    numerator = numerator + jnp.einsum('thm,hme->the', phi_query, kv_state, precision=HIGHEST_PREC)
    denominator = lax.optimization_barrier(jnp.sum(weights, axis=-1)).T + jnp.einsum('thm,hm->th', phi_query, normer, precision=HIGHEST_PREC)
    output = numerator / denominator[..., None]
    kv_state = kv_state + jnp.einsum('uhm,uhe->hme', phi_key, value_rows, precision=HIGHEST_PREC)
    normer = normer + lax.optimization_barrier(jnp.sum(phi_key, axis=0))
    return ((kv_state, normer), output)

def attend_sequence(seq_parts):
    queries, key_rows, value_rows = seq_parts
    head_value = D // H
    q_blocks = queries.reshape(N_SEQ, BLOCK, H, F)
    k_blocks = key_rows.reshape(N_SEQ, BLOCK, H, F)
    v_blocks = value_rows.reshape(N_SEQ, BLOCK, H, head_value)
    kv_start = jnp.zeros((H, FEAT, head_value), jnp.float32)
    norm_start = jnp.zeros((H, FEAT), jnp.float32)
    carried, outputs = lax.scan(jax.checkpoint(attend_block), (kv_start, norm_start), (q_blocks, k_blocks, v_blocks))
    return outputs.reshape(LMAX, H, head_value)

def grouped_sum(left_side, right_side):
    groups = N_TENSOR
    group_width = left_side.shape[1] // groups
    left_groups = left_side.reshape(left_side.shape[0], groups, group_width)
    right_groups = right_side.reshape(groups, group_width, right_side.shape[1])
    group_terms = jnp.einsum('ngw,gwe->gne', left_groups, right_groups, precision=HIGHEST_PREC)
    return low_back(lax.optimization_barrier(jnp.sum(low(group_terms), axis=0)))

def layer_forward(token_rows, attn_gain, w_query, w_key, w_value, w_output, mlp_gain, w_gate, w_up, w_down, row_mask):
    normed = low(rms_apply(token_rows, attn_gain))
    queries = low_back(low(matmul_high(normed, w_query)))
    key_rows = low_back(low(matmul_high(normed, w_key)))
    value_rows = low_back(low(matmul_high(normed, w_value)))
    head_value = D // H
    seq_parts = (queries.reshape(SEQS, LMAX, H, F), key_rows.reshape(SEQS, LMAX, H, F), value_rows.reshape(SEQS, LMAX, H, head_value))
    attended = low(lax.map(attend_sequence, seq_parts).reshape(SEQS * LMAX, D))
    residual = token_rows + grouped_sum(attended, w_output)
    normed_mlp = low(rms_apply(residual, mlp_gain))
    gate_proj = low_back(matmul_high(normed_mlp, w_gate))
    up_proj = low_back(matmul_high(normed_mlp, w_up))
    hidden = low(jax.nn.silu(gate_proj) * up_proj)
    return row_mask * (residual + grouped_sum(hidden, w_down))

def reference(tokens, lengths, attn_gain, w_query, w_key, w_value, w_output, mlp_gain, w_gate, w_up, w_down, cotangent):
    token_rows = tokens.astype(jnp.float32).reshape(SEQS * LMAX, D)
    positions = jnp.arange(LMAX, dtype=jnp.int32)
    row_mask = (positions[None, :] < lengths[:, None].astype(jnp.int32)).astype(jnp.float32).reshape(SEQS * LMAX, 1)
    forward = partial(layer_forward, row_mask=row_mask)
    result, pullback = jax.vjp(forward, token_rows, attn_gain.astype(jnp.float32), w_query.astype(jnp.float32), w_key.astype(jnp.float32), w_value.astype(jnp.float32), w_output.astype(jnp.float32), mlp_gain.astype(jnp.float32), w_gate.astype(jnp.float32), w_up.astype(jnp.float32), w_down.astype(jnp.float32))
    grads = pullback(cotangent.astype(jnp.float32).reshape(SEQS * LMAX, D))
    return (result.reshape(SEQS, LMAX, D).astype(jnp.bfloat16), grads[0].reshape(SEQS, LMAX, D), grads[1], grads[2], grads[3], grads[4], grads[5], grads[6], grads[7], grads[8], grads[9])
```

```python
import functools
import math

import jax
import jax.numpy as jnp
import numpy as np
from jax import lax
from jax.experimental import pallas as pl
from jax.experimental.pallas import tpu as pltpu
from jax.sharding import PartitionSpec as P

F = 16
FEATS = 160
LANES = 128
WIDE = 256
VMEM_LIMIT = 62 << 20
MESH = pl.DeviceIdType.MESH
BF16 = jnp.bfloat16
F32 = jnp.float32
VMEM_SPEC = pl.BlockSpec(memory_space=pltpu.VMEM)
ANY_SPEC = pl.BlockSpec(memory_space=pl.ANY)
NN = (((1,), (0,)), ((), ()))
NT = (((1,), (1,)), ((), ()))
TN = (((0,), (0,)), ((), ()))


def dot(a, b, dims=NN):
    return lax.dot_general(a, b, dims, preferred_element_type=F32)


def feature_tables(heads):
    upper_i, upper_j = np.triu_indices(F)
    pairs = len(upper_i)
    first = np.zeros((2 * heads * F, heads * WIDE), np.float32)
    second = np.zeros_like(first)
    rows = np.zeros((8, WIDE), np.float32)
    cols = np.arange(pairs)
    for h in range(heads):
        first[h * F + upper_i, h * WIDE + cols] = 1.0
        second[h * F + upper_j, h * WIDE + cols] = 1.0
        first[h * F + np.arange(F), h * WIDE + pairs + np.arange(F)] = 1.0
    rows[0, pairs + F] = 1.0
    rows[1, pairs : pairs + F + 1] = 1.0
    rows[2, :pairs] = np.where(upper_i == upper_j, 1.0 / (2 * F), 1.0 / F)
    rows[2, pairs : pairs + F] = 1.0 / math.sqrt(F)
    rows[2, pairs + F] = 1.0
    return tuple(jnp.asarray(a, BF16) for a in (first, second)) + (jnp.asarray(rows),)


def spread_table(heads, width):
    table = np.zeros((heads * width, heads * LANES), np.float32)
    for h in range(heads):
        table[h * width + np.arange(width), h * LANES + np.arange(width)] = 1.0
    return jnp.asarray(table, BF16)


class Gather:
    def __init__(self, source, slots, sems, half):
        me = lax.axis_index("tensor")
        self.x, self.y = {"tensor": me ^ 1}, {"tensor": me ^ 2}
        self.source, self.slots, self.sems, self.half = source, slots, sems, half
        self.first = [
            self.copy(source, slots(0), 0, self.x),
            self.copy(source, slots(1), 1, self.y),
        ]
        self.second = [
            self.copy(half(slots(0), 0), half(slots(2), 0), 2, self.y),
            self.copy(half(slots(1), 1), half(slots(2), 1), 3, self.x),
        ]

    def copy(self, src, dst, i, to):
        return pltpu.make_async_remote_copy(
            src, dst, self.sems.at[0, i], self.sems.at[1, i], device_id=to, device_id_type=MESH
        )

    def start(self):
        for c in self.first:
            c.start()

    def forward(self):
        for c, d in zip(self.first, self.second):
            c.wait_recv()
            d.start()

    def finish(self):
        for d in self.second:
            d.wait_recv()
        for c in self.first + self.second:
            c.wait_send()


def greet(devices):
    barrier = pltpu.get_barrier_semaphore()
    for d in devices:
        pl.semaphore_signal(barrier, inc=1, device_id=d, device_id_type=MESH)
    pl.semaphore_wait(barrier, len(devices))


def features(rows, first, second, table, scaled):
    a = dot(rows, first) + table[0:1]
    b = dot(rows, second) + table[1:2]
    out = a * b
    return out * table[2:3] if scaled else out


def head_of(rows, h):
    lane = lax.broadcasted_iota(jnp.int32, rows.shape, 1)
    return jnp.where(lane // F == h, rows, jnp.zeros_like(rows))


def attention_forward(
    nz,
    x_ref,
    gain_ref,
    wqk_ref,
    wv_ref,
    wo_ref,
    spread_ref,
    e1_ref,
    e2_ref,
    table_ref,
    qk_ref,
    kq_ref,
    v_ref,
    yx_ref,
    y_ref,
    pre_ref,
    yall_ref,
    woall_ref,
    sloc,
    pout,
    gsems,
    wsems,
    csems,
    zsems,
):
    seqs, block, width = x_ref.shape
    heads = wqk_ref.shape[0] // (2 * F)
    value = wv_ref.shape[0] // heads
    z = lax.axis_index("seq")
    t = lax.axis_index("tensor")
    core = lax.axis_index("dp")
    side = lax.rem(core, 2)
    mate = {"dp": core + 1 - 2 * side}
    up, down = {"seq": lax.rem(z + 1, nz)}, {"seq": lax.rem(z + nz - 1, nz)}
    greet([{"tensor": t ^ 1}, {"tensor": t ^ 2}, mate, up, down])

    wrows = wo_ref.shape[0] // 2
    mine = pl.ds(pl.multiple_of(side * wrows, 16), wrows)
    wo = Gather(
        wo_ref.at[mine],
        lambda s: woall_ref.at[s, mine],
        wsems,
        lambda ref, i: ref.at[pl.ds(i * (wrows // 2), wrows // 2)],
    )
    wo.start()
    swaps = [
        pltpu.make_async_remote_copy(
            woall_ref.at[s, mine],
            woall_ref.at[s, mine],
            csems.at[0, s],
            csems.at[1, s],
            device_id=mate,
            device_id_type=MESH,
        )
        for s in range(3)
    ]
    table = table_ref[...]
    ones = jnp.where(
        lax.rem(lax.broadcasted_iota(jnp.int32, (1, heads * LANES), 1), LANES) == value, 1.0, 0.0
    )
    tile = block // 2

    def project(b, i):
        at = pl.ds(i * tile, tile)
        flat = pl.ds(b * block + i * tile, tile)
        rows = x_ref[b, at].astype(F32)
        normed = rows * lax.rsqrt(jnp.mean(rows * rows, axis=-1, keepdims=True) + 1e-06)
        normed = (normed * gain_ref[...]).astype(BF16)
        qk = dot(normed, wqk_ref[...], NT)
        qk_ref[flat] = qk.astype(BF16)
        kq_ref[flat] = pltpu.roll(qk, heads * F, 1).astype(BF16)
        values = dot(normed, wv_ref[...], NT).astype(BF16)
        v_ref[flat] = (dot(values, spread_ref[...]) + ones).astype(BF16)

    def lanes(h, n):
        return pl.ds(h * n, n)

    def states(b):
        flat = pl.ds(b * block, block)
        for h in range(heads):
            wide = lanes(h, WIDE)
            phi = features(kq_ref[flat], e1_ref[:, wide], e2_ref[:, wide], table, False)
            s = dot(phi.astype(BF16), v_ref[flat, lanes(h, LANES)], TN)
            sloc[b * heads + h] = s[:FEATS]

    def send_up(j):
        return pltpu.make_async_remote_copy(
            pout.at[j],
            pre_ref.at[j],
            zsems.at[0, j],
            zsems.at[1, j],
            device_id=up,
            device_id_type=MESH,
        )

    def chain(b, who):
        for at in who:

            @pl.when(z == at)
            def _():
                for h in range(heads):
                    j = b * heads + h
                    if at == 0:
                        pre_ref[j] = jnp.zeros((FEATS, LANES), BF16)
                        pout[j] = sloc[j].astype(BF16)
                    else:
                        send_up(j).wait_recv()
                        if at < nz - 1:
                            pout[j] = (sloc[j] + pre_ref[j].astype(F32)).astype(BF16)
                    if at < nz - 1:
                        send_up(j).start()

    def attend(b, h):
        narrow = lanes(h, LANES)
        wide = lanes(h, WIDE)
        for i in range(2):
            span = (i + 1) * tile
            at = pl.ds(b * block + i * tile, tile)
            until = pl.ds(b * block, span)
            rows = qk_ref[at]
            s = dot(head_of(rows, h), kq_ref[until], NT)
            w = 1.0 + s * (1.0 / math.sqrt(F))
            w = 0.5 * (w * w) + 0.5
            row = lax.broadcasted_iota(jnp.int32, w.shape, 0) + i * tile
            col = lax.broadcasted_iota(jnp.int32, w.shape, 1)
            w = jnp.where(col <= row, w, 0.0).astype(BF16)
            num = dot(w, v_ref[until, narrow])
            phi = features(rows, e1_ref[:, wide], e2_ref[:, wide], table, True)
            num = num + dot(phi[:, :FEATS].astype(BF16), pre_ref[b * heads + h])
            recip = 1.0 / num[:, value : value + 1]
            lane = lax.broadcasted_iota(jnp.int32, num.shape, 1)
            yx_ref[at, narrow] = jnp.where(lane == value, recip, num * recip)

    def gather(b):
        flat = pl.ds(b * block, block)
        return Gather(
            y_ref.at[flat],
            lambda s: yall_ref.at[s, flat],
            gsems.at[b],
            lambda ref, i: ref.at[pl.ds(i * tile, tile)],
        )

    def pack(b):
        for i in range(2):
            at = pl.ds(b * block + i * tile, tile)
            y_ref[at] = dot(yx_ref[at].astype(BF16), spread_ref[...], NT).astype(BF16)

    gathers = [gather(b) for b in range(seqs)]
    mid = list(range(1, nz - 1))
    for b in range(seqs + 1):
        if b < seqs:
            for i in range(2):
                project(b, i)
                if b > 0 and i == 0:
                    chain(b - 1, mid[:1])
            if b > 0:
                chain(b - 1, mid[1:])
            states(b)
            chain(b, [0])
        if b > 0:
            chain(b - 1, [nz - 1])
            for h in range(heads):
                attend(b - 1, h)
                if b == seqs - 1:
                    chain(b, mid[h : h + 1] if h < heads - 1 else mid[h:])
            pack(b - 1)
            gathers[b - 1].start()
    wo.forward()
    for s in range(2):
        swaps[s].start()
    for g in gathers:
        g.forward()
    wo.finish()
    swaps[2].start()
    for g in gathers:
        g.finish()
    for s in swaps:
        s.wait()

    @pl.when(z < nz - 1)
    def _():
        for j in range(seqs * heads):
            send_up(j).wait_send()


def run_attention_forward(x, gain, wqk, wv, wo, tables):
    seqs, block, width = x.shape
    heads = wqk.shape[0] // (2 * F)
    value = wv.shape[0] // heads
    rows = seqs * block
    spread, e1, e2, table = tables
    shapes = [
        jax.ShapeDtypeStruct((rows, 2 * heads * F), BF16),
        jax.ShapeDtypeStruct((rows, 2 * heads * F), BF16),
        jax.ShapeDtypeStruct((rows, heads * LANES), BF16),
        jax.ShapeDtypeStruct((rows, heads * LANES), F32),
        jax.ShapeDtypeStruct((rows, heads * value), BF16),
        jax.ShapeDtypeStruct((seqs * heads, FEATS, LANES), BF16),
        jax.ShapeDtypeStruct((3, rows, heads * value), BF16),
        jax.ShapeDtypeStruct((3,) + wo.shape, BF16),
    ]
    return pl.pallas_call(
        functools.partial(attention_forward, lax.axis_size("seq")),
        out_shape=shapes,
        in_specs=[VMEM_SPEC] * 9,
        out_specs=[VMEM_SPEC] * 6 + [ANY_SPEC] * 2,
        scratch_shapes=[
            pltpu.VMEM((seqs * heads, FEATS, LANES), F32),
            pltpu.VMEM((seqs * heads, FEATS, LANES), BF16),
            pltpu.SemaphoreType.DMA((seqs, 2, 4)),
            pltpu.SemaphoreType.DMA((2, 4)),
            pltpu.SemaphoreType.DMA((2, 3)),
            pltpu.SemaphoreType.DMA((2, seqs * heads)),
        ],
        compiler_params=pltpu.CompilerParams(
            collective_id=0, has_side_effects=True, vmem_limit_bytes=VMEM_LIMIT
        ),
        cost_estimate=pl.CostEstimate(
            flops=2 * rows * width * heads * (2 * F + value), bytes_accessed=20 << 20, transcendentals=0
        ),
        name="attention_forward",
    )(x, gain.reshape(1, width), wqk, wv, wo, spread, e1, e2, table)


class Exchange:
    def __init__(self, sems):
        me = lax.axis_index("tensor")
        self.x, self.y = {"tensor": me ^ 1}, {"tensor": me ^ 2}
        self.sems = sems

    def copy(self, src, dst, i, to):
        return pltpu.make_async_remote_copy(
            src, dst, self.sems.at[0, i], self.sems.at[1, i], device_id=to, device_id_type=MESH
        )


def rows_at(start, count):
    return pl.ds(pl.multiple_of(start, 16), count)


class ReduceScatter(Exchange):
    def __init__(self, part, near, far, sems):
        super().__init__(sems)
        me = lax.axis_index("tensor")
        self.part, self.near, self.far = part, near, far
        self.q = q = near.shape[1] * 2
        self.half = q // 2
        self.at = [me * q, (me ^ 1) * q, (me ^ 2) * q, (me ^ 3) * q]
        over = self.at[3]
        self.first = [
            self.copy(part.at[rows_at(over, self.half)], near.at[0], 0, self.x),
            self.copy(part.at[rows_at(over + self.half, self.half)], near.at[1], 1, self.y),
        ]
        self.second = [
            self.copy(part.at[rows_at(self.at[2], q)], far.at[1], 2, self.y),
            self.copy(part.at[rows_at(self.at[1], q)], far.at[0], 3, self.x),
        ]

    def start(self):
        for c in self.first:
            c.start()

    def forward(self):
        for i, start in ((0, self.at[2]), (1, self.at[1] + self.half)):
            self.first[i].wait_recv()
            rows = rows_at(start, self.half)
            self.part[rows] = (self.part[rows].astype(F32) + self.near[i].astype(F32)).astype(BF16)
            self.second[i].start()

    def finish(self):
        for c in self.second:
            c.wait_recv()

    def total(self, start, count):
        mine = self.part[rows_at(self.at[0] + start, count)].astype(F32)
        at = pl.ds(start, count)
        return mine + self.far[0, at].astype(F32) + self.far[1, at].astype(F32)

    def drain(self):
        for c in self.first + self.second:
            c.wait_send()


class RowGather(Exchange):
    def __init__(self, source, piece, half, sems):
        super().__init__(sems)
        me = lax.axis_index("tensor")
        self.first = [
            self.copy(source, piece(me), 0, self.x),
            self.copy(source, piece(me), 1, self.y),
        ]
        self.second = [
            self.copy(half(me ^ 1, 0), half(me ^ 1, 0), 2, self.y),
            self.copy(half(me ^ 2, 1), half(me ^ 2, 1), 3, self.x),
        ]

    start = Gather.start
    forward = Gather.forward
    finish = Gather.finish


def norm_backward(rows, grad, gain):
    norm = lax.rsqrt(jnp.mean(rows * rows, axis=-1, keepdims=True) + 1e-06)
    unit = rows * norm
    gain_grad = jnp.sum(grad * unit, axis=0, keepdims=True)
    scaled = grad * gain
    mean = jnp.mean(scaled * unit, axis=-1, keepdims=True)
    return norm * (scaled - unit * mean), gain_grad


def mlp_kernel(
    x_hbm,
    y_hbm,
    yall_hbm,
    wo_hbm,
    woall_hbm,
    wg_hbm,
    wu_hbm,
    wd_hbm,
    cot_hbm,
    gain_ref,
    len_ref,
    hidden_ref,
    r_ref,
    gr_ref,
    gain_grad_ref,
    gattn_hbm,
    gsum_hbm,
    land_hbm,
    wo4,
    wg,
    wu,
    wd,
    xt,
    yt,
    ct,
    h2t,
    gmt,
    gg,
    gu,
    part,
    near,
    far,
    ga,
    stage,
    back,
    lsems,
    rsems,
    asems,
    msems,
    bsems,
):
    seqs, block, width = x_hbm.shape
    tile = xt.shape[0]
    per = block // tile
    quarter = block // 4
    tiles = seqs * per
    ff = wg.shape[0]
    z = lax.axis_index("seq")
    t = lax.axis_index("tensor")
    core = lax.axis_index("dp")
    side = lax.rem(core, 2)
    mate = {"dp": core + 1 - 2 * side}
    greet([{"tensor": t ^ 1}, {"tensor": t ^ 2}, mate])
    gain = gain_ref[...]

    def load(src, dst, i):
        return pltpu.make_async_copy(src, dst, lsems.at[i])

    weights = [
        load(wo_hbm, wo4.at[0], 0),
        *[load(woall_hbm.at[s], wo4.at[s + 1], 1 + s) for s in range(3)],
        load(wg_hbm, wg, 4),
        load(wu_hbm, wu, 5),
        load(wd_hbm, wd, 6),
    ]

    def xy_loads(i):
        b, at = i // per, lax.rem(i, per) * tile
        flat = rows_at(i * tile, tile)
        return [
            load(x_hbm.at[b, rows_at(at, tile)], xt, 7),
            load(y_hbm.at[flat], yt.at[0], 8),
            *[load(yall_hbm.at[s, flat], yt.at[s + 1], 9 + s) for s in range(3)],
        ]

    def c_load(i):
        b, at = i // per, lax.rem(i, per) * tile
        return load(cot_hbm.at[b, rows_at(at, tile)], ct, 12)

    for c in xy_loads(0):
        c.start()
    for c in weights[:4]:
        c.start()
    for c in weights[4:6]:
        c.start()
    c_load(0).start()
    weights[6].start()
    quarters = [
        load(cot_hbm.at[b, rows_at(t * quarter, quarter)], ct.at[pl.ds(b * quarter, quarter)], 13 + b)
        for b in range(seqs)
    ]

    def mask(b, start, count):
        at = z * block + start + lax.broadcasted_iota(jnp.int32, (count, 1), 0)
        return (at < len_ref[b]).astype(F32)

    scatters = [
        ReduceScatter(part.at[pl.ds(b * block, block)], near.at[b], far.at[b], rsems.at[b])
        for b in range(seqs)
    ]
    gathers = []
    for b in range(seqs):

        def piece(i, b=b):
            return gattn_hbm.at[rows_at(b * block + i * quarter, quarter)]

        def half(i, h, b=b):
            return gattn_hbm.at[rows_at(b * block + i * quarter + h * (quarter // 2), quarter // 2)]

        gathers.append(RowGather(ga.at[b], piece, half, asems.at[b]))
    own_rows = [
        pltpu.make_async_copy(
            ga.at[b], gattn_hbm.at[rows_at(b * block + t * quarter, quarter)], bsems.at[b]
        )
        for b in range(seqs)
    ]

    def tile_step(i, first):
        b = i // per
        local = lax.rem(i, per)
        flat = rows_at(i * tile, tile)
        for c in xy_loads(i):
            c.wait()
        if first:
            for c in weights[:4]:
                c.wait()
        r = xt[...].astype(F32)
        for s in range(4):
            r = r + dot(yt[s], wo4[s])

        @pl.when(i + 1 < tiles)
        def _():
            for c in xy_loads(i + 1):
                c.start()

        @pl.when(t // 2 == local)
        def _():
            r_ref[b] = jnp.where(lax.rem(t, 2) == 0, r[:quarter], r[quarter:])

        h2 = r * lax.rsqrt(jnp.mean(r * r, axis=-1, keepdims=True) + 1e-06) * gain
        h2 = h2.astype(BF16)
        cols = pl.ds(pl.multiple_of(i * tile, LANES), tile)
        h2t[:, cols] = h2.T
        if first:
            for c in weights[4:6]:
                c.wait()
        gate = dot(h2, wg[...], NT)
        up = dot(h2, wu[...], NT)
        c_load(i).wait()
        gm = (ct[...].astype(F32) * mask(b, local * tile, tile)).astype(BF16)
        gmt[:, cols] = gm.T
        if first:
            weights[6].wait()
        gh = dot(gm, wd[...], NT)

        @pl.when(i + 1 < tiles)
        def _():
            c_load(i + 1).start()

        sig = 1.0 / (1.0 + jnp.exp(-gate))
        silu = gate * sig
        hidden_ref[flat] = (silu * up).astype(BF16)
        gg[flat] = (gh * up * (sig * (1.0 + gate * (1.0 - sig)))).astype(BF16)
        gu[flat] = (gh * silu).astype(BF16)
        part[flat] = (dot(gg[flat], wg[...]) + dot(gu[flat], wu[...])).astype(BF16)

    tile_step(0, True)

    def rest(i, carry):
        tile_step(i, False)
        for b in range(seqs):

            @pl.when(i == (b + 1) * per - 1)
            def _():
                scatters[b].start()

            if b < seqs - 1:

                @pl.when(i == (b + 1) * per)
                def _():
                    scatters[b].forward()

        return carry

    lax.fori_loop(1, tiles, rest, 0)
    for c in quarters:
        c.start()

    def mixed(b):
        scatters[b].finish()
        quarters[b].wait()
        grad = scatters[b].total(0, quarter)
        out = ct[pl.ds(b * quarter, quarter)].astype(F32) * mask(b, t * quarter, quarter)
        gr, gain_grad = norm_backward(r_ref[b], grad, gain)
        gr = gr + out
        gr_ref[b] = gr
        ga[b] = gr.astype(BF16)
        if b == 0:
            gain_grad_ref[...] = gain_grad
        else:
            gain_grad_ref[...] += gain_grad
        gathers[b].start()
        own_rows[b].start()

    mixed(0)
    lefts = (h2t, h2t, gmt)
    rights = (gg, gu, hidden_ref)
    half_rows = width // 2
    piece_rows = stage.shape[1]
    pieces = half_rows // piece_rows

    def product(base, n, m):
        return dot(lefts[n][rows_at(base + m * piece_rows, piece_rows)], rights[n][...])

    def to_mate(n, m):
        slot = (n * pieces + m) % 2
        return pltpu.make_async_remote_copy(
            stage.at[slot],
            land_hbm.at[n, rows_at(m * piece_rows, piece_rows)],
            msems.at[0, slot],
            msems.at[1, n * pieces + m],
            device_id=mate,
            device_id_type=MESH,
        )

    def from_mate(n, m):
        return pltpu.make_async_copy(
            land_hbm.at[n, rows_at(m * piece_rows, piece_rows)], back, bsems.at[2]
        )

    def to_sum(n, m):
        slot = (n * pieces + m) % 2
        return pltpu.make_async_copy(
            stage.at[slot], gsum_hbm.at[n, rows_at(m * piece_rows, piece_rows)], bsems.at[3 + slot]
        )

    work = [(n, m) for n in range(3) for m in range(pieces)]
    steps = [lambda: scatters[1].forward(), lambda: gathers[0].forward(), None, lambda: mixed(1)]
    for k, (n, m) in enumerate(work):
        out = product((1 - side) * half_rows, n, m)
        if k >= 2:
            to_mate(*work[k - 2]).wait_send()
        stage[k % 2] = out.astype(BF16)
        to_mate(n, m).start()
        if k < len(steps) and steps[k] is not None:
            steps[k]()
    for k in (len(work) - 2, len(work) - 1):
        to_mate(*work[k]).wait_send()
    for k, (n, m) in enumerate(work):
        to_mate(n, m).wait_recv()
        from_mate(n, m).start()
        out = product(side * half_rows, n, m)
        from_mate(n, m).wait()
        out = out + back[...].astype(F32)
        if k >= 2:
            to_sum(*work[k - 2]).wait()
        stage[k % 2] = out.astype(BF16)
        to_sum(n, m).start()
    for k in (len(work) - 2, len(work) - 1):
        to_sum(*work[k]).wait()
    gathers[1].forward()
    for b in range(seqs):
        own_rows[b].wait()
        gathers[b].finish()
        scatters[b].drain()


def run_mlp(x, y, yall, wo, woall, wg, wu, wd, cot, gain, lengths):
    seqs, block, width = x.shape
    rows = seqs * block
    value, ff = wo.shape[0], wg.shape[1]
    tile, quarter = block // 2, block // 4
    piece_rows = width // 8
    shapes = [
        jax.ShapeDtypeStruct((rows, ff), BF16),
        jax.ShapeDtypeStruct((seqs, quarter, width), F32),
        jax.ShapeDtypeStruct((seqs, quarter, width), F32),
        jax.ShapeDtypeStruct((1, width), F32),
        jax.ShapeDtypeStruct((rows, width), BF16),
        jax.ShapeDtypeStruct((3, width // 2, ff), BF16),
        jax.ShapeDtypeStruct((3, width // 2, ff), BF16),
    ]
    vm = pltpu.VMEM
    scratch = [
        vm((4, value, width), BF16),
        vm((ff, width), BF16),
        vm((ff, width), BF16),
        vm((ff, width), BF16),
        vm((tile, width), BF16),
        vm((4, tile, value), BF16),
        vm((tile, width), BF16),
        vm((width, rows), BF16),
        vm((width, rows), BF16),
        vm((rows, ff), BF16),
        vm((rows, ff), BF16),
        vm((rows, width), BF16),
        vm((seqs, 2, quarter // 2, width), BF16),
        vm((seqs, 2, quarter, width), BF16),
        vm((seqs, quarter, width), BF16),
        vm((2, piece_rows, ff), BF16),
        vm((piece_rows, ff), BF16),
        pltpu.SemaphoreType.DMA((15,)),
        pltpu.SemaphoreType.DMA((seqs, 2, 4)),
        pltpu.SemaphoreType.DMA((seqs, 2, 4)),
        pltpu.SemaphoreType.DMA((2, 12)),
        pltpu.SemaphoreType.DMA((5,)),
    ]
    return pl.pallas_call(
        mlp_kernel,
        out_shape=shapes,
        in_specs=[ANY_SPEC] * 9 + [VMEM_SPEC, pl.BlockSpec(memory_space=pltpu.SMEM)],
        out_specs=[VMEM_SPEC] * 4 + [ANY_SPEC] * 3,
        scratch_shapes=scratch,
        compiler_params=pltpu.CompilerParams(
            collective_id=1, has_side_effects=True, vmem_limit_bytes=VMEM_LIMIT
        ),
        cost_estimate=pl.CostEstimate(
            flops=2 * rows * width * (4 * value + 8 * ff), bytes_accessed=60 << 20, transcendentals=0
        ),
        name="mlp_forward_backward",
    )(x, y, yall, wo, woall, wg.T, wu.T, wd, cot, gain.reshape(1, width), lengths)


def attention_backward(
    nz,
    x_hbm,
    gain_ref,
    qk_ref,
    kq_ref,
    v_ref,
    yx_ref,
    pre_ref,
    gattn_ref,
    wo_ref,
    wqk_ref,
    wv_ref,
    gr_ref,
    gains_ref,
    spread_ref,
    e1_ref,
    e2_ref,
    f1_ref,
    f2_ref,
    table_ref,
    grads_ref,
    gains_out,
    gt_hbm,
    gn,
    gv,
    gvb,
    gqk,
    gqkb,
    yb,
    gat,
    h1t,
    sloc,
    sout,
    suf,
    xt,
    xq,
    part,
    near,
    far,
    gq,
    stage,
    land,
    total,
    zland,
    gsend,
    gland,
    lsems,
    zsems,
    rsems,
    asems,
    msems,
    dsems,
    ksems,
):
    seqs, block, width = x_hbm.shape
    heads = wqk_ref.shape[0] // (2 * F)
    value = wv_ref.shape[0] // heads
    tile, quarter = block // 2, block // 4
    rows = seqs * block
    z = lax.axis_index("seq")
    t = lax.axis_index("tensor")
    core = lax.axis_index("dp")
    side = lax.rem(core, 2)
    mate = {"dp": core + 1 - 2 * side}
    others = [{"seq": lax.rem(z + k, nz)} for k in range(1, nz)]
    greet([{"tensor": t ^ 1}, {"tensor": t ^ 2}, mate] + others)
    down = others[-1]
    gain = gain_ref[...]
    table = table_ref[...]
    scale = table[2:3, :FEATS]

    def lanes(h, n):
        return pl.ds(h * n, n)

    def x_load(i):
        b, at = i // 2, (i % 2) * tile
        return pltpu.make_async_copy(x_hbm.at[b, pl.ds(at, tile)], xt.at[i % 2], lsems.at[i % 2])

    quarters = [
        pltpu.make_async_copy(
            x_hbm.at[b, rows_at(t * quarter, quarter)], xq.at[b], lsems.at[2 + b]
        )
        for b in range(seqs)
    ]
    x_load(0).start()
    x_load(1).start()
    for c in quarters:
        c.start()

    def value_grads(i):
        at = pl.ds(i * tile, tile)
        ga = gattn_ref[at]
        gy = dot(dot(ga, wo_ref[...], NT).astype(BF16), spread_ref[...])
        gat[:, pl.ds(i * tile, tile)] = ga.T
        yb[at] = yx_ref[at].astype(BF16)
        for h in range(heads):
            narrow = lanes(h, LANES)
            g, y = gy[:, h * LANES : (h + 1) * LANES], yx_ref[at, narrow]
            recip = y[:, value : value + 1]
            den = -jnp.sum(g * y, axis=-1, keepdims=True)
            lane = lax.broadcasted_iota(jnp.int32, g.shape, 1)
            gn[at, narrow] = (jnp.where(lane == value, den, g) * recip).astype(BF16)

    def expand(ref, at, h):
        a = dot(ref[at], e1_ref[:, h * WIDE : h * WIDE + FEATS]) + table[0:1, :FEATS]
        b = dot(ref[at], e2_ref[:, h * WIDE : h * WIDE + FEATS]) + table[1:2, :FEATS]
        return a, b

    def states(b):
        flat = pl.ds(b * block, block)
        for h in range(heads):
            a, c = expand(qk_ref, flat, h)
            phi = (a * c * scale).astype(BF16)
            sloc[b * heads + h] = dot(phi, gn[flat, lanes(h, LANES)], TN)

    def send_down(j):
        return pltpu.make_async_remote_copy(
            sout.at[j], suf.at[j], zsems.at[0, j], zsems.at[1, j], device_id=down, device_id_type=MESH
        )

    def chain(b, who):
        for at in who:

            @pl.when(z == nz - 1 - at)
            def _():
                for h in range(heads):
                    j = b * heads + h
                    if at == 0:
                        suf[j] = jnp.zeros((FEATS, LANES), BF16)
                        sout[j] = sloc[j].astype(BF16)
                    else:
                        send_down(j).wait_recv()
                        if at < nz - 1:
                            sout[j] = (sloc[j] + suf[j].astype(F32)).astype(BF16)
                    if at < nz - 1:
                        send_down(j).start()

    def contract(a, c, grad, h, first, second):
        wide = slice(h * WIDE, h * WIDE + FEATS)
        return dot((grad * c).astype(BF16), first[:, wide], NT) + dot(
            (grad * a).astype(BF16), second[:, wide], NT
        )

    def local(b, h):
        narrow = lanes(h, LANES)
        for i in range(2):
            span = (i + 1) * tile
            at = pl.ds(b * block + i * tile, tile)
            until = pl.ds(b * block, span)
            s = dot(head_of(qk_ref[at], h), kq_ref[until], NT)
            w = 1.0 + s * (1.0 / math.sqrt(F))
            row = lax.broadcasted_iota(jnp.int32, w.shape, 0) + i * tile
            col = lax.broadcasted_iota(jnp.int32, w.shape, 1)
            seen = col <= row
            kernel = jnp.where(seen, 0.5 * (w * w) + 0.5, 0.0).astype(BF16)
            grad = gn[at, narrow]
            gs = dot(grad, v_ref[until, narrow], NT) * (w * (1.0 / math.sqrt(F)))
            gs = jnp.where(seen, gs, 0.0).astype(BF16)
            gv[until, narrow] += dot(kernel, grad, TN)
            gqk[until] += dot(gs, head_of(kq_ref[at], heads + h), TN)
            a, c = expand(qk_ref, at, h)
            gphi = dot(grad, pre_ref[b * heads + h], NT) * scale
            gqk[at] += dot(gs, head_of(kq_ref[until], h)) + contract(a, c, gphi, h, e1_ref, e2_ref)

    def state_grads(b, h):
        narrow = lanes(h, LANES)
        flat = pl.ds(b * block, block)
        later = suf[b * heads + h]
        a, c = expand(kq_ref, flat, h)
        gphi = dot(v_ref[flat, narrow], later, NT)
        gqk[flat] += contract(a, c, gphi, h, f1_ref, f2_ref)
        gv[flat, narrow] += dot((a * c).astype(BF16), later)

    def norm_grads(b):
        for i in range(2):
            at = pl.ds(b * block + i * tile, tile)
            gvb[at] = gv[at].astype(BF16)
            gqkb[at] = gqk[at].astype(BF16)
            packed = dot(gvb[at], spread_ref[...], NT).astype(BF16)
            part[at] = (dot(gqkb[at], wqk_ref[...]) + dot(packed, wv_ref[...])).astype(BF16)

    def normed_rows(i):
        x_load(i).wait()
        r = xt[i % 2].astype(F32)
        h1 = r * lax.rsqrt(jnp.mean(r * r, axis=-1, keepdims=True) + 1e-06) * gain
        h1t[:, pl.ds(i * tile, tile)] = h1.astype(BF16).T
        if i + 2 < 2 * seqs:
            x_load(i + 2).start()

    scatters = [
        ReduceScatter(part.at[pl.ds(b * block, block)], near.at[b], far.at[b], rsems.at[b])
        for b in range(seqs)
    ]
    gathers = []
    for b in range(seqs):

        def piece(i, b=b):
            return gt_hbm.at[b, rows_at(i * quarter, quarter)]

        def half(i, h, b=b):
            return gt_hbm.at[b, rows_at(i * quarter + h * (quarter // 2), quarter // 2)]

        gathers.append(RowGather(gq.at[b], piece, half, asems.at[b]))
    own_rows = [
        pltpu.make_async_copy(gq.at[b], gt_hbm.at[b, rows_at(t * quarter, quarter)], lsems.at[4 + b])
        for b in range(seqs)
    ]

    half_rows = width // 2
    chunk = half_rows // nz
    spans = [pl.ds(0, heads * LANES), pl.ds(heads * LANES, 2 * heads * F + heads * LANES)]

    def product(p, base):
        at = rows_at(base, half_rows)
        if p == 0:
            return dot(gat[at], yb[...])
        return jnp.concatenate([dot(h1t[at], gqkb[...]), dot(h1t[at], gvb[...])], axis=1)

    def to_mate(p):
        return pltpu.make_async_remote_copy(
            stage.at[:, spans[p]],
            land.at[:, spans[p]],
            msems.at[0, p],
            msems.at[1, p],
            device_id=mate,
            device_id_type=MESH,
        )

    def to_chunks(p):
        return [
            pltpu.make_async_remote_copy(
                total.at[rows_at(lax.rem(z + k, nz) * chunk, chunk), spans[p]],
                zland.at[k - 1, :, spans[p]],
                dsems.at[0, p, k - 1],
                dsems.at[1, p, k - 1],
                device_id=others[k - 1],
                device_id_type=MESH,
            )
            for k in range(1, nz)
        ]

    def send_half(p):
        stage[:, spans[p]] = product(p, (1 - side) * half_rows).astype(BF16)
        to_mate(p).start()

    def sum_half(p):
        out = product(p, side * half_rows)
        to_mate(p).wait_recv()
        total[:, spans[p]] = (out + land[:, spans[p]].astype(F32)).astype(BF16)
        for c in to_chunks(p):
            c.start()

    def tokens(b):
        scatters[b].finish()
        quarters[b].wait()
        grad, gain_grad = norm_backward(
            xq[b].astype(F32), scatters[b].total(0, quarter), gain
        )
        gq[b] = (grad + gr_ref[b]).astype(BF16)
        gathers[b].start()
        own_rows[b].start()
        if b == 0:
            gsend[0] = jnp.concatenate(
                [gain_grad, gains_ref[...], jnp.zeros((6, width), F32)], axis=0
            )
        else:
            gsend[0, 0:1] += gain_grad

    gv[...] = jnp.zeros_like(gv)
    gqk[...] = jnp.zeros_like(gqk)
    mid = list(range(1, nz - 1))
    value_grads(0)
    value_grads(1)
    states(0)
    chain(0, [0])
    for b in range(1, seqs):
        value_grads(2 * b)
        chain(b - 1, mid[:1])
        value_grads(2 * b + 1)
        states(b)
        chain(b - 1, mid[1:])
        chain(b, [0])
    for b in range(seqs):
        for h in range(heads):
            local(b, h)
            if b == 0:
                chain(1, mid[h : h + 1] if h < heads - 1 else mid[h:])
        chain(b, [nz - 1])
        if b > 0:
            scatters[b - 1].forward()
        for h in range(heads):
            state_grads(b, h)
        norm_grads(b)
        scatters[b].start()
    send_half(0)
    tokens(0)
    for i in range(2 * seqs):
        normed_rows(i)
    scatters[1].forward()
    send_half(1)
    gathers[0].forward()
    sum_half(0)
    tokens(1)
    sum_half(1)

    hops = [{"tensor": t ^ 1}, {"tensor": t ^ 2}, mate]
    for i, to in enumerate(hops):
        c = pltpu.make_async_remote_copy(
            gsend.at[i], gland.at[i], ksems.at[0, i], ksems.at[1, i], device_id=to, device_id_type=MESH
        )
        c.start()
        c.wait()
        gsend[i + 1] = gsend[i] + gland[i]
    last = len(hops)
    copies = [
        pltpu.make_async_remote_copy(
            gsend.at[last],
            gland.at[last + k],
            ksems.at[0, last + k],
            ksems.at[1, last + k],
            device_id=others[k],
            device_id_type=MESH,
        )
        for k in range(nz - 1)
    ]
    for c in copies:
        c.start()
    gathers[1].forward()
    for p in range(2):
        for c in to_chunks(p):
            c.wait()
        out = total[rows_at(z * chunk, chunk), spans[p]].astype(F32)
        for k in range(nz - 1):
            out = out + zland[k, :, spans[p]].astype(F32)
        grads_ref[:, spans[p]] = out
        to_mate(p).wait_send()
    gains = gsend[last]
    for k, c in enumerate(copies):
        c.wait()
        gains = gains + gland[last + k]
    gains_out[...] = gains
    for b in range(seqs):
        own_rows[b].wait()
        gathers[b].finish()
        scatters[b].drain()

    @pl.when(z > 0)
    def _():
        for j in range(seqs * heads):
            send_down(j).wait_send()


def run_attention_backward(
    x, gain, qk, kq, v_ext, yx, pre, gattn, wo, wqk, wv, gr, gains, tables
):
    seqs, block, width = x.shape
    rows = seqs * block
    heads = wqk.shape[0] // (2 * F)
    quarter, tile = block // 4, block // 2
    nz = lax.axis_size("seq")
    spread, e1, e2, table = tables
    half = heads * F
    f1, f2 = jnp.roll(e1, half, 0), jnp.roll(e2, half, 0)
    chunk = width // 2 // nz
    cols = 2 * heads * LANES + 2 * heads * F
    shapes = [
        jax.ShapeDtypeStruct((chunk, cols), F32),
        jax.ShapeDtypeStruct((8, width), F32),
        jax.ShapeDtypeStruct(x.shape, BF16),
    ]
    vm, dma = pltpu.VMEM, pltpu.SemaphoreType.DMA
    wide = heads * LANES
    scratch = [
        vm((rows, wide), BF16),
        vm((rows, wide), F32),
        vm((rows, wide), BF16),
        vm((rows, 2 * half), F32),
        vm((rows, 2 * half), BF16),
        vm((rows, wide), BF16),
        vm((width, rows), BF16),
        vm((width, rows), BF16),
        vm((seqs * heads, FEATS, LANES), F32),
        vm((seqs * heads, FEATS, LANES), BF16),
        vm((seqs * heads, FEATS, LANES), BF16),
        vm((2, tile, width), BF16),
        vm((seqs, quarter, width), BF16),
        vm((rows, width), BF16),
        vm((seqs, 2, quarter // 2, width), BF16),
        vm((seqs, 2, quarter, width), BF16),
        vm((seqs, quarter, width), BF16),
        vm((width // 2, cols), BF16),
        vm((width // 2, cols), BF16),
        vm((width // 2, cols), BF16),
        vm((nz - 1, chunk, cols), BF16),
        vm((4, 8, width), F32),
        vm((3 + nz - 1, 8, width), F32),
        dma((4 + seqs,)),
        dma((2, seqs * heads)),
        dma((seqs, 2, 4)),
        dma((seqs, 2, 4)),
        dma((2, 2)),
        dma((2, 2, nz - 1)),
        dma((2, 3 + nz - 1)),
    ]
    return pl.pallas_call(
        functools.partial(attention_backward, nz),
        out_shape=shapes,
        in_specs=[ANY_SPEC] + [VMEM_SPEC] * 18,
        out_specs=[VMEM_SPEC] * 2 + [ANY_SPEC],
        scratch_shapes=scratch,
        compiler_params=pltpu.CompilerParams(
            collective_id=2, has_side_effects=True, vmem_limit_bytes=VMEM_LIMIT
        ),
        cost_estimate=pl.CostEstimate(
            flops=8 * rows * width * wide, bytes_accessed=30 << 20, transcendentals=0
        ),
        name="attention_backward",
    )(x, gain.reshape(1, width), qk, kq, v_ext, yx, pre, gattn, wo, wqk, wv, gr, gains, spread, e1, e2, f1, f2, table)


def shards(
    tokens,
    lengths,
    attn_gain,
    w_query,
    w_key,
    w_value,
    w_output,
    mlp_gain,
    w_gate,
    w_up,
    w_down,
    cotangent,
):
    seqs, block, width = tokens.shape
    heads = w_query.shape[1] // F
    value = w_value.shape[1] // heads
    quarter = block // 4
    chips = lax.axis_size("dp") // 2
    t = lax.axis_index("tensor")
    tables = (spread_table(heads, value),) + feature_tables(heads)
    wqk = jnp.concatenate([w_query.T, w_key.T], axis=0)
    wv = w_value.T
    qk, kq, v_ext, yx, y, pre, yall, woall = run_attention_forward(
        tokens, attn_gain, wqk, wv, w_output, tables
    )
    hidden, r_own, gr_own, mlp_gain_grad, grad_attn, gsum, _ = run_mlp(
        tokens, y, yall, w_output, woall, w_gate, w_up, w_down, cotangent, mlp_gain, lengths
    )
    attn_grads, gains, grad_tokens = run_attention_backward(
        tokens, attn_gain, qk, kq, v_ext, yx, pre, grad_attn, w_output, wqk, wv, gr_own, mlp_gain_grad, tables
    )

    mlp_part = dot(hidden, w_down).astype(BF16).reshape(seqs, block, width)
    mlp_out = lax.psum_scatter(mlp_part, "tensor", scatter_dimension=1, tiled=True).astype(F32)
    positions = lax.axis_index("seq") * block + t * quarter + jnp.arange(quarter, dtype=jnp.int32)
    mask = (positions[None, :] < lengths[:, None]).astype(F32)[:, :, None]
    block_out = lax.all_gather((mask * (r_own + mlp_out)).astype(BF16), "tensor", axis=1, tiled=True)

    if chips == 1:
        mlp_grads = [
            lax.psum_scatter(gsum[i], "seq", scatter_dimension=0, tiled=True).astype(F32)
            for i in range(3)
        ]
    else:
        pairs = [[2 * i, 2 * i + 1] for i in range(chips)]

        def scatter(a, copies):
            a = (a.astype(F32) * (1.0 / copies)).astype(BF16)
            return lax.psum_scatter(a, ("dp", "seq"), scatter_dimension=0, tiled=True).astype(F32)

        def joined(a, axis):
            return lax.all_gather(a, "dp", axis=axis, tiled=True, axis_index_groups=pairs)

        both = joined(gsum, 1)
        mlp_grads = [scatter(both[i], 2) for i in range(3)]
        whole = lax.all_gather(attn_grads.astype(BF16), "seq", axis=0, tiled=True)
        attn_grads = scatter(joined(whole, 0), 2 * lax.axis_size("seq"))
        gains = lax.psum(gains, "dp") * 0.5
    share = width // (lax.axis_size("dp") * lax.axis_size("seq"))
    place = (lax.axis_index("dp") * lax.axis_size("seq") + lax.axis_index("seq")) * share
    gains = lax.dynamic_slice_in_dim(gains, place, share, 1)

    def unspread(a):
        return a.reshape(share, heads, LANES)[:, :, :value].reshape(share, heads * value)

    edge, half = heads * LANES, heads * F
    return (
        block_out,
        grad_tokens.astype(F32),
        gains[0],
        attn_grads[:, edge : edge + half],
        attn_grads[:, edge + half : edge + 2 * half],
        unspread(attn_grads[:, edge + 2 * half :]),
        unspread(attn_grads[:, :edge]).T,
        gains[1],
        mlp_grads[0],
        mlp_grads[1],
        mlp_grads[2].T,
    )


def solution(mesh):
    in_specs = (
        P("dp", "seq", None),
        P("dp"),
        P(),
        P(None, "tensor"),
        P(None, "tensor"),
        P(None, "tensor"),
        P("tensor", None),
        P(),
        P(None, "tensor"),
        P(None, "tensor"),
        P("tensor", None),
        P("dp", "seq", None),
    )
    out_specs = (
        P("dp", "seq", None),
        P("dp", "seq", None),
        P(("dp", "seq")),
        P(("dp", "seq"), "tensor"),
        P(("dp", "seq"), "tensor"),
        P(("dp", "seq"), "tensor"),
        P("tensor", ("dp", "seq")),
        P(("dp", "seq")),
        P(("dp", "seq"), "tensor"),
        P(("dp", "seq"), "tensor"),
        P("tensor", ("dp", "seq")),
    )
    return jax.shard_map(shards, mesh=mesh, in_specs=in_specs, out_specs=out_specs, check_vma=False)
```

```python
import functools
import math

import jax
import jax.numpy as jnp
import numpy as np
from jax import lax
from jax.experimental import pallas as pl
from jax.experimental.pallas import tpu as pltpu
from jax.sharding import PartitionSpec as P

F = 16
FEATS = 160
LANES = 128
WIDE = 256
VMEM_LIMIT = 62 << 20
MESH = pl.DeviceIdType.MESH
BF16 = jnp.bfloat16
F32 = jnp.float32
VMEM_SPEC = pl.BlockSpec(memory_space=pltpu.VMEM)
ANY_SPEC = pl.BlockSpec(memory_space=pl.ANY)
NN = (((1,), (0,)), ((), ()))
NT = (((1,), (1,)), ((), ()))
TN = (((0,), (0,)), ((), ()))


def dot(a, b, dims=NN):
    return lax.dot_general(a, b, dims, preferred_element_type=F32)


def feature_tables(heads):
    upper_i, upper_j = np.triu_indices(F)
    pairs = len(upper_i)
    first = np.zeros((2 * heads * F, heads * WIDE), np.float32)
    second = np.zeros_like(first)
    rows = np.zeros((8, WIDE), np.float32)
    cols = np.arange(pairs)
    for h in range(heads):
        first[h * F + upper_i, h * WIDE + cols] = 1.0
        second[h * F + upper_j, h * WIDE + cols] = 1.0
        first[h * F + np.arange(F), h * WIDE + pairs + np.arange(F)] = 1.0
    rows[0, pairs + F] = 1.0
    rows[1, pairs : pairs + F + 1] = 1.0
    rows[2, :pairs] = np.where(upper_i == upper_j, 1.0 / (2 * F), 1.0 / F)
    rows[2, pairs : pairs + F] = 1.0 / math.sqrt(F)
    rows[2, pairs + F] = 1.0
    return tuple(jnp.asarray(a, BF16) for a in (first, second)) + (jnp.asarray(rows),)


def spread_table(heads, width):
    table = np.zeros((heads * width, heads * LANES), np.float32)
    for h in range(heads):
        table[h * width + np.arange(width), h * LANES + np.arange(width)] = 1.0
    return jnp.asarray(table, BF16)


def rows_at(start, count):
    return pl.ds(pl.multiple_of(start, 16), count)


class Gather:
    def __init__(self, source, slots, sems, half):
        me = lax.axis_index("tensor")
        self.x, self.y = {"tensor": me ^ 1}, {"tensor": me ^ 2}
        self.source, self.slots, self.sems, self.half = source, slots, sems, half
        self.first = [
            self.copy(source, slots(0), 0, self.x),
            self.copy(source, slots(1), 1, self.y),
        ]
        self.second = [
            self.copy(half(slots(0), 0), half(slots(2), 0), 2, self.y),
            self.copy(half(slots(1), 1), half(slots(2), 1), 3, self.x),
        ]

    def copy(self, src, dst, i, to):
        return pltpu.make_async_remote_copy(
            src, dst, self.sems.at[0, i], self.sems.at[1, i], device_id=to, device_id_type=MESH
        )

    def start(self):
        for c in self.first:
            c.start()

    def forward(self):
        for c, d in zip(self.first, self.second):
            c.wait_recv()
            d.start()

    def arrive(self):
        for d in self.second:
            d.wait_recv()

    def leave(self):
        for c in self.first + self.second:
            c.wait_send()

    def finish(self):
        self.arrive()
        self.leave()


def greet(devices):
    barrier = pltpu.get_barrier_semaphore()
    for d in devices:
        pl.semaphore_signal(barrier, inc=1, device_id=d, device_id_type=MESH)
    pl.semaphore_wait(barrier, len(devices))


def features(rows, first, second, table, scaled):
    a = dot(rows, first) + table[0:1]
    b = dot(rows, second) + table[1:2]
    out = a * b
    return out * table[2:3] if scaled else out


def head_of(rows, h):
    lane = lax.broadcasted_iota(jnp.int32, rows.shape, 1)
    return jnp.where(lane // F == h, rows, jnp.zeros_like(rows))


def attention_forward(
    nz,
    x_hbm,
    gain_ref,
    wq_hbm,
    wk_hbm,
    wv_ref,
    wo_ref,
    cot_hbm,
    wd_hbm,
    len_ref,
    spread_ref,
    e1_ref,
    e2_ref,
    table_ref,
    qk_ref,
    kq_ref,
    pre_ref,
    v_hbm,
    yx_hbm,
    y_hbm,
    gh_hbm,
    gmt_hbm,
    yall_ref,
    woall_ref,
    wqk_ref,
    x_ref,
    cot_ref,
    wd_ref,
    v_ref,
    yx_ref,
    y_ref,
    gh_ref,
    gmt_ref,
    sloc,
    pout,
    gsems,
    wsems,
    csems,
    zsems,
    lsems,
    osems,
):
    seqs, block, width = x_hbm.shape
    heads = wq_hbm.shape[0] // F
    value = wv_ref.shape[0] // heads
    z = lax.axis_index("seq")
    t = lax.axis_index("tensor")
    core = lax.axis_index("dp")
    side = lax.rem(core, 2)
    mate = {"dp": core + 1 - 2 * side}
    up, down = {"seq": lax.rem(z + 1, nz)}, {"seq": lax.rem(z + nz - 1, nz)}
    greet([{"tensor": t ^ 1}, {"tensor": t ^ 2}, mate, up, down])

    tile = block // 2
    x_loads = [
        pltpu.make_async_copy(
            x_hbm.at[i // 2, pl.ds((i % 2) * tile, tile)],
            x_ref.at[i // 2, pl.ds((i % 2) * tile, tile)],
            lsems.at[i],
        )
        for i in range(2 * seqs)
    ]
    late = [
        pltpu.make_async_copy(cot_hbm, cot_ref, lsems.at[2 * seqs]),
        pltpu.make_async_copy(wd_hbm, wd_ref, lsems.at[2 * seqs + 1]),
    ]
    half = heads * F
    joins = [
        pltpu.make_async_copy(w, wqk_ref.at[pl.ds(i * half, half)], lsems.at[2 * seqs + 2 + i])
        for i, w in enumerate((wq_hbm, wk_hbm))
    ]
    for c in joins + x_loads + late:
        c.start()

    wrows = wo_ref.shape[0] // 4
    cut = wrows // 32 * 16 + 16
    zbit = lax.rem(z, 2)

    def part(s, zb):
        return woall_ref.at[s, rows_at((2 * side + zb) * wrows, wrows)]

    wo = Gather(
        wo_ref.at[rows_at((2 * side + zbit) * wrows, wrows)],
        lambda s: part(s, zbit),
        wsems,
        lambda ref, i: ref.at[pl.ds(0, cut)] if i == 0 else ref.at[pl.ds(cut, wrows - cut)],
    )
    wo.start()

    def share(s, i):
        ref = part(s, zbit if i < 2 else 1 - zbit)
        to = {"seq": z ^ 1} if i == 1 else mate
        return pltpu.make_async_remote_copy(
            ref, ref, csems.at[0, 3 * i + s], csems.at[1, 3 * i + s], device_id=to, device_id_type=MESH
        )

    gain = gain_ref[...].reshape(1, width)
    table = table_ref[...]
    ones = jnp.where(
        lax.rem(lax.broadcasted_iota(jnp.int32, (1, heads * LANES), 1), LANES) == value, 1.0, 0.0
    )
    def project(b, i):
        at = pl.ds(i * tile, tile)
        flat = pl.ds(b * block + i * tile, tile)
        x_loads[2 * b + i].wait()
        rows = x_ref[b, at].astype(F32)
        normed = rows * lax.rsqrt(jnp.mean(rows * rows, axis=-1, keepdims=True) + 1e-06)
        normed = (normed * gain).astype(BF16)
        qk = dot(normed, wqk_ref[...], NT)
        qk_ref[flat] = qk.astype(BF16)
        kq_ref[flat] = pltpu.roll(qk, heads * F, 1).astype(BF16)
        values = dot(normed, wv_ref[...], NT).astype(BF16)
        v_ref[flat] = (dot(values, spread_ref[...]) + ones).astype(BF16)

    def lanes(h, n):
        return pl.ds(h * n, n)

    def states(b):
        flat = pl.ds(b * block, block)
        for h in range(heads):
            wide = lanes(h, WIDE)
            phi = features(kq_ref[flat], e1_ref[:, wide], e2_ref[:, wide], table, False)
            s = dot(phi.astype(BF16), v_ref[flat, lanes(h, LANES)], TN)
            sloc[b * heads + h] = s[:FEATS]

    def send_up(j):
        return pltpu.make_async_remote_copy(
            pout.at[j],
            pre_ref.at[j],
            zsems.at[0, j],
            zsems.at[1, j],
            device_id=up,
            device_id_type=MESH,
        )

    def chain(b, who):
        for at in who:

            @pl.when(z == at)
            def _():
                for h in range(heads):
                    j = b * heads + h
                    if at == 0:
                        pre_ref[j] = jnp.zeros((FEATS, LANES), BF16)
                        pout[j] = sloc[j].astype(BF16)
                    else:
                        send_up(j).wait_recv()
                        if at < nz - 1:
                            pout[j] = (sloc[j] + pre_ref[j].astype(F32)).astype(BF16)
                    if at < nz - 1:
                        send_up(j).start()

    def attend(b, h):
        narrow = lanes(h, LANES)
        wide = lanes(h, WIDE)
        for i in range(2):
            span = (i + 1) * tile
            at = pl.ds(b * block + i * tile, tile)
            until = pl.ds(b * block, span)
            rows = qk_ref[at]
            s = dot(head_of(rows, h), kq_ref[until], NT)
            w = 1.0 + s * (1.0 / math.sqrt(F))
            w = 0.5 * (w * w) + 0.5
            row = lax.broadcasted_iota(jnp.int32, w.shape, 0) + i * tile
            col = lax.broadcasted_iota(jnp.int32, w.shape, 1)
            w = jnp.where(col <= row, w, 0.0).astype(BF16)
            num = dot(w, v_ref[until, narrow])
            phi = features(rows, e1_ref[:, wide], e2_ref[:, wide], table, True)
            num = num + dot(phi[:, :FEATS].astype(BF16), pre_ref[b * heads + h])
            recip = 1.0 / num[:, value : value + 1]
            lane = lax.broadcasted_iota(jnp.int32, num.shape, 1)
            yx_ref[at, narrow] = jnp.where(lane == value, recip, num * recip)

    def gather(b):
        flat = pl.ds(b * block, block)
        return Gather(
            y_ref.at[flat],
            lambda s: yall_ref.at[s, flat],
            gsems.at[b],
            lambda ref, i: ref.at[pl.ds(i * tile, tile)],
        )

    def pack(b):
        for i in range(2):
            at = pl.ds(b * block + i * tile, tile)
            y_ref[at] = dot(yx_ref[at].astype(BF16), spread_ref[...], NT).astype(BF16)

    def put(src, dst, i):
        return pltpu.make_async_copy(src, dst, osems.at[i])

    def hidden_outs(i):
        at = pl.ds(i * tile, tile)
        return [
            put(gh_ref.at[at], gh_hbm.at[at], 2 * i),
            put(gmt_ref.at[:, at], gmt_hbm.at[:, at], 2 * i + 1),
        ]

    first_out = 4 * seqs
    outs = [
        put(v_ref, v_hbm, first_out),
        put(yx_ref, yx_hbm, first_out + 1),
        put(y_ref, y_hbm, first_out + 2),
    ]

    def hidden_grads(i):
        b, local = i // 2, i % 2
        at = z * block + local * tile + lax.broadcasted_iota(jnp.int32, (tile, 1), 0)
        mask = (at < len_ref[b]).astype(F32)
        gm = (cot_ref[b, pl.ds(local * tile, tile)].astype(F32) * mask).astype(BF16)
        gmt_ref[:, pl.ds(i * tile, tile)] = gm.T
        gh_ref[pl.ds(i * tile, tile)] = dot(gm, wd_ref[...], NT).astype(BF16)
        for c in hidden_outs(i):
            c.start()

    gathers = [gather(b) for b in range(seqs)]
    mid = list(range(1, nz - 1))
    for c in joins:
        c.wait()
    for b in range(seqs + 1):
        if b < seqs:
            for i in range(2):
                project(b, i)
                if b > 0 and i == 0:
                    chain(b - 1, mid[:1])
            if b > 0:
                chain(b - 1, mid[1:])
                wo.forward()
                for s in range(2):
                    share(s, 0).start()
            states(b)
            chain(b, [0])
        if b > 0:
            chain(b - 1, [nz - 1])
            if b == seqs:
                for s in range(2):
                    share(s, 1).start()
            for h in range(heads):
                attend(b - 1, h)
                if b == seqs - 1:
                    chain(b, mid[h : h + 1] if h < heads - 1 else mid[h:])
            pack(b - 1)
            gathers[b - 1].start()
    for c in outs:
        c.start()
    wo.arrive()
    share(2, 0).start()
    share(2, 1).start()
    for c in late:
        c.wait()
    hidden_grads(0)
    for s in range(2):
        share(s, 1).wait_recv()
        share(s, 2).start()
    gathers[0].forward()
    for i in range(1, 2 * seqs):
        hidden_grads(i)
    for g in gathers[1:]:
        g.forward()
    share(2, 1).wait_recv()
    share(2, 2).start()
    for c in outs:
        c.wait()
    for i in range(2 * seqs):
        for c in hidden_outs(i):
            c.wait()
    wo.leave()
    for g in gathers:
        g.finish()
    for s in range(3):
        share(s, 0).wait()
        share(s, 1).wait_send()
        share(s, 2).wait()

    @pl.when(z < nz - 1)
    def _():
        for j in range(seqs * heads):
            send_up(j).wait_send()


def run_attention_forward(x, gain, wq, wk, wv, wo, cot, wd, lengths, tables):
    seqs, block, width = x.shape
    heads = wq.shape[0] // F
    value = wv.shape[0] // heads
    rows = seqs * block
    spread, e1, e2, table = tables
    shape = jax.ShapeDtypeStruct
    wide, ff = heads * LANES, wd.shape[0]
    shapes = [
        shape((rows, 2 * heads * F), BF16),
        shape((rows, 2 * heads * F), BF16),
        shape((seqs * heads, FEATS, LANES), BF16),
        shape((rows, wide), BF16),
        shape((rows, wide), F32),
        shape((rows, heads * value), BF16),
        shape((rows, ff), BF16),
        shape((width, rows), BF16),
        shape((3, rows, heads * value), BF16),
        shape((3,) + wo.shape, BF16),
    ]
    vm, dma = pltpu.VMEM, pltpu.SemaphoreType.DMA
    smem = pl.BlockSpec(memory_space=pltpu.SMEM)
    return pl.pallas_call(
        functools.partial(attention_forward, lax.axis_size("seq")),
        out_shape=shapes,
        in_specs=[ANY_SPEC, VMEM_SPEC] + [ANY_SPEC] * 2 + [VMEM_SPEC] + [ANY_SPEC] * 3 + [smem] + [VMEM_SPEC] * 4,
        out_specs=[VMEM_SPEC] * 3 + [ANY_SPEC] * 7,
        scratch_shapes=[
            vm((2 * heads * F, width), BF16),
            vm(x.shape, BF16),
            vm(x.shape, BF16),
            vm(wd.shape, BF16),
            vm((rows, wide), BF16),
            vm((rows, wide), F32),
            vm((rows, heads * value), BF16),
            vm((rows, ff), BF16),
            vm((width, rows), BF16),
            vm((seqs * heads, FEATS, LANES), F32),
            vm((seqs * heads, FEATS, LANES), BF16),
            dma((seqs, 2, 4)),
            dma((2, 4)),
            dma((2, 9)),
            dma((2, seqs * heads)),
            dma((2 * seqs + 4,)),
            dma((4 * seqs + 3,)),
        ],
        compiler_params=pltpu.CompilerParams(
            collective_id=0, has_side_effects=True, vmem_limit_bytes=VMEM_LIMIT
        ),
        cost_estimate=pl.CostEstimate(
            flops=2 * rows * width * heads * (2 * F + value), bytes_accessed=20 << 20, transcendentals=0
        ),
        name="attention_forward",
    )(x, gain, wq, wk, wv, wo, cot, wd, lengths, spread, e1, e2, table)


class Exchange:
    def __init__(self, sems):
        me = lax.axis_index("tensor")
        self.x, self.y = {"tensor": me ^ 1}, {"tensor": me ^ 2}
        self.sems = sems

    def copy(self, src, dst, i, to):
        return pltpu.make_async_remote_copy(
            src, dst, self.sems.at[0, i], self.sems.at[1, i], device_id=to, device_id_type=MESH
        )


class ReduceScatter(Exchange):
    def __init__(self, part, near, far, sems):
        super().__init__(sems)
        me = lax.axis_index("tensor")
        self.part, self.near, self.far = part, near, far
        self.q = q = near[0].shape[0] * 2
        self.half = q // 2
        self.at = [me * q, (me ^ 1) * q, (me ^ 2) * q, (me ^ 3) * q]
        over = self.at[3]
        self.first = [
            self.copy(part.at[rows_at(over, self.half)], near[0], 0, self.x),
            self.copy(part.at[rows_at(over + self.half, self.half)], near[1], 1, self.y),
        ]
        self.second = [
            self.copy(part.at[rows_at(self.at[2], q)], far[1], 2, self.y),
            self.copy(part.at[rows_at(self.at[1], q)], far[0], 3, self.x),
        ]

    def start(self):
        for c in self.first:
            c.start()

    def forward(self):
        for i, start in ((0, self.at[2]), (1, self.at[1] + self.half)):
            self.first[i].wait_recv()
            rows = rows_at(start, self.half)
            self.part[rows] = (self.part[rows].astype(F32) + self.near[i][...].astype(F32)).astype(BF16)
            self.second[i].start()

    def total(self):
        for c in self.second:
            c.wait_recv()
        mine = self.part[rows_at(self.at[0], self.q)].astype(F32)
        return mine + self.far[0][...].astype(F32) + self.far[1][...].astype(F32)

    def drain(self):
        for c in self.first + self.second:
            c.wait_send()


class RowGather(Exchange):
    def __init__(self, source, piece, half, sems):
        super().__init__(sems)
        me = lax.axis_index("tensor")
        self.first = [
            self.copy(source, piece(me), 0, self.x),
            self.copy(source, piece(me), 1, self.y),
        ]
        self.second = [
            self.copy(half(me ^ 1, 0), half(me ^ 1, 0), 2, self.y),
            self.copy(half(me ^ 2, 1), half(me ^ 2, 1), 3, self.x),
        ]

    start = Gather.start
    forward = Gather.forward
    arrive = Gather.arrive
    leave = Gather.leave
    finish = Gather.finish


def norm_backward(rows, grad, gain):
    norm = lax.rsqrt(jnp.mean(rows * rows, axis=-1, keepdims=True) + 1e-06)
    unit = rows * norm
    gain_grad = jnp.sum(grad * unit, axis=0, keepdims=True)
    scaled = grad * gain
    mean = jnp.mean(scaled * unit, axis=-1, keepdims=True)
    return norm * (scaled - unit * mean), gain_grad


def own_rows(value, t, count):
    parts = [value[i * count : (i + 1) * count] for i in range(4)]
    low = jnp.where(t == 0, parts[0], parts[1])
    return jnp.where(t < 2, low, jnp.where(t == 2, parts[2], parts[3]))


def mlp_kernel(
    nz,
    x_hbm,
    y_hbm,
    yall_hbm,
    wo_hbm,
    woall_hbm,
    wg_hbm,
    wu_hbm,
    wd_hbm,
    gh_hbm,
    gmt_hbm,
    cot_hbm,
    gain_ref,
    len_ref,
    r_ref,
    gain_grad_ref,
    down_ref,
    block_ref,
    gr_hbm,
    gattn_hbm,
    gsum_hbm,
    gdown_hbm,
    land_hbm,
    zland_hbm,
    wo4,
    wg,
    wu,
    wd,
    xt,
    yt,
    ght,
    h2t,
    gmt,
    gg,
    gu,
    hid,
    part,
    near,
    far,
    ga,
    grs,
    stage,
    back,
    keep,
    lsems,
    rsems,
    asems,
    msems,
    bsems,
    dsems,
    osems,
    psems,
    free_sem,
):
    seqs, block, width = x_hbm.shape
    tile = xt.shape[0]
    per = block // tile
    quarter = tile // 4
    tiles = seqs * per
    z = lax.axis_index("seq")
    t = lax.axis_index("tensor")
    core = lax.axis_index("dp")
    side = lax.rem(core, 2)
    mate = {"dp": core + 1 - 2 * side}
    near_z, far_z = {"seq": z ^ 1}, {"seq": z ^ 2}
    greet([{"tensor": t ^ 1}, {"tensor": t ^ 2}, mate, near_z, far_z])
    gain = gain_ref[...].reshape(1, width)

    def load(src, dst, i):
        return pltpu.make_async_copy(src, dst, lsems.at[i])

    weights = [
        load(wo_hbm, wo4.at[0], 0),
        *[load(woall_hbm.at[s], wo4.at[s + 1], 1 + s) for s in range(3)],
        load(wg_hbm, wg, 4),
        load(wu_hbm, wu, 5),
    ]
    late = [load(gmt_hbm, gmt, 6), load(wd_hbm, wd, 7)]

    def xy_loads(i):
        b, at = i // per, lax.rem(i, per) * tile
        flat = rows_at(i * tile, tile)
        return [
            load(x_hbm.at[b, rows_at(at, tile)], xt, 8),
            load(y_hbm.at[flat], yt.at[0], 9),
            *[load(yall_hbm.at[s, flat], yt.at[s + 1], 10 + s) for s in range(3)],
        ]

    def g_load(i):
        return load(gh_hbm.at[rows_at(i * tile, tile)], ght, 13)

    def c_load(i):
        b, at = i // per, lax.rem(i, per) * tile + t * quarter
        return load(cot_hbm.at[b, rows_at(at, quarter)], ga.at[i], 14 + i)

    for c in xy_loads(0) + weights + [g_load(0)] + [c_load(i) for i in range(tiles)] + late:
        c.start()

    def scatter(i):
        return ReduceScatter(
            part.at[rows_at(i * tile, tile)],
            [near.at[i, k] for k in range(2)],
            [far.at[i, k] for k in range(2)],
            rsems.at[i],
        )

    def mlp_scatter(i):
        source = wo4.at[i, pl.ds(0, tile)]
        near_ref = [wo4.at[i, pl.ds(tile + k * (quarter // 2), quarter // 2)] for k in range(2)]
        far_ref = [wo4.at[i, pl.ds(tile + (k + 1) * quarter, quarter)] for k in range(2)]
        return ReduceScatter(source, near_ref, far_ref, psems.at[i])

    def gather(i):
        def piece(k):
            return gattn_hbm.at[rows_at(i * tile + k * quarter, quarter)]

        def half(k, h):
            start = i * tile + k * quarter + h * (quarter // 2)
            return gattn_hbm.at[rows_at(start, quarter // 2)]

        return RowGather(ga.at[i], piece, half, asems.at[i])

    def place(i):
        at = rows_at(i * tile + t * quarter, quarter)
        return [
            pltpu.make_async_copy(ga.at[i], gattn_hbm.at[at], osems.at[0, i]),
            pltpu.make_async_copy(grs, gr_hbm.at[i], osems.at[1, i]),
        ]

    def tile_step(i, first):
        flat = rows_at(i * tile, tile)
        for c in xy_loads(i):
            c.wait()
        if first:
            for c in weights[:4]:
                c.wait()
        r = xt[...].astype(F32)
        for s in range(4):
            r = r + dot(yt[s], wo4[s])

        @pl.when(i + 1 < tiles)
        def _():
            for c in xy_loads(i + 1):
                c.start()

        r_ref[i] = own_rows(r, t, quarter)
        h2 = r * lax.rsqrt(jnp.mean(r * r, axis=-1, keepdims=True) + 1e-06) * gain
        h2 = h2.astype(BF16)
        h2t[:, pl.ds(pl.multiple_of(i * tile, LANES), tile)] = h2.T
        if first:
            for c in weights[4:6]:
                c.wait()
        gate = dot(h2, wg[...], NT)
        up = dot(h2, wu[...], NT)
        if not first:
            scatter(i - 1).forward()
        g_load(i).wait()
        gh = ght[...].astype(F32)
        sig = 1.0 / (1.0 + jnp.exp(-gate))
        silu = gate * sig
        hid[flat] = (silu * up).astype(BF16)
        gg[flat] = (gh * up * (sig * (1.0 + gate * (1.0 - sig)))).astype(BF16)
        gu[flat] = (gh * silu).astype(BF16)

        @pl.when(i + 1 < tiles)
        def _():
            g_load(i + 1).start()

        part[flat] = (dot(gg[flat], wg[...]) + dot(gu[flat], wu[...])).astype(BF16)
        scatter(i).start()

    def mixed(i, first):
        b = i // per
        grad = scatter(i).total()
        c_load(i).wait()
        at = z * block + lax.rem(i, per) * tile + t * quarter
        at = at + lax.broadcasted_iota(jnp.int32, (quarter, 1), 0)
        out = ga[i].astype(F32) * (at < len_ref[b]).astype(F32)
        gr, gain_grad = norm_backward(r_ref[i], grad, gain)
        gr = gr + out
        if first:
            gain_grad_ref[...] = gain_grad
        else:
            gain_grad_ref[...] += gain_grad
            place(i - 1)[1].wait()
        grs[...] = gr
        ga[i] = gr.astype(BF16)
        gather(i).start()
        for c in place(i):
            c.start()

    tile_step(0, True)

    def rest(i, carry):
        tile_step(i, False)
        return carry

    lax.fori_loop(1, tiles - 1, rest, 0)
    mixed(0, True)
    tile_step(tiles - 1, False)

    lefts = (gmt, h2t, h2t)
    rights = (hid, gg, gu)
    half_rows = width // 2
    chunk = stage.shape[1]
    last = tiles - 1

    def product(n, base, m):
        return dot(lefts[n][rows_at(base + m * chunk, chunk)], rights[n][...])

    def to_mate(n, m, slot):
        return pltpu.make_async_remote_copy(
            stage.at[slot],
            land_hbm.at[n, m],
            msems.at[0, slot],
            msems.at[1, n * nz + m],
            device_id=mate,
            device_id_type=MESH,
        )

    def from_mate(n, m):
        return pltpu.make_async_copy(land_hbm.at[n, m], back, bsems.at[0])

    def to_sum(n, m, slot):
        at = gdown_hbm.at[m] if n == 0 else gsum_hbm.at[m, n - 1]
        return pltpu.make_async_copy(stage.at[slot], at, bsems.at[1 + slot])

    over = [z ^ 3, z ^ 1]
    across = [
        pltpu.make_async_remote_copy(
            gdown_hbm.at[over[k]],
            zland_hbm.at[k],
            dsems.at[0, k],
            dsems.at[1, k],
            device_id=near_z,
            device_id_type=MESH,
        )
        for k in range(2)
    ]
    beyond = pltpu.make_async_remote_copy(
        keep, zland_hbm.at[2], dsems.at[0, 2], dsems.at[1, 2], device_id=far_z, device_id_type=MESH
    )

    def landed(k):
        c = pltpu.make_async_copy(zland_hbm.at[k], back, bsems.at[0])
        c.start()
        c.wait()
        return back[...].astype(F32)

    def pass_on():
        across[0].wait_recv()
        keep[...] = (keep[...].astype(F32) + landed(0)).astype(BF16)
        beyond.start()

    def step_mlp(i):
        flat = rows_at(i * tile, tile)
        wo4[i, :tile] = dot(hid[flat], wd[...]).astype(BF16)
        mlp_scatter(i).start()

    def block_rows(i):
        b = i // per
        at = z * block + lax.rem(i, per) * tile + t * quarter
        at = at + lax.broadcasted_iota(jnp.int32, (quarter, 1), 0)
        mask = (at < len_ref[b]).astype(F32)
        block_ref[i] = (mask * (r_ref[i] + mlp_scatter(i).total())).astype(BF16)

    for to in ({"tensor": t ^ 1}, {"tensor": t ^ 2}):
        pl.semaphore_signal(free_sem, inc=1, device_id=to, device_id_type=MESH)
    late[0].wait()
    late[1].wait()
    gather(0).forward()
    mixed(1, False)
    steps = {
        0: lambda: mixed(last - 1, False),
        3: lambda: scatter(last).forward(),
        4: lambda: pl.semaphore_wait(free_sem, 2),
        5: lambda: step_mlp(0),
        6: lambda: step_mlp(1),
        7: lambda: step_mlp(2),
        8: lambda: step_mlp(3),
        9: lambda: gather(1).forward(),
        11: lambda: mixed(last, False),
        13: lambda: gather(last - 1).forward(),
        17: lambda: gather(last).forward(),
        18: lambda: mlp_scatter(0).forward(),
        19: lambda: mlp_scatter(1).forward(),
        20: lambda: mlp_scatter(2).forward(),
        21: lambda: mlp_scatter(3).forward(),
    }
    count = 0
    for n in range(3):
        sent = []
        for m in range(nz):
            if m >= 2:
                to_mate(n, *sent[m - 2]).wait_send()
            stage[m % 2] = product(n, (1 - side) * half_rows, m).astype(BF16)
            to_mate(n, m, m % 2).start()
            sent.append((m, m % 2))
            steps.get(count, lambda: None)()
            count += 1
        for m in range(nz - 2, nz):
            to_mate(n, *sent[m]).wait_send()
        order = [z ^ 3, z ^ 1, z ^ 2, z] if n == 0 else list(range(nz))
        for k, m in enumerate(order):
            to_mate(n, m, 0).wait_recv()
            from_mate(n, m).start()
            out = product(n, side * half_rows, m)
            from_mate(n, m).wait()
            out = out + back[...].astype(F32)
            if n == 0 and k >= 2:
                if k == 2:
                    keep[...] = out.astype(BF16)
                else:
                    down_ref[...] = out
            else:
                if k >= 2:
                    to_sum(n, order[k - 2], k % 2).wait()
                stage[k % 2] = out.astype(BF16)
                to_sum(n, m, k % 2).start()
            if n == 0 and k < 2:
                to_sum(n, m, k % 2).wait()
                across[k].start()
            steps.get(count, lambda: None)()
            count += 1
        if n > 0:
            for k in range(nz - 2, nz):
                to_sum(n, order[k], k % 2).wait()
        if n == 1:
            pass_on()
    across[1].wait_recv()
    down_ref[...] += landed(1)
    place(last)[1].wait()
    for i in range(tiles):
        place(i)[0].wait()
        gather(i).finish()
        scatter(i).drain()
    for c in across:
        c.wait_send()
    for i in range(tiles):
        block_rows(i)
        mlp_scatter(i).drain()
    beyond.wait_recv()
    down_ref[...] += landed(2)
    beyond.wait_send()


def run_mlp(x, y, yall, wo, woall, wg, wu, wd, gh, gmt, cot, gain, lengths):
    seqs, block, width = x.shape
    rows = seqs * block
    nz = lax.axis_size("seq")
    value, ff = wo.shape[0], wd.shape[0]
    tile = block // 2
    tiles, quarter = rows // tile, tile // 4
    chunk = width // 2 // nz
    shape = jax.ShapeDtypeStruct
    shapes = [
        shape((tiles, quarter, width), F32),
        shape((1, width), F32),
        shape((chunk, ff), F32),
        shape((tiles, quarter, width), BF16),
        shape((tiles, quarter, width), F32),
        shape((rows, width), BF16),
        shape((nz, 2, chunk, ff), BF16),
        shape((nz, chunk, ff), BF16),
        shape((3, nz, chunk, ff), BF16),
        shape((3, chunk, ff), BF16),
    ]
    vm, dma = pltpu.VMEM, pltpu.SemaphoreType.DMA
    scratch = [
        vm((4, value, width), BF16),
        vm((ff, width), BF16),
        vm((ff, width), BF16),
        vm((ff, width), BF16),
        vm((tile, width), BF16),
        vm((4, tile, value), BF16),
        vm((tile, ff), BF16),
        vm((width, rows), BF16),
        vm((width, rows), BF16),
        vm((rows, ff), BF16),
        vm((rows, ff), BF16),
        vm((rows, ff), BF16),
        vm((rows, width), BF16),
        vm((tiles, 2, quarter // 2, width), BF16),
        vm((tiles, 2, quarter, width), BF16),
        vm((tiles, quarter, width), BF16),
        vm((quarter, width), F32),
        vm((2, chunk, ff), BF16),
        vm((chunk, ff), BF16),
        vm((chunk, ff), BF16),
        dma((14 + tiles,)),
        dma((tiles, 2, 4)),
        dma((tiles, 2, 4)),
        dma((2, 3 * nz)),
        dma((3,)),
        dma((2, 3)),
        dma((2, tiles)),
        dma((tiles, 2, 4)),
        pltpu.SemaphoreType.REGULAR,
    ]
    return pl.pallas_call(
        functools.partial(mlp_kernel, nz),
        out_shape=shapes,
        in_specs=[ANY_SPEC] * 11 + [VMEM_SPEC, pl.BlockSpec(memory_space=pltpu.SMEM)],
        out_specs=[VMEM_SPEC] * 4 + [ANY_SPEC] * 6,
        scratch_shapes=scratch,
        compiler_params=pltpu.CompilerParams(
            collective_id=1, has_side_effects=True, vmem_limit_bytes=VMEM_LIMIT
        ),
        cost_estimate=pl.CostEstimate(
            flops=2 * rows * width * (4 * value + 8 * ff), bytes_accessed=60 << 20, transcendentals=0
        ),
        name="mlp_forward_backward",
    )(x, y, yall, wo, woall, wg.T, wu.T, wd, gh, gmt, cot, gain, lengths)


def attention_backward(
    nz,
    x_hbm,
    gain_ref,
    qk_ref,
    kq_ref,
    v_ref,
    yx_ref,
    pre_ref,
    gattn_ref,
    wo_ref,
    wq_hbm,
    wk_hbm,
    wv_hbm,
    gr_hbm,
    gains_ref,
    block_hbm,
    spread_ref,
    e1_ref,
    e2_ref,
    f1_ref,
    f2_ref,
    table_ref,
    grads_ref,
    gains_out,
    gt_hbm,
    bo_hbm,
    wqk_ref,
    wv_ref,
    gr_ref,
    gn,
    gv,
    gvb,
    gqk,
    gqkb,
    yb,
    gat,
    h1t,
    sloc,
    sout,
    suf,
    xt,
    xq,
    part,
    near,
    far,
    gq,
    stage,
    land,
    total,
    zland,
    zsum,
    gsend,
    gland,
    lsems,
    zsems,
    rsems,
    asems,
    msems,
    dsems,
    ksems,
    asems2,
    osems,
):
    seqs, block, width = x_hbm.shape
    heads = wq_hbm.shape[0] // F
    value = wv_hbm.shape[0] // heads
    tile = block // 2
    quarter = tile // 4
    rows = seqs * block
    tiles = rows // tile
    z = lax.axis_index("seq")
    t = lax.axis_index("tensor")
    core = lax.axis_index("dp")
    side = lax.rem(core, 2)
    mate = {"dp": core + 1 - 2 * side}
    others = [{"seq": lax.rem(z + k, nz)} for k in range(1, nz)]
    greet([{"tensor": t ^ 1}, {"tensor": t ^ 2}, mate] + others)
    down = others[-1]
    near_z, far_z = {"seq": z ^ 1}, {"seq": z ^ 2}
    gain = gain_ref[...].reshape(1, width)
    table = table_ref[...]
    scale = table[2:3, :FEATS]

    def lanes(h, n):
        return pl.ds(h * n, n)

    def x_load(i):
        b, at = i // 2, (i % 2) * tile
        return pltpu.make_async_copy(x_hbm.at[b, pl.ds(at, tile)], xt.at[i % 2], lsems.at[i % 2])

    quarters = [
        pltpu.make_async_copy(
            x_hbm.at[u // 2, rows_at((u % 2) * tile + t * quarter, quarter)], xq.at[u], lsems.at[2 + u]
        )
        for u in range(tiles)
    ]
    x_load(0).start()
    x_load(1).start()
    weights = [
        pltpu.make_async_copy(src, dst, lsems.at[2 + tiles + i])
        for i, (src, dst) in enumerate(
            (
                (wq_hbm, wqk_ref.at[pl.ds(0, heads * F)]),
                (wk_hbm, wqk_ref.at[pl.ds(heads * F, heads * F)]),
                (wv_hbm, wv_ref),
                (gr_hbm, gr_ref),
            )
        )
    ]
    for c in quarters + weights:
        c.start()

    def value_grads(i):
        at = pl.ds(i * tile, tile)
        ga = gattn_ref[at]
        gy = dot(dot(ga, wo_ref[...], NT).astype(BF16), spread_ref[...])
        gat[:, pl.ds(i * tile, tile)] = ga.T
        yb[at] = yx_ref[at].astype(BF16)
        for h in range(heads):
            narrow = lanes(h, LANES)
            g, y = gy[:, h * LANES : (h + 1) * LANES], yx_ref[at, narrow]
            recip = y[:, value : value + 1]
            den = -jnp.sum(g * y, axis=-1, keepdims=True)
            lane = lax.broadcasted_iota(jnp.int32, g.shape, 1)
            gn[at, narrow] = (jnp.where(lane == value, den, g) * recip).astype(BF16)

    def expand(ref, at, h):
        a = dot(ref[at], e1_ref[:, h * WIDE : h * WIDE + FEATS]) + table[0:1, :FEATS]
        b = dot(ref[at], e2_ref[:, h * WIDE : h * WIDE + FEATS]) + table[1:2, :FEATS]
        return a, b

    def states(b):
        flat = pl.ds(b * block, block)
        for h in range(heads):
            a, c = expand(qk_ref, flat, h)
            phi = (a * c * scale).astype(BF16)
            sloc[b * heads + h] = dot(phi, gn[flat, lanes(h, LANES)], TN)

    def send_down(j):
        return pltpu.make_async_remote_copy(
            sout.at[j], suf.at[j], zsems.at[0, j], zsems.at[1, j], device_id=down, device_id_type=MESH
        )

    def chain(b, who):
        for at in who:

            @pl.when(z == nz - 1 - at)
            def _():
                for h in range(heads):
                    j = b * heads + h
                    if at == 0:
                        suf[j] = jnp.zeros((FEATS, LANES), BF16)
                        sout[j] = sloc[j].astype(BF16)
                    else:
                        send_down(j).wait_recv()
                        if at < nz - 1:
                            sout[j] = (sloc[j] + suf[j].astype(F32)).astype(BF16)
                    if at < nz - 1:
                        send_down(j).start()

    def contract(a, c, grad, h, first, second):
        wide = slice(h * WIDE, h * WIDE + FEATS)
        return dot((grad * c).astype(BF16), first[:, wide], NT) + dot(
            (grad * a).astype(BF16), second[:, wide], NT
        )

    def local(b, h):
        narrow = lanes(h, LANES)
        for i in range(2):
            span = (i + 1) * tile
            at = pl.ds(b * block + i * tile, tile)
            until = pl.ds(b * block, span)
            s = dot(head_of(qk_ref[at], h), kq_ref[until], NT)
            w = 1.0 + s * (1.0 / math.sqrt(F))
            row = lax.broadcasted_iota(jnp.int32, w.shape, 0) + i * tile
            col = lax.broadcasted_iota(jnp.int32, w.shape, 1)
            seen = col <= row
            kernel = jnp.where(seen, 0.5 * (w * w) + 0.5, 0.0).astype(BF16)
            grad = gn[at, narrow]
            gs = dot(grad, v_ref[until, narrow], NT) * (w * (1.0 / math.sqrt(F)))
            gs = jnp.where(seen, gs, 0.0).astype(BF16)
            gv[until, narrow] += dot(kernel, grad, TN)
            gqk[until] += dot(gs, head_of(kq_ref[at], heads + h), TN)
            a, c = expand(qk_ref, at, h)
            gphi = dot(grad, pre_ref[b * heads + h], NT) * scale
            gqk[at] += dot(gs, head_of(kq_ref[until], h)) + contract(a, c, gphi, h, e1_ref, e2_ref)

    def state_grads(b, h):
        narrow = lanes(h, LANES)
        flat = pl.ds(b * block, block)
        later = suf[b * heads + h]
        a, c = expand(kq_ref, flat, h)
        gphi = dot(v_ref[flat, narrow], later, NT)
        gqk[flat] += contract(a, c, gphi, h, f1_ref, f2_ref)
        gv[flat, narrow] += dot((a * c).astype(BF16), later)

    def norm_grads(b):
        for i in range(2):
            at = pl.ds(b * block + i * tile, tile)
            gvb[at] = gv[at].astype(BF16)
            gqkb[at] = gqk[at].astype(BF16)
            packed = dot(gvb[at], spread_ref[...], NT).astype(BF16)
            part[at] = (dot(gqkb[at], wqk_ref[...]) + dot(packed, wv_ref[...])).astype(BF16)

    def normed_rows(i):
        x_load(i).wait()
        r = xt[i % 2].astype(F32)
        h1 = r * lax.rsqrt(jnp.mean(r * r, axis=-1, keepdims=True) + 1e-06) * gain
        h1t[:, pl.ds(i * tile, tile)] = h1.astype(BF16).T
        if i + 2 < 2 * seqs:
            x_load(i + 2).start()

    def scatter_of(source, near_ref, far_ref, sems, u):
        return ReduceScatter(
            source.at[pl.ds(u * tile, tile)],
            [near_ref.at[u, k] for k in range(2)],
            [far_ref.at[u, k] for k in range(2)],
            sems.at[u],
        )

    scatters = [scatter_of(part, near, far, rsems, u) for u in range(tiles)]

    def gather_of(source, place, sems, u):
        def piece(k):
            return place.at[u // 2, rows_at((u % 2) * tile + k * quarter, quarter)]

        def half(k, h):
            start = (u % 2) * tile + k * quarter + h * (quarter // 2)
            return place.at[u // 2, rows_at(start, quarter // 2)]

        return RowGather(source.at[u], piece, half, sems.at[u]), piece(t)

    def own_copy(source, place, i, u):
        return pltpu.make_async_copy(source.at[u], place, osems.at[i, u])

    pairs = [gather_of(gq, gt_hbm, asems, u) for u in range(tiles)]
    gathers = [g for g, _ in pairs]
    own_rows = [own_copy(gq, p, 0, u) for u, (_, p) in enumerate(pairs)]
    pairs = [gather_of(block_hbm, bo_hbm, asems2, u) for u in range(tiles)]
    out_gathers = [g for g, _ in pairs]
    own_rows += [own_copy(block_hbm, p, 1, u) for u, (_, p) in enumerate(pairs)]

    half_rows = width // 2
    chunk = half_rows // nz
    spans = [pl.ds(0, heads * LANES), pl.ds(heads * LANES, 2 * heads * F + heads * LANES)]

    def product(p, base):
        at = rows_at(base, half_rows)
        if p == 0:
            return dot(gat[at], yb[...])
        return jnp.concatenate([dot(h1t[at], gqkb[...]), dot(h1t[at], gvb[...])], axis=1)

    def to_mate(p):
        return pltpu.make_async_remote_copy(
            stage.at[:, spans[p]],
            land.at[:, spans[p]],
            msems.at[0, p],
            msems.at[1, p],
            device_id=mate,
            device_id_type=MESH,
        )

    def to_near(p, k):
        return pltpu.make_async_remote_copy(
            total.at[rows_at((z ^ (3, 1)[k]) * chunk, chunk), spans[p]],
            zland.at[k, :, spans[p]],
            dsems.at[0, p, k],
            dsems.at[1, p, k],
            device_id=near_z,
            device_id_type=MESH,
        )

    def to_far(p):
        return pltpu.make_async_remote_copy(
            zsum.at[:, spans[p]],
            zland.at[2, :, spans[p]],
            dsems.at[0, p, 2],
            dsems.at[1, p, 2],
            device_id=far_z,
            device_id_type=MESH,
        )

    def pass_on(p):
        to_near(p, 0).wait_recv()
        mine = total[rows_at((z ^ 2) * chunk, chunk), spans[p]].astype(F32)
        zsum[:, spans[p]] = (mine + zland[0, :, spans[p]].astype(F32)).astype(BF16)
        to_far(p).start()

    def conclude(p):
        to_near(p, 1).wait_recv()
        to_far(p).wait_recv()
        out = total[rows_at(z * chunk, chunk), spans[p]].astype(F32)
        grads_ref[:, spans[p]] = (
            out + zland[1, :, spans[p]].astype(F32) + zland[2, :, spans[p]].astype(F32)
        )
        for k in range(2):
            to_near(p, k).wait_send()
        to_far(p).wait_send()
        to_mate(p).wait_send()

    def send_half(p):
        stage[:, spans[p]] = product(p, (1 - side) * half_rows).astype(BF16)
        to_mate(p).start()

    def sum_half(p):
        out = product(p, side * half_rows)
        to_mate(p).wait_recv()
        total[:, spans[p]] = (out + land[:, spans[p]].astype(F32)).astype(BF16)
        for k in range(2):
            to_near(p, k).start()

    def tokens(b):
        quarters[b].wait()
        grad, gain_grad = norm_backward(xq[b].astype(F32), scatters[b].total(), gain)
        gq[b] = (grad + gr_ref[b]).astype(BF16)
        gathers[b].start()
        own_rows[b].start()
        if b == 0:
            gsend[0] = jnp.concatenate(
                [gain_grad, gains_ref[...], jnp.zeros((6, width), F32)], axis=0
            )
        else:
            gsend[0, 0:1] += gain_grad

    gv[...] = jnp.zeros_like(gv)
    gqk[...] = jnp.zeros_like(gqk)
    mid = list(range(1, nz - 1))
    for g, c in zip(out_gathers, own_rows[tiles:]):
        g.start()
        c.start()
    value_grads(0)
    value_grads(1)
    states(0)
    chain(0, [0])
    value_grads(2)
    chain(0, mid[:1])
    value_grads(3)
    states(1)
    chain(0, mid[1:])
    chain(1, [0])
    for h in range(heads):
        local(0, h)
        chain(1, mid[h : h + 1] if h < heads - 1 else mid[h:])
    out_gathers[0].forward()
    out_gathers[1].forward()
    for c in weights:
        c.wait()
    send_half(0)
    for b in range(seqs):
        chain(b, [nz - 1])
        for h in range(heads):
            state_grads(b, h)
        norm_grads(b)
        scatters[2 * b].start()
        scatters[2 * b + 1].start()
        if b == 0:
            out_gathers[2].forward()
            out_gathers[3].forward()
            for h in range(heads):
                local(1, h)
    sum_half(0)
    scatters[0].forward()
    scatters[1].forward()
    normed_rows(0)
    normed_rows(1)
    scatters[2].forward()
    scatters[3].forward()
    normed_rows(2)
    normed_rows(3)
    tokens(0)
    tokens(1)
    send_half(1)
    sum_half(1)
    pass_on(0)
    tokens(2)
    tokens(3)
    gathers[0].forward()
    gathers[1].forward()
    pass_on(1)

    hops = [{"tensor": t ^ 1}, {"tensor": t ^ 2}, mate]
    for i, to in enumerate(hops):
        c = pltpu.make_async_remote_copy(
            gsend.at[i], gland.at[i], ksems.at[0, i], ksems.at[1, i], device_id=to, device_id_type=MESH
        )
        c.start()
        c.wait()
        gsend[i + 1] = gsend[i] + gland[i]
    last = len(hops)
    copies = [
        pltpu.make_async_remote_copy(
            gsend.at[last],
            gland.at[last + k],
            ksems.at[0, last + k],
            ksems.at[1, last + k],
            device_id=others[k],
            device_id_type=MESH,
        )
        for k in range(nz - 1)
    ]
    for c in copies:
        c.start()
    gathers[2].forward()
    gathers[3].forward()
    for p in range(2):
        conclude(p)
    gains = gsend[last]
    for k, c in enumerate(copies):
        c.wait()
        gains = gains + gland[last + k]
    gains_out[...] = gains
    for c in own_rows:
        c.wait()
    for g in out_gathers + gathers:
        g.finish()
    for c in scatters:
        c.drain()

    @pl.when(z > 0)
    def _():
        for j in range(seqs * heads):
            send_down(j).wait_send()


def run_attention_backward(
    x, gain, qk, kq, v_ext, yx, pre, gattn, wo, wq, wk, wv, gr, gains, block_rows, tables
):
    seqs, block, width = x.shape
    rows = seqs * block
    heads = wq.shape[0] // F
    tile = block // 2
    tiles, quarter = rows // tile, tile // 4
    nz = lax.axis_size("seq")
    spread, e1, e2, table = tables
    half = heads * F
    f1, f2 = jnp.roll(e1, half, 0), jnp.roll(e2, half, 0)
    chunk = width // 2 // nz
    cols = 2 * heads * LANES + 2 * heads * F
    shapes = [
        jax.ShapeDtypeStruct((chunk, cols), F32),
        jax.ShapeDtypeStruct((8, width), F32),
        jax.ShapeDtypeStruct(x.shape, BF16),
        jax.ShapeDtypeStruct(x.shape, BF16),
    ]
    vm, dma = pltpu.VMEM, pltpu.SemaphoreType.DMA
    wide = heads * LANES
    scratch = [
        vm((2 * half, width), BF16),
        vm(wv.shape, BF16),
        vm((tiles, quarter, width), F32),
        vm((rows, wide), BF16),
        vm((rows, wide), F32),
        vm((rows, wide), BF16),
        vm((rows, 2 * half), F32),
        vm((rows, 2 * half), BF16),
        vm((rows, wide), BF16),
        vm((width, rows), BF16),
        vm((width, rows), BF16),
        vm((seqs * heads, FEATS, LANES), F32),
        vm((seqs * heads, FEATS, LANES), BF16),
        vm((seqs * heads, FEATS, LANES), BF16),
        vm((2, tile, width), BF16),
        vm((tiles, quarter, width), BF16),
        vm((rows, width), BF16),
        vm((tiles, 2, quarter // 2, width), BF16),
        vm((tiles, 2, quarter, width), BF16),
        vm((tiles, quarter, width), BF16),
        vm((width // 2, cols), BF16),
        vm((width // 2, cols), BF16),
        vm((width // 2, cols), BF16),
        vm((3, chunk, cols), BF16),
        vm((chunk, cols), BF16),
        vm((4, 8, width), F32),
        vm((3 + nz - 1, 8, width), F32),
        dma((6 + tiles,)),
        dma((2, seqs * heads)),
        dma((tiles, 2, 4)),
        dma((tiles, 2, 4)),
        dma((2, 2)),
        dma((2, 2, 3)),
        dma((2, 3 + nz - 1)),
        dma((tiles, 2, 4)),
        dma((2, tiles)),
    ]
    return pl.pallas_call(
        functools.partial(attention_backward, nz),
        out_shape=shapes,
        in_specs=[ANY_SPEC] + [VMEM_SPEC] * 8 + [ANY_SPEC] * 4 + [VMEM_SPEC, ANY_SPEC] + [VMEM_SPEC] * 6,
        out_specs=[VMEM_SPEC] * 2 + [ANY_SPEC] * 2,
        scratch_shapes=scratch,
        compiler_params=pltpu.CompilerParams(
            collective_id=2, has_side_effects=True, vmem_limit_bytes=VMEM_LIMIT
        ),
        cost_estimate=pl.CostEstimate(
            flops=8 * rows * width * wide, bytes_accessed=30 << 20, transcendentals=0
        ),
        name="attention_backward",
    )(
        x,
        gain,
        qk,
        kq,
        v_ext,
        yx,
        pre,
        gattn,
        wo,
        wq,
        wk,
        wv,
        gr,
        gains,
        block_rows,
        spread,
        e1,
        e2,
        f1,
        f2,
        table,
    )


def finish_kernel(gt_ref, bo_ref, gt_out, bo_out):
    gt_out[...] = gt_ref[...].astype(F32)
    bo_out[...] = bo_ref[...]


def finish(gt, bo):
    seqs, block, width = gt.shape
    spec = pl.BlockSpec((1, block // 4, width), lambda b, i: (b, i, 0))
    return pl.pallas_call(
        finish_kernel,
        grid=(seqs, 4),
        out_shape=[jax.ShapeDtypeStruct(gt.shape, F32), jax.ShapeDtypeStruct(bo.shape, BF16)],
        in_specs=[spec, spec],
        out_specs=[spec, spec],
        cost_estimate=pl.CostEstimate(flops=0, bytes_accessed=20 << 20, transcendentals=0),
        name="finish",
    )(gt, bo)


def shards(
    tokens,
    lengths,
    attn_gain,
    w_query,
    w_key,
    w_value,
    w_output,
    mlp_gain,
    w_gate,
    w_up,
    w_down,
    cotangent,
):
    seqs, block, width = tokens.shape
    heads = w_query.shape[1] // F
    value = w_value.shape[1] // heads
    chips = lax.axis_size("dp") // 2
    tables = (spread_table(heads, value),) + feature_tables(heads)
    wq, wk, wv = w_query.T, w_key.T, w_value.T
    qk, kq, pre, v_ext, yx, y, gh, gmt, yall, woall = run_attention_forward(
        tokens, attn_gain, wq, wk, wv, w_output, cotangent, w_down, lengths, tables
    )
    _, mlp_gain_grad, down_grads, block_rows, gr, gattn, gsum, _, _, _ = run_mlp(
        tokens, y, yall, w_output, woall, w_gate, w_up, w_down, gh, gmt, cotangent, mlp_gain, lengths
    )
    attn_grads, gains, grad_tokens, block_out = run_attention_backward(
        tokens,
        attn_gain,
        qk,
        kq,
        v_ext,
        yx,
        pre,
        gattn,
        w_output,
        wq,
        wk,
        wv,
        gr,
        mlp_gain_grad,
        block_rows,
        tables,
    )
    grad_tokens, block_out = finish(grad_tokens, block_out)
    nz, _, chunk, ff = gsum.shape
    if chips == 1:
        sums = lax.psum_scatter(gsum.reshape(-1, ff), "seq", scatter_dimension=0, tiled=True)
        gate_grads, up_grads = sums[:chunk].astype(F32), sums[chunk:].astype(F32)
    else:
        pairs = [[2 * i, 2 * i + 1] for i in range(chips)]

        def joined(a):
            return lax.all_gather(a, "dp", axis=0, tiled=True, axis_index_groups=pairs)

        def scatter(a, copies):
            a = (a.astype(F32) * (1.0 / copies)).astype(BF16)
            return lax.psum_scatter(a, ("dp", "seq"), scatter_dimension=0, tiled=True).astype(F32)

        def respread(a):
            whole = lax.all_gather(a.astype(BF16), "seq", axis=0, tiled=True)
            return scatter(joined(whole), 2 * nz)

        gate_grads, up_grads = [
            scatter(joined(gsum[:, i].reshape(nz * chunk, ff)), 2) for i in range(2)
        ]
        attn_grads, down_grads = respread(attn_grads), respread(down_grads)
        gains = lax.psum(gains, "dp") * 0.5
    share = width // (lax.axis_size("dp") * lax.axis_size("seq"))
    place = (lax.axis_index("dp") * lax.axis_size("seq") + lax.axis_index("seq")) * share
    gains = lax.dynamic_slice_in_dim(gains, place, share, 1)

    def unspread(a):
        return a.reshape(share, heads, LANES)[:, :, :value].reshape(share, heads * value)

    edge, half = heads * LANES, heads * F
    return (
        block_out,
        grad_tokens,
        gains[0],
        attn_grads[:, edge : edge + half],
        attn_grads[:, edge + half : edge + 2 * half],
        unspread(attn_grads[:, edge + 2 * half :]),
        unspread(attn_grads[:, :edge]).T,
        gains[1],
        gate_grads,
        up_grads,
        down_grads.T,
    )


def solution(mesh):
    in_specs = (
        P("dp", "seq", None),
        P("dp"),
        P(),
        P(None, "tensor"),
        P(None, "tensor"),
        P(None, "tensor"),
        P("tensor", None),
        P(),
        P(None, "tensor"),
        P(None, "tensor"),
        P("tensor", None),
        P("dp", "seq", None),
    )
    out_specs = (
        P("dp", "seq", None),
        P("dp", "seq", None),
        P(("dp", "seq")),
        P(("dp", "seq"), "tensor"),
        P(("dp", "seq"), "tensor"),
        P(("dp", "seq"), "tensor"),
        P("tensor", ("dp", "seq")),
        P(("dp", "seq")),
        P(("dp", "seq"), "tensor"),
        P(("dp", "seq"), "tensor"),
        P("tensor", ("dp", "seq")),
    )
    return jax.shard_map(shards, mesh=mesh, in_specs=in_specs, out_specs=out_specs, check_vma=False)
```

```python
import functools
import math

import jax
import jax.numpy as jnp
import numpy as np
from jax import lax
from jax.experimental import pallas as pl
from jax.experimental.pallas import tpu as pltpu
from jax.sharding import PartitionSpec as P

F = 16
FEATS = 160
LANES = 128
WIDE = 256
VMEM_LIMIT = 62 << 20
MESH = pl.DeviceIdType.MESH
BF16 = jnp.bfloat16
F32 = jnp.float32
VMEM_SPEC = pl.BlockSpec(memory_space=pltpu.VMEM)
ANY_SPEC = pl.BlockSpec(memory_space=pl.ANY)
NN = (((1,), (0,)), ((), ()))
NT = (((1,), (1,)), ((), ()))
TN = (((0,), (0,)), ((), ()))


def dot(a, b, dims=NN):
    return lax.dot_general(a, b, dims, preferred_element_type=F32)


def feature_tables(heads):
    upper_i, upper_j = np.triu_indices(F)
    pairs = len(upper_i)
    first = np.zeros((2 * heads * F, heads * WIDE), np.float32)
    second = np.zeros_like(first)
    rows = np.zeros((8, WIDE), np.float32)
    cols = np.arange(pairs)
    for h in range(heads):
        first[h * F + upper_i, h * WIDE + cols] = 1.0
        second[h * F + upper_j, h * WIDE + cols] = 1.0
        first[h * F + np.arange(F), h * WIDE + pairs + np.arange(F)] = 1.0
    rows[0, pairs + F] = 1.0
    rows[1, pairs : pairs + F + 1] = 1.0
    rows[2, :pairs] = np.where(upper_i == upper_j, 1.0 / (2 * F), 1.0 / F)
    rows[2, pairs : pairs + F] = 1.0 / math.sqrt(F)
    rows[2, pairs + F] = 1.0
    return tuple(jnp.asarray(a, BF16) for a in (first, second)) + (jnp.asarray(rows),)


def spread_table(heads, width):
    table = np.zeros((heads * width, heads * LANES), np.float32)
    for h in range(heads):
        table[h * width + np.arange(width), h * LANES + np.arange(width)] = 1.0
    return jnp.asarray(table, BF16)


def rows_at(start, count):
    return pl.ds(pl.multiple_of(start, 16), count)


class Gather:
    def __init__(self, source, slots, sems, half):
        me = lax.axis_index("tensor")
        self.x, self.y = {"tensor": me ^ 1}, {"tensor": me ^ 2}
        self.source, self.slots, self.sems, self.half = source, slots, sems, half
        self.first = [
            self.copy(source, slots(0), 0, self.x),
            self.copy(source, slots(1), 1, self.y),
        ]
        self.second = [
            self.copy(half(slots(0), 0), half(slots(2), 0), 2, self.y),
            self.copy(half(slots(1), 1), half(slots(2), 1), 3, self.x),
        ]

    def copy(self, src, dst, i, to):
        return pltpu.make_async_remote_copy(
            src, dst, self.sems.at[0, i], self.sems.at[1, i], device_id=to, device_id_type=MESH
        )

    def start(self):
        for c in self.first:
            c.start()

    def forward(self):
        for c, d in zip(self.first, self.second):
            c.wait_recv()
            d.start()

    def arrive(self):
        for d in self.second:
            d.wait_recv()

    def leave(self):
        for c in self.first + self.second:
            c.wait_send()

    def finish(self):
        self.arrive()
        self.leave()


def greet(devices):
    barrier = pltpu.get_barrier_semaphore()
    for d in devices:
        pl.semaphore_signal(barrier, inc=1, device_id=d, device_id_type=MESH)
    pl.semaphore_wait(barrier, len(devices))


def features(rows, first, second, table, scaled):
    a = dot(rows, first) + table[0:1]
    b = dot(rows, second) + table[1:2]
    out = a * b
    return out * table[2:3] if scaled else out


def head_of(rows, h):
    lane = lax.broadcasted_iota(jnp.int32, rows.shape, 1)
    return jnp.where(lane // F == h, rows, jnp.zeros_like(rows))


def attention_forward(
    nz,
    x_hbm,
    gain_ref,
    wq_hbm,
    wk_hbm,
    wv_ref,
    wo_ref,
    cot_hbm,
    wd_hbm,
    len_ref,
    spread_ref,
    e1_ref,
    e2_ref,
    table_ref,
    qk_ref,
    kq_ref,
    pre_ref,
    v_hbm,
    yx_hbm,
    y_hbm,
    gh_hbm,
    gmt_hbm,
    yall_ref,
    woall_ref,
    wqk_ref,
    x_ref,
    cot_ref,
    wd_ref,
    v_ref,
    yx_ref,
    y_ref,
    gh_ref,
    gmt_ref,
    sloc,
    pout,
    gsems,
    wsems,
    csems,
    zsems,
    lsems,
    osems,
):
    seqs, block, width = x_hbm.shape
    heads = wq_hbm.shape[0] // F
    value = wv_ref.shape[0] // heads
    z = lax.axis_index("seq")
    t = lax.axis_index("tensor")
    core = lax.axis_index("dp")
    side = lax.rem(core, 2)
    mate = {"dp": core + 1 - 2 * side}
    up, down = {"seq": lax.rem(z + 1, nz)}, {"seq": lax.rem(z + nz - 1, nz)}
    greet([{"tensor": t ^ 1}, {"tensor": t ^ 2}, mate, up, down])

    tile = block // 2
    x_loads = [
        pltpu.make_async_copy(
            x_hbm.at[i // 2, pl.ds((i % 2) * tile, tile)],
            x_ref.at[i // 2, pl.ds((i % 2) * tile, tile)],
            lsems.at[i],
        )
        for i in range(2 * seqs)
    ]
    late = [
        pltpu.make_async_copy(cot_hbm, cot_ref, lsems.at[2 * seqs]),
        pltpu.make_async_copy(wd_hbm, wd_ref, lsems.at[2 * seqs + 1]),
    ]
    half = heads * F
    joins = [
        pltpu.make_async_copy(w, wqk_ref.at[pl.ds(i * half, half)], lsems.at[2 * seqs + 2 + i])
        for i, w in enumerate((wq_hbm, wk_hbm))
    ]
    for c in joins + x_loads + late:
        c.start()

    wrows = wo_ref.shape[0] // 4
    cut = wrows // 32 * 16 + 16
    zbit = lax.rem(z, 2)

    def part(s, zb):
        return woall_ref.at[s, rows_at((2 * side + zb) * wrows, wrows)]

    wo = Gather(
        wo_ref.at[rows_at((2 * side + zbit) * wrows, wrows)],
        lambda s: part(s, zbit),
        wsems,
        lambda ref, i: ref.at[pl.ds(0, cut)] if i == 0 else ref.at[pl.ds(cut, wrows - cut)],
    )
    wo.start()

    def share(s, i):
        ref = part(s, zbit if i < 2 else 1 - zbit)
        to = {"seq": z ^ 1} if i == 1 else mate
        return pltpu.make_async_remote_copy(
            ref, ref, csems.at[0, 3 * i + s], csems.at[1, 3 * i + s], device_id=to, device_id_type=MESH
        )

    gain = gain_ref[...].reshape(1, width)
    table = table_ref[...]
    ones = jnp.where(
        lax.rem(lax.broadcasted_iota(jnp.int32, (1, heads * LANES), 1), LANES) == value, 1.0, 0.0
    )
    def project(b, i):
        at = pl.ds(i * tile, tile)
        flat = pl.ds(b * block + i * tile, tile)
        x_loads[2 * b + i].wait()
        rows = x_ref[b, at].astype(F32)
        normed = rows * lax.rsqrt(jnp.mean(rows * rows, axis=-1, keepdims=True) + 1e-06)
        normed = (normed * gain).astype(BF16)
        qk = dot(normed, wqk_ref[...], NT)
        qk_ref[flat] = qk.astype(BF16)
        kq_ref[flat] = pltpu.roll(qk, heads * F, 1).astype(BF16)
        values = dot(normed, wv_ref[...], NT).astype(BF16)
        v_ref[flat] = (dot(values, spread_ref[...]) + ones).astype(BF16)

    def lanes(h, n):
        return pl.ds(h * n, n)

    def states(b):
        flat = pl.ds(b * block, block)
        for h in range(heads):
            wide = lanes(h, WIDE)
            phi = features(kq_ref[flat], e1_ref[:, wide], e2_ref[:, wide], table, False)
            s = dot(phi.astype(BF16), v_ref[flat, lanes(h, LANES)], TN)
            sloc[b * heads + h] = s[:FEATS]

    def send_up(j):
        return pltpu.make_async_remote_copy(
            pout.at[j],
            pre_ref.at[j],
            zsems.at[0, j],
            zsems.at[1, j],
            device_id=up,
            device_id_type=MESH,
        )

    def chain(b, who):
        for at in who:

            @pl.when(z == at)
            def _():
                for h in range(heads):
                    j = b * heads + h
                    if at == 0:
                        pre_ref[j] = jnp.zeros((FEATS, LANES), BF16)
                        pout[j] = sloc[j].astype(BF16)
                    else:
                        send_up(j).wait_recv()
                        if at < nz - 1:
                            pout[j] = (sloc[j] + pre_ref[j].astype(F32)).astype(BF16)
                    if at < nz - 1:
                        send_up(j).start()

    def attend(b, h):
        narrow = lanes(h, LANES)
        wide = lanes(h, WIDE)
        for i in range(2):
            span = (i + 1) * tile
            at = pl.ds(b * block + i * tile, tile)
            until = pl.ds(b * block, span)
            rows = qk_ref[at]
            s = dot(head_of(rows, h), kq_ref[until], NT)
            w = 1.0 + s * (1.0 / math.sqrt(F))
            w = 0.5 * (w * w) + 0.5
            row = lax.broadcasted_iota(jnp.int32, w.shape, 0) + i * tile
            col = lax.broadcasted_iota(jnp.int32, w.shape, 1)
            w = jnp.where(col <= row, w, 0.0).astype(BF16)
            num = dot(w, v_ref[until, narrow])
            phi = features(rows, e1_ref[:, wide], e2_ref[:, wide], table, True)
            num = num + dot(phi[:, :FEATS].astype(BF16), pre_ref[b * heads + h])
            recip = 1.0 / num[:, value : value + 1]
            lane = lax.broadcasted_iota(jnp.int32, num.shape, 1)
            yx_ref[at, narrow] = jnp.where(lane == value, recip, num * recip)

    def gather(b):
        flat = pl.ds(b * block, block)
        return Gather(
            y_ref.at[flat],
            lambda s: yall_ref.at[s, flat],
            gsems.at[b],
            lambda ref, i: ref.at[pl.ds(i * tile, tile)],
        )

    def pack(b):
        for i in range(2):
            at = pl.ds(b * block + i * tile, tile)
            y_ref[at] = dot(yx_ref[at].astype(BF16), spread_ref[...], NT).astype(BF16)

    def put(src, dst, i):
        return pltpu.make_async_copy(src, dst, osems.at[i])

    def hidden_outs(i):
        at = pl.ds(i * tile, tile)
        return [
            put(gh_ref.at[at], gh_hbm.at[at], 2 * i),
            put(gmt_ref.at[:, at], gmt_hbm.at[:, at], 2 * i + 1),
        ]

    first_out = 4 * seqs
    outs = [
        put(v_ref, v_hbm, first_out),
        put(yx_ref, yx_hbm, first_out + 1),
        put(y_ref, y_hbm, first_out + 2),
    ]

    def hidden_grads(i):
        b, local = i // 2, i % 2
        at = z * block + local * tile + lax.broadcasted_iota(jnp.int32, (tile, 1), 0)
        mask = (at < len_ref[b]).astype(F32)
        gm = (cot_ref[b, pl.ds(local * tile, tile)].astype(F32) * mask).astype(BF16)
        gmt_ref[:, pl.ds(i * tile, tile)] = gm.T
        gh_ref[pl.ds(i * tile, tile)] = dot(gm, wd_ref[...], NT).astype(BF16)
        for c in hidden_outs(i):
            c.start()

    gathers = [gather(b) for b in range(seqs)]
    mid = list(range(1, nz - 1))
    for c in joins:
        c.wait()
    for b in range(seqs + 1):
        if b < seqs:
            for i in range(2):
                project(b, i)
                if b > 0 and i == 0:
                    chain(b - 1, mid[:1])
            if b > 0:
                chain(b - 1, mid[1:])
                wo.forward()
                for s in range(2):
                    share(s, 0).start()
            states(b)
            chain(b, [0])
        if b > 0:
            chain(b - 1, [nz - 1])
            if b == seqs:
                for s in range(2):
                    share(s, 1).start()
            for h in range(heads):
                attend(b - 1, h)
                if b == seqs - 1:
                    chain(b, mid[h : h + 1] if h < heads - 1 else mid[h:])
            pack(b - 1)
            gathers[b - 1].start()
    for c in outs:
        c.start()
    wo.arrive()
    share(2, 0).start()
    share(2, 1).start()
    for c in late:
        c.wait()
    hidden_grads(0)
    for s in range(2):
        share(s, 1).wait_recv()
        share(s, 2).start()
    gathers[0].forward()
    for i in range(1, 2 * seqs):
        hidden_grads(i)
    for g in gathers[1:]:
        g.forward()
    share(2, 1).wait_recv()
    share(2, 2).start()
    for c in outs:
        c.wait()
    for i in range(2 * seqs):
        for c in hidden_outs(i):
            c.wait()
    wo.leave()
    for g in gathers:
        g.finish()
    for s in range(3):
        share(s, 0).wait()
        share(s, 1).wait_send()
        share(s, 2).wait()

    @pl.when(z < nz - 1)
    def _():
        for j in range(seqs * heads):
            send_up(j).wait_send()


def run_attention_forward(x, gain, wq, wk, wv, wo, cot, wd, lengths, tables):
    seqs, block, width = x.shape
    heads = wq.shape[0] // F
    value = wv.shape[0] // heads
    rows = seqs * block
    spread, e1, e2, table = tables
    shape = jax.ShapeDtypeStruct
    wide, ff = heads * LANES, wd.shape[0]
    shapes = [
        shape((rows, 2 * heads * F), BF16),
        shape((rows, 2 * heads * F), BF16),
        shape((seqs * heads, FEATS, LANES), BF16),
        shape((rows, wide), BF16),
        shape((rows, wide), F32),
        shape((rows, heads * value), BF16),
        shape((rows, ff), BF16),
        shape((width, rows), BF16),
        shape((3, rows, heads * value), BF16),
        shape((3,) + wo.shape, BF16),
    ]
    vm, dma = pltpu.VMEM, pltpu.SemaphoreType.DMA
    smem = pl.BlockSpec(memory_space=pltpu.SMEM)
    return pl.pallas_call(
        functools.partial(attention_forward, lax.axis_size("seq")),
        out_shape=shapes,
        in_specs=[ANY_SPEC, VMEM_SPEC] + [ANY_SPEC] * 2 + [VMEM_SPEC] + [ANY_SPEC] * 3 + [smem] + [VMEM_SPEC] * 4,
        out_specs=[VMEM_SPEC] * 3 + [ANY_SPEC] * 7,
        scratch_shapes=[
            vm((2 * heads * F, width), BF16),
            vm(x.shape, BF16),
            vm(x.shape, BF16),
            vm(wd.shape, BF16),
            vm((rows, wide), BF16),
            vm((rows, wide), F32),
            vm((rows, heads * value), BF16),
            vm((rows, ff), BF16),
            vm((width, rows), BF16),
            vm((seqs * heads, FEATS, LANES), F32),
            vm((seqs * heads, FEATS, LANES), BF16),
            dma((seqs, 2, 4)),
            dma((2, 4)),
            dma((2, 9)),
            dma((2, seqs * heads)),
            dma((2 * seqs + 4,)),
            dma((4 * seqs + 3,)),
        ],
        compiler_params=pltpu.CompilerParams(
            collective_id=0, has_side_effects=True, vmem_limit_bytes=VMEM_LIMIT
        ),
        cost_estimate=pl.CostEstimate(
            flops=2 * rows * width * heads * (2 * F + value), bytes_accessed=20 << 20, transcendentals=0
        ),
        name="attention_forward",
    )(x, gain, wq, wk, wv, wo, cot, wd, lengths, spread, e1, e2, table)


class Exchange:
    def __init__(self, sems):
        me = lax.axis_index("tensor")
        self.x, self.y = {"tensor": me ^ 1}, {"tensor": me ^ 2}
        self.sems = sems

    def copy(self, src, dst, i, to):
        return pltpu.make_async_remote_copy(
            src, dst, self.sems.at[0, i], self.sems.at[1, i], device_id=to, device_id_type=MESH
        )


class ReduceScatter(Exchange):
    def __init__(self, part, near, far, sems):
        super().__init__(sems)
        me = lax.axis_index("tensor")
        self.part, self.near, self.far = part, near, far
        self.q = q = near[0].shape[0] * 2
        self.half = q // 2
        self.at = [me * q, (me ^ 1) * q, (me ^ 2) * q, (me ^ 3) * q]
        over = self.at[3]
        self.first = [
            self.copy(part.at[rows_at(over, self.half)], near[0], 0, self.x),
            self.copy(part.at[rows_at(over + self.half, self.half)], near[1], 1, self.y),
        ]
        self.second = [
            self.copy(part.at[rows_at(self.at[2], q)], far[1], 2, self.y),
            self.copy(part.at[rows_at(self.at[1], q)], far[0], 3, self.x),
        ]

    def start(self):
        for c in self.first:
            c.start()

    def forward(self):
        for i, start in ((0, self.at[2]), (1, self.at[1] + self.half)):
            self.first[i].wait_recv()
            rows = rows_at(start, self.half)
            self.part[rows] = (self.part[rows].astype(F32) + self.near[i][...].astype(F32)).astype(BF16)
            self.second[i].start()

    def total(self):
        for c in self.second:
            c.wait_recv()
        mine = self.part[rows_at(self.at[0], self.q)].astype(F32)
        return mine + self.far[0][...].astype(F32) + self.far[1][...].astype(F32)

    def drain(self):
        for c in self.first + self.second:
            c.wait_send()


class RowGather(Exchange):
    def __init__(self, source, piece, half, sems):
        super().__init__(sems)
        me = lax.axis_index("tensor")
        self.first = [
            self.copy(source, piece(me), 0, self.x),
            self.copy(source, piece(me), 1, self.y),
        ]
        self.second = [
            self.copy(half(me ^ 1, 0), half(me ^ 1, 0), 2, self.y),
            self.copy(half(me ^ 2, 1), half(me ^ 2, 1), 3, self.x),
        ]

    start = Gather.start
    forward = Gather.forward
    arrive = Gather.arrive
    leave = Gather.leave
    finish = Gather.finish


def norm_backward(rows, grad, gain):
    norm = lax.rsqrt(jnp.mean(rows * rows, axis=-1, keepdims=True) + 1e-06)
    unit = rows * norm
    gain_grad = jnp.sum(grad * unit, axis=0, keepdims=True)
    scaled = grad * gain
    mean = jnp.mean(scaled * unit, axis=-1, keepdims=True)
    return norm * (scaled - unit * mean), gain_grad


def own_rows(value, t, count):
    parts = [value[i * count : (i + 1) * count] for i in range(4)]
    low = jnp.where(t == 0, parts[0], parts[1])
    return jnp.where(t < 2, low, jnp.where(t == 2, parts[2], parts[3]))


def mlp_kernel(
    nz,
    x_hbm,
    y_hbm,
    yall_hbm,
    wo_hbm,
    woall_hbm,
    wg_hbm,
    wu_hbm,
    wd_hbm,
    gh_hbm,
    gmt_hbm,
    cot_hbm,
    gain_ref,
    len_ref,
    r_ref,
    gain_grad_ref,
    down_ref,
    block_hbm,
    gr_hbm,
    gattn_hbm,
    gsum_hbm,
    land_hbm,
    zland_hbm,
    wo4,
    wg,
    wu,
    wd,
    xt,
    yt,
    ght,
    h2t,
    gmt,
    gg,
    gu,
    hid,
    part,
    near,
    far,
    ga,
    grs,
    stage,
    back,
    keep,
    lsems,
    rsems,
    asems,
    msems,
    bsems,
    dsems,
    osems,
    psems,
    free_sem,
):
    seqs, block, width = x_hbm.shape
    tile = xt.shape[0]
    per = block // tile
    quarter = tile // 4
    tiles = seqs * per
    z = lax.axis_index("seq")
    t = lax.axis_index("tensor")
    core = lax.axis_index("dp")
    side = lax.rem(core, 2)
    mate = {"dp": core + 1 - 2 * side}
    near_z, far_z = {"seq": z ^ 1}, {"seq": z ^ 2}
    greet([{"tensor": t ^ 1}, {"tensor": t ^ 2}, mate, near_z, far_z])
    gain = gain_ref[...].reshape(1, width)

    def load(src, dst, i):
        return pltpu.make_async_copy(src, dst, lsems.at[i])

    weights = [
        load(wo_hbm, wo4.at[0], 0),
        *[load(woall_hbm.at[s], wo4.at[s + 1], 1 + s) for s in range(3)],
        load(wg_hbm, wg, 4),
        load(wu_hbm, wu, 5),
    ]
    late = [load(gmt_hbm, gmt, 6), load(wd_hbm, wd, 7)]

    def xy_loads(i):
        b, at = i // per, lax.rem(i, per) * tile
        flat = rows_at(i * tile, tile)
        return [
            load(x_hbm.at[b, rows_at(at, tile)], xt, 8),
            load(y_hbm.at[flat], yt.at[0], 9),
            *[load(yall_hbm.at[s, flat], yt.at[s + 1], 10 + s) for s in range(3)],
        ]

    def g_load(i):
        return load(gh_hbm.at[rows_at(i * tile, tile)], ght, 13)

    def c_load(i):
        b, at = i // per, lax.rem(i, per) * tile + t * quarter
        return load(cot_hbm.at[b, rows_at(at, quarter)], ga.at[i], 14 + i)

    for c in xy_loads(0) + weights + [g_load(0)] + [c_load(i) for i in range(tiles)] + late:
        c.start()

    def scatter(i):
        return ReduceScatter(
            part.at[rows_at(i * tile, tile)],
            [near.at[i, k] for k in range(2)],
            [far.at[i, k] for k in range(2)],
            rsems.at[i],
        )

    def mlp_scatter(i):
        source = wo4.at[i, pl.ds(0, tile)]
        near_ref = [wo4.at[i, pl.ds(tile + k * (quarter // 2), quarter // 2)] for k in range(2)]
        far_ref = [wo4.at[i, pl.ds(tile + (k + 1) * quarter, quarter)] for k in range(2)]
        return ReduceScatter(source, near_ref, far_ref, psems.at[i])

    def gather(i):
        def piece(k):
            return gattn_hbm.at[rows_at(i * tile + k * quarter, quarter)]

        def half(k, h):
            start = i * tile + k * quarter + h * (quarter // 2)
            return gattn_hbm.at[rows_at(start, quarter // 2)]

        return RowGather(ga.at[i], piece, half, asems.at[i])

    def place(i):
        at = rows_at(i * tile + t * quarter, quarter)
        return [
            pltpu.make_async_copy(ga.at[i], gattn_hbm.at[at], osems.at[0, i]),
            pltpu.make_async_copy(grs, gr_hbm.at[i], osems.at[1, i]),
        ]

    def tile_step(i, first):
        flat = rows_at(i * tile, tile)
        for c in xy_loads(i):
            c.wait()
        if first:
            for c in weights[:4]:
                c.wait()
        r = xt[...].astype(F32)
        for s in range(4):
            r = r + dot(yt[s], wo4[s])

        @pl.when(i + 1 < tiles)
        def _():
            for c in xy_loads(i + 1):
                c.start()

        r_ref[i] = own_rows(r, t, quarter)
        h2 = r * lax.rsqrt(jnp.mean(r * r, axis=-1, keepdims=True) + 1e-06) * gain
        h2 = h2.astype(BF16)
        h2t[:, pl.ds(pl.multiple_of(i * tile, LANES), tile)] = h2.T
        if first:
            for c in weights[4:6]:
                c.wait()
        gate = dot(h2, wg[...], NT)
        up = dot(h2, wu[...], NT)
        if not first:
            scatter(i - 1).forward()
        g_load(i).wait()
        gh = ght[...].astype(F32)
        sig = 1.0 / (1.0 + jnp.exp(-gate))
        silu = gate * sig
        hid[flat] = (silu * up).astype(BF16)
        gg[flat] = (gh * up * (sig * (1.0 + gate * (1.0 - sig)))).astype(BF16)
        gu[flat] = (gh * silu).astype(BF16)

        @pl.when(i + 1 < tiles)
        def _():
            g_load(i + 1).start()

        part[flat] = (dot(gg[flat], wg[...]) + dot(gu[flat], wu[...])).astype(BF16)
        scatter(i).start()

    def mixed(i, first):
        b = i // per
        grad = scatter(i).total()
        c_load(i).wait()
        at = z * block + lax.rem(i, per) * tile + t * quarter
        at = at + lax.broadcasted_iota(jnp.int32, (quarter, 1), 0)
        out = ga[i].astype(F32) * (at < len_ref[b]).astype(F32)
        gr, gain_grad = norm_backward(r_ref[i], grad, gain)
        gr = gr + out
        if first:
            gain_grad_ref[...] = gain_grad
        else:
            gain_grad_ref[...] += gain_grad
            place(i - 1)[1].wait()
        grs[...] = gr
        ga[i] = gr.astype(BF16)
        gather(i).start()
        for c in place(i):
            c.start()

    tile_step(0, True)

    def rest(i, carry):
        tile_step(i, False)
        return carry

    lax.fori_loop(1, tiles - 1, rest, 0)
    mixed(0, True)
    tile_step(tiles - 1, False)

    lefts = (gmt, h2t, h2t)
    rights = (hid, gg, gu)
    half_rows = width // 2
    chunk = back.shape[0]
    last = tiles - 1

    def product(n, base, m):
        return dot(lefts[n][rows_at(base + m * chunk, chunk)], rights[n][...])

    def to_mate(n, m, slot):
        return pltpu.make_async_remote_copy(
            stage.at[slot],
            land_hbm.at[n, m],
            msems.at[0, slot],
            msems.at[1, n * nz + m],
            device_id=mate,
            device_id_type=MESH,
        )

    def from_mate(n, m):
        return pltpu.make_async_copy(land_hbm.at[n, m], back, bsems.at[0])

    def to_sum(n, m, slot):
        return pltpu.make_async_copy(stage.at[slot], gsum_hbm.at[n, m], bsems.at[slot - 1])

    across = [
        pltpu.make_async_remote_copy(
            gsum_hbm.at[n, k],
            zland_hbm.at[n, k],
            dsems.at[0, 2 * n + k],
            dsems.at[1, 2 * n + k],
            device_id=near_z,
            device_id_type=MESH,
        )
        for n in range(2)
        for k in range(2)
    ]
    beyond = pltpu.make_async_remote_copy(
        keep, zland_hbm.at[0, 2], dsems.at[0, 4], dsems.at[1, 4], device_id=far_z, device_id_type=MESH
    )

    def landed(k):
        c = pltpu.make_async_copy(zland_hbm.at[0, k], back, bsems.at[0])
        c.start()
        c.wait()
        return back[...].astype(F32)

    def pass_on():
        across[0].wait_recv()
        keep[...] = (keep[...].astype(F32) + landed(0)).astype(BF16)
        beyond.start()

    def step_mlp(i):
        flat = rows_at(i * tile, tile)
        wo4[i, :tile] = dot(hid[flat], wd[...]).astype(BF16)
        mlp_scatter(i).start()

    def block_out(i):
        return pltpu.make_async_copy(ga.at[i], block_hbm.at[i], osems.at[0, i])

    def block_rows(i):
        b = i // per
        at = z * block + lax.rem(i, per) * tile + t * quarter
        at = at + lax.broadcasted_iota(jnp.int32, (quarter, 1), 0)
        mask = (at < len_ref[b]).astype(F32)
        ga[i] = (mask * (r_ref[i] + mlp_scatter(i).total())).astype(BF16)
        block_out(i).start()

    for to in ({"tensor": t ^ 1}, {"tensor": t ^ 2}):
        pl.semaphore_signal(free_sem, inc=1, device_id=to, device_id_type=MESH)
    late[0].wait()
    late[1].wait()
    gather(0).forward()
    mixed(1, False)
    steps = {
        0: lambda: mixed(last - 1, False),
        3: lambda: scatter(last).forward(),
        4: lambda: pl.semaphore_wait(free_sem, 2),
        5: lambda: step_mlp(0),
        6: lambda: step_mlp(1),
        7: lambda: step_mlp(2),
        8: lambda: step_mlp(3),
        9: lambda: gather(1).forward(),
        11: lambda: mixed(last, False),
        13: lambda: gather(last - 1).forward(),
        16: lambda: mlp_scatter(0).forward(),
        17: lambda: (gather(last).forward(), mlp_scatter(1).forward()),
        18: lambda: mlp_scatter(2).forward(),
        19: lambda: mlp_scatter(3).forward(),
    }
    count = 0

    def step():
        nonlocal count
        steps.get(count, lambda: None)()
        count += 1

    order = [z ^ 3, z ^ 1, z ^ 2, z]
    for n in range(3):

        def for_mate(k):
            if k >= 2:
                to_mate(n, order[k - 2], k % 2).wait_send()
            stage[k % 2] = product(n, (1 - side) * half_rows, order[k]).astype(BF16)
            to_mate(n, order[k], k % 2).start()
            step()

        def for_own(k):
            m = order[k]
            to_mate(n, m, 0).wait_recv()
            from_mate(n, m).start()
            out = product(n, side * half_rows, m)
            from_mate(n, m).wait()
            out = out + back[...].astype(F32)
            if n == 0 and k == 2:
                keep[...] = out.astype(BF16)
            elif n == 0 and k == 3:
                down_ref[...] = out
            else:
                if k > 0 and (n == 2 or k == 3):
                    to_sum(n, k - 1, 2).wait()
                stage[2] = out.astype(BF16)
                to_sum(n, k, 2).start()
            if n < 2 and k < 2:
                to_sum(n, k, 2).wait()
                across[2 * n + k].start()
            step()

        for_mate(0)
        for_mate(1)
        for_own(0)
        for_mate(2)
        for_own(1)
        for_mate(3)
        for_own(2)
        for_own(3)
        for k in range(nz - 2, nz):
            to_mate(n, order[k], k % 2).wait_send()
        if n > 0:
            to_sum(n, nz - 1, 2).wait()
        if n == 1:
            pass_on()
    across[1].wait_recv()
    down_ref[...] += landed(1)
    place(last)[1].wait()
    for i in range(tiles):
        place(i)[0].wait()
        gather(i).finish()
        scatter(i).drain()
    for c in across:
        c.wait_send()
    for i in range(tiles):
        block_rows(i)
        mlp_scatter(i).drain()
    for i in range(tiles):
        block_out(i).wait()
    for c in across[2:]:
        c.wait_recv()
    beyond.wait_recv()
    down_ref[...] += landed(2)
    beyond.wait_send()


def run_mlp(x, y, yall, wo, woall, wg, wu, wd, gh, gmt, cot, gain, lengths):
    seqs, block, width = x.shape
    rows = seqs * block
    nz = lax.axis_size("seq")
    value, ff = wo.shape[0], wd.shape[0]
    tile = block // 2
    tiles, quarter = rows // tile, tile // 4
    chunk = width // 2 // nz
    shape = jax.ShapeDtypeStruct
    shapes = [
        shape((tiles, quarter, width), F32),
        shape((1, width), F32),
        shape((chunk, ff), F32),
        shape((tiles, quarter, width), BF16),
        shape((tiles, quarter, width), F32),
        shape((rows, width), BF16),
        shape((3, 4, chunk, ff), BF16),
        shape((3, nz, chunk, ff), BF16),
        shape((2, 3, chunk, ff), BF16),
    ]
    vm, dma = pltpu.VMEM, pltpu.SemaphoreType.DMA
    scratch = [
        vm((4, value, width), BF16),
        vm((ff, width), BF16),
        vm((ff, width), BF16),
        vm((ff, width), BF16),
        vm((tile, width), BF16),
        vm((4, tile, value), BF16),
        vm((tile, ff), BF16),
        vm((width, rows), BF16),
        vm((width, rows), BF16),
        vm((rows, ff), BF16),
        vm((rows, ff), BF16),
        vm((rows, ff), BF16),
        vm((rows, width), BF16),
        vm((tiles, 2, quarter // 2, width), BF16),
        vm((tiles, 2, quarter, width), BF16),
        vm((tiles, quarter, width), BF16),
        vm((quarter, width), F32),
        vm((3, chunk, ff), BF16),
        vm((chunk, ff), BF16),
        vm((chunk, ff), BF16),
        dma((14 + tiles,)),
        dma((tiles, 2, 4)),
        dma((tiles, 2, 4)),
        dma((2, 3 * nz)),
        dma((3,)),
        dma((2, 5)),
        dma((2, tiles)),
        dma((tiles, 2, 4)),
        pltpu.SemaphoreType.REGULAR,
    ]
    return pl.pallas_call(
        functools.partial(mlp_kernel, nz),
        out_shape=shapes,
        in_specs=[ANY_SPEC] * 11 + [VMEM_SPEC, pl.BlockSpec(memory_space=pltpu.SMEM)],
        out_specs=[VMEM_SPEC] * 3 + [ANY_SPEC] * 6,
        scratch_shapes=scratch,
        compiler_params=pltpu.CompilerParams(
            collective_id=1, has_side_effects=True, vmem_limit_bytes=VMEM_LIMIT
        ),
        cost_estimate=pl.CostEstimate(
            flops=2 * rows * width * (4 * value + 8 * ff), bytes_accessed=60 << 20, transcendentals=0
        ),
        name="mlp_forward_backward",
    )(x, y, yall, wo, woall, wg.T, wu.T, wd, gh, gmt, cot, gain, lengths)


def attention_backward(
    nz,
    x_hbm,
    gain_ref,
    qk_ref,
    kq_ref,
    v_ref,
    yx_ref,
    pre_ref,
    gattn_ref,
    wo_ref,
    wq_hbm,
    wk_hbm,
    wv_hbm,
    gr_hbm,
    gains_ref,
    block_hbm,
    gsum_hbm,
    gland_hbm,
    spread_ref,
    e1_ref,
    e2_ref,
    f1_ref,
    f2_ref,
    table_ref,
    grads_ref,
    gains_out,
    gate_ref,
    up_ref,
    gt_hbm,
    bo_hbm,
    wqk_ref,
    wv_ref,
    gr_ref,
    gn,
    gv,
    gvb,
    gqk,
    gqkb,
    yb,
    gat,
    h1t,
    sloc,
    sout,
    suf,
    xt,
    xq,
    part,
    near,
    far,
    gq,
    stage,
    land,
    total,
    zland,
    zsum,
    gsend,
    gland,
    gload,
    gfar,
    uload,
    uland,
    ufar,
    lsems,
    zsems,
    rsems,
    asems,
    msems,
    dsems,
    ksems,
    asems2,
    osems,
    hsems,
    fsems,
    usems,
):
    seqs, block, width = x_hbm.shape
    heads = wq_hbm.shape[0] // F
    value = wv_hbm.shape[0] // heads
    tile = block // 2
    quarter = tile // 4
    rows = seqs * block
    tiles = rows // tile
    z = lax.axis_index("seq")
    t = lax.axis_index("tensor")
    core = lax.axis_index("dp")
    side = lax.rem(core, 2)
    mate = {"dp": core + 1 - 2 * side}
    others = [{"seq": lax.rem(z + k, nz)} for k in range(1, nz)]
    greet([{"tensor": t ^ k} for k in (1, 2, 3)] + [mate] + others)
    down = others[-1]
    near_z, far_z = {"seq": z ^ 1}, {"seq": z ^ 2}
    gain = gain_ref[...].reshape(1, width)
    table = table_ref[...]
    scale = table[2:3, :FEATS]

    def lanes(h, n):
        return pl.ds(h * n, n)

    def x_load(i):
        b, at = i // 2, (i % 2) * tile
        return pltpu.make_async_copy(x_hbm.at[b, pl.ds(at, tile)], xt.at[i % 2], lsems.at[i % 2])

    quarters = [
        pltpu.make_async_copy(
            x_hbm.at[u // 2, rows_at((u % 2) * tile + t * quarter, quarter)], xq.at[u], lsems.at[2 + u]
        )
        for u in range(tiles)
    ]
    x_load(0).start()
    x_load(1).start()
    weights = [
        pltpu.make_async_copy(src, dst, lsems.at[2 + tiles + i])
        for i, (src, dst) in enumerate(
            (
                (wq_hbm, wqk_ref.at[pl.ds(0, heads * F)]),
                (wk_hbm, wqk_ref.at[pl.ds(heads * F, heads * F)]),
                (wv_hbm, wv_ref),
                (gr_hbm, gr_ref),
            )
        )
    ]
    for c in quarters + weights:
        c.start()

    def value_grads(i):
        at = pl.ds(i * tile, tile)
        ga = gattn_ref[at]
        gy = dot(dot(ga, wo_ref[...], NT).astype(BF16), spread_ref[...])
        gat[:, pl.ds(i * tile, tile)] = ga.T
        yb[at] = yx_ref[at].astype(BF16)
        for h in range(heads):
            narrow = lanes(h, LANES)
            g, y = gy[:, h * LANES : (h + 1) * LANES], yx_ref[at, narrow]
            recip = y[:, value : value + 1]
            den = -jnp.sum(g * y, axis=-1, keepdims=True)
            lane = lax.broadcasted_iota(jnp.int32, g.shape, 1)
            gn[at, narrow] = (jnp.where(lane == value, den, g) * recip).astype(BF16)

    def expand(ref, at, h):
        a = dot(ref[at], e1_ref[:, h * WIDE : h * WIDE + FEATS]) + table[0:1, :FEATS]
        b = dot(ref[at], e2_ref[:, h * WIDE : h * WIDE + FEATS]) + table[1:2, :FEATS]
        return a, b

    def states(b):
        flat = pl.ds(b * block, block)
        for h in range(heads):
            a, c = expand(qk_ref, flat, h)
            phi = (a * c * scale).astype(BF16)
            sloc[b * heads + h] = dot(phi, gn[flat, lanes(h, LANES)], TN)

    def send_down(j):
        return pltpu.make_async_remote_copy(
            sout.at[j], suf.at[j], zsems.at[0, j], zsems.at[1, j], device_id=down, device_id_type=MESH
        )

    def chain(b, who):
        for at in who:

            @pl.when(z == nz - 1 - at)
            def _():
                for h in range(heads):
                    j = b * heads + h
                    if at == 0:
                        suf[j] = jnp.zeros((FEATS, LANES), BF16)
                        sout[j] = sloc[j].astype(BF16)
                    else:
                        send_down(j).wait_recv()
                        if at < nz - 1:
                            sout[j] = (sloc[j] + suf[j].astype(F32)).astype(BF16)
                    if at < nz - 1:
                        send_down(j).start()

    def contract(a, c, grad, h, first, second):
        wide = slice(h * WIDE, h * WIDE + FEATS)
        return dot((grad * c).astype(BF16), first[:, wide], NT) + dot(
            (grad * a).astype(BF16), second[:, wide], NT
        )

    def local(b, h):
        narrow = lanes(h, LANES)
        for i in range(2):
            span = (i + 1) * tile
            at = pl.ds(b * block + i * tile, tile)
            until = pl.ds(b * block, span)
            s = dot(head_of(qk_ref[at], h), kq_ref[until], NT)
            w = 1.0 + s * (1.0 / math.sqrt(F))
            row = lax.broadcasted_iota(jnp.int32, w.shape, 0) + i * tile
            col = lax.broadcasted_iota(jnp.int32, w.shape, 1)
            seen = col <= row
            kernel = jnp.where(seen, 0.5 * (w * w) + 0.5, 0.0).astype(BF16)
            grad = gn[at, narrow]
            gs = dot(grad, v_ref[until, narrow], NT) * (w * (1.0 / math.sqrt(F)))
            gs = jnp.where(seen, gs, 0.0).astype(BF16)
            gv[until, narrow] += dot(kernel, grad, TN)
            gqk[until] += dot(gs, head_of(kq_ref[at], heads + h), TN)
            a, c = expand(qk_ref, at, h)
            gphi = dot(grad, pre_ref[b * heads + h], NT) * scale
            gqk[at] += dot(gs, head_of(kq_ref[until], h)) + contract(a, c, gphi, h, e1_ref, e2_ref)

    def state_grads(b, h):
        narrow = lanes(h, LANES)
        flat = pl.ds(b * block, block)
        later = suf[b * heads + h]
        a, c = expand(kq_ref, flat, h)
        gphi = dot(v_ref[flat, narrow], later, NT)
        gqk[flat] += contract(a, c, gphi, h, f1_ref, f2_ref)
        gv[flat, narrow] += dot((a * c).astype(BF16), later)

    def norm_grads(b):
        for i in range(2):
            at = pl.ds(b * block + i * tile, tile)
            gvb[at] = gv[at].astype(BF16)
            gqkb[at] = gqk[at].astype(BF16)
            packed = dot(gvb[at], spread_ref[...], NT).astype(BF16)
            part[at] = (dot(gqkb[at], wqk_ref[...]) + dot(packed, wv_ref[...])).astype(BF16)

    def normed_rows(i):
        x_load(i).wait()
        r = xt[i % 2].astype(F32)
        h1 = r * lax.rsqrt(jnp.mean(r * r, axis=-1, keepdims=True) + 1e-06) * gain
        h1t[:, pl.ds(i * tile, tile)] = h1.astype(BF16).T
        if i + 2 < 2 * seqs:
            x_load(i + 2).start()

    def scatter_of(source, near_ref, far_ref, sems, u):
        return ReduceScatter(
            source.at[pl.ds(u * tile, tile)],
            [near_ref.at[u, k] for k in range(2)],
            [far_ref.at[u, k] for k in range(2)],
            sems.at[u],
        )

    scatters = [scatter_of(part, near, far, rsems, u) for u in range(tiles)]

    def gather_of(source, place, sems, u):
        def piece(k):
            return place.at[u // 2, rows_at((u % 2) * tile + k * quarter, quarter)]

        def half(k, h):
            start = (u % 2) * tile + k * quarter + h * (quarter // 2)
            return place.at[u // 2, rows_at(start, quarter // 2)]

        return RowGather(source.at[u], piece, half, sems.at[u]), piece(t)

    def own_copy(source, place, i, u):
        return pltpu.make_async_copy(source.at[u], place, osems.at[i, u])

    pairs = [gather_of(gq, gt_hbm, asems, u) for u in range(tiles)]
    gathers = [g for g, _ in pairs]
    own_rows = [own_copy(gq, p, 0, u) for u, (_, p) in enumerate(pairs)]
    pairs = [gather_of(block_hbm, bo_hbm, asems2, u) for u in range(tiles)]
    out_gathers = [g for g, _ in pairs]
    own_rows += [own_copy(block_hbm, p, 1, u) for u, (_, p) in enumerate(pairs)]

    gate_loads = [
        pltpu.make_async_copy(src, gload.at[i], hsems.at[i])
        for i, src in enumerate(
            (gsum_hbm.at[1, 2], gland_hbm.at[1, 0], gsum_hbm.at[1, 3], gland_hbm.at[1, 1])
        )
    ]
    gate_out = pltpu.make_async_remote_copy(
        gload.at[0], gfar, fsems.at[0], fsems.at[1], device_id=far_z, device_id_type=MESH
    )
    up_loads = [
        pltpu.make_async_copy(gsum_hbm.at[2, 2 + i], uload.at[i], hsems.at[4 + i]) for i in range(2)
    ]
    up_near = [
        pltpu.make_async_remote_copy(
            gsum_hbm.at[2, k], uland.at[k], usems.at[0, k], usems.at[1, k], device_id=near_z, device_id_type=MESH
        )
        for k in range(2)
    ]
    up_out = pltpu.make_async_remote_copy(
        uload.at[0], ufar, usems.at[0, 2], usems.at[1, 2], device_id=far_z, device_id_type=MESH
    )
    for c in gate_loads + up_loads:
        c.start()

    def pass_up():
        up_near[0].wait_recv()
        up_loads[0].wait()
        uload[0] = (uload[0].astype(F32) + uland[0].astype(F32)).astype(BF16)
        up_out.start()


    half_rows = width // 2
    chunk = half_rows // nz
    spans = [pl.ds(0, heads * LANES), pl.ds(heads * LANES, 2 * heads * F + heads * LANES)]

    def product(p, base):
        at = rows_at(base, half_rows)
        if p == 0:
            return dot(gat[at], yb[...])
        return jnp.concatenate([dot(h1t[at], gqkb[...]), dot(h1t[at], gvb[...])], axis=1)

    def to_mate(p):
        return pltpu.make_async_remote_copy(
            stage.at[:, spans[p]],
            land.at[:, spans[p]],
            msems.at[0, p],
            msems.at[1, p],
            device_id=mate,
            device_id_type=MESH,
        )

    def to_near(p, k):
        return pltpu.make_async_remote_copy(
            total.at[rows_at((z ^ (3, 1)[k]) * chunk, chunk), spans[p]],
            zland.at[k, :, spans[p]],
            dsems.at[0, p, k],
            dsems.at[1, p, k],
            device_id=near_z,
            device_id_type=MESH,
        )

    def to_far(p):
        return pltpu.make_async_remote_copy(
            zsum.at[:, spans[p]],
            zland.at[2, :, spans[p]],
            dsems.at[0, p, 2],
            dsems.at[1, p, 2],
            device_id=far_z,
            device_id_type=MESH,
        )

    def pass_on(p):
        to_near(p, 0).wait_recv()
        mine = total[rows_at((z ^ 2) * chunk, chunk), spans[p]].astype(F32)
        zsum[:, spans[p]] = (mine + zland[0, :, spans[p]].astype(F32)).astype(BF16)
        to_far(p).start()

    def conclude(p):
        to_near(p, 1).wait_recv()
        to_far(p).wait_recv()
        out = total[rows_at(z * chunk, chunk), spans[p]].astype(F32)
        grads_ref[:, spans[p]] = (
            out + zland[1, :, spans[p]].astype(F32) + zland[2, :, spans[p]].astype(F32)
        )
        for k in range(2):
            to_near(p, k).wait_send()
        to_far(p).wait_send()
        to_mate(p).wait_send()

    def send_half(p):
        stage[:, spans[p]] = product(p, (1 - side) * half_rows).astype(BF16)
        to_mate(p).start()

    def sum_half(p):
        out = product(p, side * half_rows)
        to_mate(p).wait_recv()
        total[:, spans[p]] = (out + land[:, spans[p]].astype(F32)).astype(BF16)
        for k in range(2):
            to_near(p, k).start()

    def tokens(b):
        quarters[b].wait()
        grad, gain_grad = norm_backward(xq[b].astype(F32), scatters[b].total(), gain)
        gq[b] = (grad + gr_ref[b]).astype(BF16)
        gathers[b].start()
        own_rows[b].start()
        if b == 0:
            gsend[0] = jnp.concatenate(
                [gain_grad, gains_ref[...], jnp.zeros((6, width), F32)], axis=0
            )
        else:
            gsend[0, 0:1] += gain_grad

    gv[...] = jnp.zeros_like(gv)
    gqk[...] = jnp.zeros_like(gqk)
    mid = list(range(1, nz - 1))
    for g, c in zip(out_gathers, own_rows[tiles:]):
        g.start()
        c.start()
    value_grads(0)
    value_grads(1)
    states(0)
    chain(0, [0])
    local(0, 0)
    chain(0, mid[:1])
    local(0, 1)
    local(0, 2)
    chain(0, mid[1:])
    local(0, 3)
    for h in range(4, heads):
        local(0, h)
    value_grads(2)
    value_grads(3)
    states(1)
    chain(1, [0])
    for c in weights + gate_loads:
        c.wait()
    gload[0] = (gload[0].astype(F32) + gload[1].astype(F32)).astype(BF16)
    chain(0, [nz - 1])
    for h in range(heads):
        state_grads(0, h)
    norm_grads(0)
    scatters[0].start()
    scatters[1].start()
    chain(1, mid[:1])
    out_gathers[0].forward()
    out_gathers[1].forward()
    for h in range(heads):
        local(1, h)
        if h == heads // 2 - 1:
            chain(1, mid[1:])
    scatters[0].forward()
    scatters[1].forward()
    chain(1, [nz - 1])
    up_near[0].start()
    gate_out.start()
    up_near[1].start()
    for h in range(heads):
        state_grads(1, h)
    norm_grads(1)
    scatters[2].start()
    scatters[3].start()
    out_gathers[2].forward()
    out_gathers[3].forward()
    send_half(0)
    for i in range(2 * seqs):
        normed_rows(i)
    scatters[2].forward()
    scatters[3].forward()
    send_half(1)
    tokens(0)
    tokens(1)
    sum_half(0)
    sum_half(1)
    pass_up()
    tokens(2)
    gathers[0].forward()
    gathers[1].forward()
    tokens(3)

    def gain_copy(i, slot, to):
        return pltpu.make_async_remote_copy(
            gsend.at[i], gland.at[slot], ksems.at[0, slot], ksems.at[1, slot], device_id=to, device_id_type=MESH
        )

    hops = [
        [gain_copy(0, k, {"tensor": t ^ (k + 1)}) for k in range(3)],
        [gain_copy(1, 3, mate)],
        [gain_copy(2, 4 + k, others[k]) for k in range(nz - 1)],
    ]

    def gather_gains(i, first):
        out = gsend[i]
        for k, c in enumerate(hops[i]):
            c.wait()
            out = out + gland[first + k]
        if i < 2:
            gsend[i + 1] = out
            for c in hops[i + 1]:
                c.start()
        else:
            gains_out[...] = out

    for c in hops[0]:
        c.start()
    pass_on(0)
    gathers[2].forward()
    gathers[3].forward()
    gather_gains(0, 0)
    pass_on(1)
    gather_gains(1, 3)
    gate_out.wait()
    gate_ref[...] = gload[2].astype(F32) + gload[3].astype(F32) + gfar[...].astype(F32)
    up_near[1].wait_recv()
    up_out.wait()
    up_loads[1].wait()
    up_ref[...] = uload[1].astype(F32) + uland[1].astype(F32) + ufar[...].astype(F32)
    for c in up_near:
        c.wait_send()
    for p in range(2):
        conclude(p)
    gather_gains(2, 4)
    for c in own_rows:
        c.wait()
    for g in out_gathers + gathers:
        g.finish()
    for c in scatters:
        c.drain()

    @pl.when(z > 0)
    def _():
        for j in range(seqs * heads):
            send_down(j).wait_send()


def run_attention_backward(
    x, gain, qk, kq, v_ext, yx, pre, gattn, wo, wq, wk, wv, gr, gains, block_rows, gsum, gland, tables
):
    seqs, block, width = x.shape
    rows = seqs * block
    heads = wq.shape[0] // F
    tile = block // 2
    tiles, quarter = rows // tile, tile // 4
    nz = lax.axis_size("seq")
    spread, e1, e2, table = tables
    half = heads * F
    f1, f2 = jnp.roll(e1, half, 0), jnp.roll(e2, half, 0)
    chunk = width // 2 // nz
    cols = 2 * heads * LANES + 2 * heads * F
    shapes = [
        jax.ShapeDtypeStruct((chunk, cols), F32),
        jax.ShapeDtypeStruct((8, width), F32),
        jax.ShapeDtypeStruct(gsum.shape[2:], F32),
        jax.ShapeDtypeStruct(gsum.shape[2:], F32),
        jax.ShapeDtypeStruct(x.shape, BF16),
        jax.ShapeDtypeStruct(x.shape, BF16),
    ]
    vm, dma = pltpu.VMEM, pltpu.SemaphoreType.DMA
    wide = heads * LANES
    scratch = [
        vm((2 * half, width), BF16),
        vm(wv.shape, BF16),
        vm((tiles, quarter, width), F32),
        vm((rows, wide), BF16),
        vm((rows, wide), F32),
        vm((rows, wide), BF16),
        vm((rows, 2 * half), F32),
        vm((rows, 2 * half), BF16),
        vm((rows, wide), BF16),
        vm((width, rows), BF16),
        vm((width, rows), BF16),
        vm((seqs * heads, FEATS, LANES), F32),
        vm((seqs * heads, FEATS, LANES), BF16),
        vm((seqs * heads, FEATS, LANES), BF16),
        vm((2, tile, width), BF16),
        vm((tiles, quarter, width), BF16),
        vm((rows, width), BF16),
        vm((tiles, 2, quarter // 2, width), BF16),
        vm((tiles, 2, quarter, width), BF16),
        vm((tiles, quarter, width), BF16),
        vm((width // 2, cols), BF16),
        vm((width // 2, cols), BF16),
        vm((width // 2, cols), BF16),
        vm((3, chunk, cols), BF16),
        vm((chunk, cols), BF16),
        vm((4, 8, width), F32),
        vm((4 + nz - 1, 8, width), F32),
        vm((4,) + gsum.shape[2:], BF16),
        vm(gsum.shape[2:], BF16),
        vm((2,) + gsum.shape[2:], BF16),
        vm((2,) + gsum.shape[2:], BF16),
        vm(gsum.shape[2:], BF16),
        dma((6 + tiles,)),
        dma((2, seqs * heads)),
        dma((tiles, 2, 4)),
        dma((tiles, 2, 4)),
        dma((2, 2)),
        dma((2, 2, 3)),
        dma((2, 4 + nz - 1)),
        dma((tiles, 2, 4)),
        dma((2, tiles)),
        dma((6,)),
        dma((2,)),
        dma((2, 3)),
    ]
    return pl.pallas_call(
        functools.partial(attention_backward, nz),
        out_shape=shapes,
        in_specs=[ANY_SPEC] + [VMEM_SPEC] * 8 + [ANY_SPEC] * 4 + [VMEM_SPEC] + [ANY_SPEC] * 3 + [VMEM_SPEC] * 6,
        out_specs=[VMEM_SPEC] * 4 + [ANY_SPEC] * 2,
        scratch_shapes=scratch,
        compiler_params=pltpu.CompilerParams(
            collective_id=2, has_side_effects=True, vmem_limit_bytes=VMEM_LIMIT
        ),
        cost_estimate=pl.CostEstimate(
            flops=8 * rows * width * wide, bytes_accessed=30 << 20, transcendentals=0
        ),
        name="attention_backward",
    )(
        x,
        gain,
        qk,
        kq,
        v_ext,
        yx,
        pre,
        gattn,
        wo,
        wq,
        wk,
        wv,
        gr,
        gains,
        block_rows,
        gsum,
        gland,
        spread,
        e1,
        e2,
        f1,
        f2,
        table,
    )


def finish_kernel(gt_ref, bo_ref, gt_out, bo_out):
    gt_out[...] = gt_ref[...].astype(F32)
    bo_out[...] = bo_ref[...]


def finish(gt, bo):
    seqs, block, width = gt.shape
    spec = pl.BlockSpec((1, block // 4, width), lambda b, i: (b, i, 0))
    return pl.pallas_call(
        finish_kernel,
        grid=(seqs, 4),
        out_shape=[jax.ShapeDtypeStruct(gt.shape, F32), jax.ShapeDtypeStruct(bo.shape, BF16)],
        in_specs=[spec, spec],
        out_specs=[spec, spec],
        cost_estimate=pl.CostEstimate(flops=0, bytes_accessed=20 << 20, transcendentals=0),
        name="finish",
    )(gt, bo)


def shards(
    tokens,
    lengths,
    attn_gain,
    w_query,
    w_key,
    w_value,
    w_output,
    mlp_gain,
    w_gate,
    w_up,
    w_down,
    cotangent,
):
    seqs, block, width = tokens.shape
    heads = w_query.shape[1] // F
    value = w_value.shape[1] // heads
    chips = lax.axis_size("dp") // 2
    tables = (spread_table(heads, value),) + feature_tables(heads)
    wq, wk, wv = w_query.T, w_key.T, w_value.T
    qk, kq, pre, v_ext, yx, y, gh, gmt, yall, woall = run_attention_forward(
        tokens, attn_gain, wq, wk, wv, w_output, cotangent, w_down, lengths, tables
    )
    _, mlp_gain_grad, down_grads, block_rows, gr, gattn, gsum, _, gland = run_mlp(
        tokens, y, yall, w_output, woall, w_gate, w_up, w_down, gh, gmt, cotangent, mlp_gain, lengths
    )
    attn_grads, gains, gate_grads, up_grads, grad_tokens, block_out = run_attention_backward(
        tokens,
        attn_gain,
        qk,
        kq,
        v_ext,
        yx,
        pre,
        gattn,
        w_output,
        wq,
        wk,
        wv,
        gr,
        mlp_gain_grad,
        block_rows,
        gsum,
        gland,
        tables,
    )
    grad_tokens, block_out = finish(grad_tokens, block_out)
    if chips > 1:
        nz = lax.axis_size("seq")
        pairs = [[2 * i, 2 * i + 1] for i in range(chips)]

        def respread(a):
            a = lax.all_gather(a.astype(BF16), "seq", axis=0, tiled=True)
            a = lax.all_gather(a, "dp", axis=0, tiled=True, axis_index_groups=pairs)
            a = (a.astype(F32) * (0.5 / nz)).astype(BF16)
            return lax.psum_scatter(a, ("dp", "seq"), scatter_dimension=0, tiled=True).astype(F32)

        attn_grads, down_grads, gate_grads, up_grads = [
            respread(a) for a in (attn_grads, down_grads, gate_grads, up_grads)
        ]
        gains = lax.psum(gains, "dp") * 0.5
    share = width // (lax.axis_size("dp") * lax.axis_size("seq"))
    place = (lax.axis_index("dp") * lax.axis_size("seq") + lax.axis_index("seq")) * share
    gains = lax.dynamic_slice_in_dim(gains, place, share, 1)

    def unspread(a):
        return a.reshape(share, heads, LANES)[:, :, :value].reshape(share, heads * value)

    edge, half = heads * LANES, heads * F
    return (
        block_out,
        grad_tokens,
        gains[0],
        attn_grads[:, edge : edge + half],
        attn_grads[:, edge + half : edge + 2 * half],
        unspread(attn_grads[:, edge + 2 * half :]),
        unspread(attn_grads[:, :edge]).T,
        gains[1],
        gate_grads,
        up_grads,
        down_grads.T,
    )


def solution(mesh):
    in_specs = (
        P("dp", "seq", None),
        P("dp"),
        P(),
        P(None, "tensor"),
        P(None, "tensor"),
        P(None, "tensor"),
        P("tensor", None),
        P(),
        P(None, "tensor"),
        P(None, "tensor"),
        P("tensor", None),
        P("dp", "seq", None),
    )
    out_specs = (
        P("dp", "seq", None),
        P("dp", "seq", None),
        P(("dp", "seq")),
        P(("dp", "seq"), "tensor"),
        P(("dp", "seq"), "tensor"),
        P(("dp", "seq"), "tensor"),
        P("tensor", ("dp", "seq")),
        P(("dp", "seq")),
        P(("dp", "seq"), "tensor"),
        P(("dp", "seq"), "tensor"),
        P("tensor", ("dp", "seq")),
    )
    return jax.shard_map(shards, mesh=mesh, in_specs=in_specs, out_specs=out_specs, check_vma=False)
```

```python
import functools
import math

import jax
import jax.numpy as jnp
import numpy as np
from jax import lax
from jax.experimental import pallas as pl
from jax.experimental.pallas import tpu as pltpu
from jax.sharding import PartitionSpec as P

F = 16
FEATS = 160
LANES = 128
WIDE = 256
VMEM_LIMIT = 62 << 20
MESH = pl.DeviceIdType.MESH
BF16 = jnp.bfloat16
F32 = jnp.float32
VMEM_SPEC = pl.BlockSpec(memory_space=pltpu.VMEM)
ANY_SPEC = pl.BlockSpec(memory_space=pl.ANY)
NN = (((1,), (0,)), ((), ()))
NT = (((1,), (1,)), ((), ()))
TN = (((0,), (0,)), ((), ()))


def dot(a, b, dims=NN):
    return lax.dot_general(a, b, dims, preferred_element_type=F32)


def feature_tables(heads):
    upper_i, upper_j = np.triu_indices(F)
    pairs = len(upper_i)
    first = np.zeros((2 * heads * F, heads * WIDE), np.float32)
    second = np.zeros_like(first)
    rows = np.zeros((8, WIDE), np.float32)
    cols = np.arange(pairs)
    for h in range(heads):
        first[h * F + upper_i, h * WIDE + cols] = 1.0
        second[h * F + upper_j, h * WIDE + cols] = 1.0
        first[h * F + np.arange(F), h * WIDE + pairs + np.arange(F)] = 1.0
    rows[0, pairs + F] = 1.0
    rows[1, pairs : pairs + F + 1] = 1.0
    rows[2, :pairs] = np.where(upper_i == upper_j, 1.0 / (2 * F), 1.0 / F)
    rows[2, pairs : pairs + F] = 1.0 / math.sqrt(F)
    rows[2, pairs + F] = 1.0
    return tuple(jnp.asarray(a, BF16) for a in (first, second)) + (jnp.asarray(rows),)


def spread_table(heads, width):
    table = np.zeros((heads * width, heads * LANES), np.float32)
    for h in range(heads):
        table[h * width + np.arange(width), h * LANES + np.arange(width)] = 1.0
    return jnp.asarray(table, BF16)


def rows_at(start, count):
    return pl.ds(pl.multiple_of(start, 16), count)


class Gather:
    def __init__(self, source, slots, sems, half):
        me = lax.axis_index("tensor")
        self.x, self.y = {"tensor": me ^ 1}, {"tensor": me ^ 2}
        self.source, self.slots, self.sems, self.half = source, slots, sems, half
        self.first = [
            self.copy(source, slots(0), 0, self.x),
            self.copy(source, slots(1), 1, self.y),
        ]
        self.second = [
            self.copy(half(slots(0), 0), half(slots(2), 0), 2, self.y),
            self.copy(half(slots(1), 1), half(slots(2), 1), 3, self.x),
        ]

    def copy(self, src, dst, i, to):
        return pltpu.make_async_remote_copy(
            src, dst, self.sems.at[0, i], self.sems.at[1, i], device_id=to, device_id_type=MESH
        )

    def start(self):
        for c in self.first:
            c.start()

    def forward(self):
        for c, d in zip(self.first, self.second):
            c.wait_recv()
            d.start()

    def arrive(self):
        for d in self.second:
            d.wait_recv()

    def leave(self):
        for c in self.first + self.second:
            c.wait_send()

    def finish(self):
        self.arrive()
        self.leave()


def greet(devices):
    barrier = pltpu.get_barrier_semaphore()
    for d in devices:
        pl.semaphore_signal(barrier, inc=1, device_id=d, device_id_type=MESH)
    pl.semaphore_wait(barrier, len(devices))


def features(rows, first, second, table, scaled):
    a = dot(rows, first) + table[0:1]
    b = dot(rows, second) + table[1:2]
    out = a * b
    return out * table[2:3] if scaled else out


def head_of(rows, h):
    lane = lax.broadcasted_iota(jnp.int32, rows.shape, 1)
    return jnp.where(lane // F == h, rows, jnp.zeros_like(rows))


def attention_forward(
    nz,
    x_hbm,
    gain_ref,
    wq_hbm,
    wk_hbm,
    wv_ref,
    wo_ref,
    cot_hbm,
    wd_hbm,
    len_ref,
    spread_ref,
    e1_ref,
    e2_ref,
    table_ref,
    qk_ref,
    kq_ref,
    pre_ref,
    v_hbm,
    yx_hbm,
    y_hbm,
    gh_hbm,
    gmt_hbm,
    yall_ref,
    woall_ref,
    wqk_ref,
    x_ref,
    cot_ref,
    wd_ref,
    v_ref,
    yx_ref,
    y_ref,
    gh_ref,
    gmt_ref,
    sloc,
    pout,
    gsems,
    wsems,
    csems,
    zsems,
    lsems,
    osems,
):
    seqs, block, width = x_hbm.shape
    heads = wq_hbm.shape[0] // F
    value = wv_ref.shape[0] // heads
    z = lax.axis_index("seq")
    t = lax.axis_index("tensor")
    core = lax.axis_index("dp")
    side = lax.rem(core, 2)
    mate = {"dp": core + 1 - 2 * side}
    up, down = {"seq": lax.rem(z + 1, nz)}, {"seq": lax.rem(z + nz - 1, nz)}
    greet([{"tensor": t ^ 1}, {"tensor": t ^ 2}, mate, up, down])

    tile = block // 2
    x_loads = [
        pltpu.make_async_copy(
            x_hbm.at[i // 2, pl.ds((i % 2) * tile, tile)],
            x_ref.at[i // 2, pl.ds((i % 2) * tile, tile)],
            lsems.at[i],
        )
        for i in range(2 * seqs)
    ]
    late = [
        pltpu.make_async_copy(cot_hbm, cot_ref, lsems.at[2 * seqs]),
        pltpu.make_async_copy(wd_hbm, wd_ref, lsems.at[2 * seqs + 1]),
    ]
    half = heads * F
    joins = [
        pltpu.make_async_copy(w, wqk_ref.at[pl.ds(i * half, half)], lsems.at[2 * seqs + 2 + i])
        for i, w in enumerate((wq_hbm, wk_hbm))
    ]
    for c in joins + x_loads + late:
        c.start()

    wrows = wo_ref.shape[0] // 4
    cut = wrows // 32 * 16 + 16
    zbit = lax.rem(z, 2)

    def part(s, zb):
        return woall_ref.at[s, rows_at((2 * side + zb) * wrows, wrows)]

    wo = Gather(
        wo_ref.at[rows_at((2 * side + zbit) * wrows, wrows)],
        lambda s: part(s, zbit),
        wsems,
        lambda ref, i: ref.at[pl.ds(0, cut)] if i == 0 else ref.at[pl.ds(cut, wrows - cut)],
    )
    wo.start()

    def share(s, i):
        ref = part(s, zbit if i < 2 else 1 - zbit)
        to = {"seq": z ^ 1} if i == 1 else mate
        return pltpu.make_async_remote_copy(
            ref, ref, csems.at[0, 3 * i + s], csems.at[1, 3 * i + s], device_id=to, device_id_type=MESH
        )

    gain = gain_ref[...].reshape(1, width)
    table = table_ref[...]
    ones = jnp.where(
        lax.rem(lax.broadcasted_iota(jnp.int32, (1, heads * LANES), 1), LANES) == value, 1.0, 0.0
    )
    def project(b, i):
        at = pl.ds(i * tile, tile)
        flat = pl.ds(b * block + i * tile, tile)
        x_loads[2 * b + i].wait()
        rows = x_ref[b, at].astype(F32)
        normed = rows * lax.rsqrt(jnp.mean(rows * rows, axis=-1, keepdims=True) + 1e-06)
        normed = (normed * gain).astype(BF16)
        qk = dot(normed, wqk_ref[...], NT)
        qk_ref[flat] = qk.astype(BF16)
        kq_ref[flat] = pltpu.roll(qk, heads * F, 1).astype(BF16)
        values = dot(normed, wv_ref[...], NT).astype(BF16)
        v_ref[flat] = (dot(values, spread_ref[...]) + ones).astype(BF16)

    def lanes(h, n):
        return pl.ds(h * n, n)

    def states(b):
        flat = pl.ds(b * block, block)
        for h in range(heads):
            wide = lanes(h, WIDE)
            phi = features(kq_ref[flat], e1_ref[:, wide], e2_ref[:, wide], table, False)
            s = dot(phi.astype(BF16), v_ref[flat, lanes(h, LANES)], TN)
            sloc[b * heads + h] = s[:FEATS]

    def send_up(j):
        return pltpu.make_async_remote_copy(
            pout.at[j],
            pre_ref.at[j],
            zsems.at[0, j],
            zsems.at[1, j],
            device_id=up,
            device_id_type=MESH,
        )

    def chain(b, who):
        for at in who:

            @pl.when(z == at)
            def _():
                for h in range(heads):
                    j = b * heads + h
                    if at == 0:
                        pre_ref[j] = jnp.zeros((FEATS, LANES), BF16)
                        pout[j] = sloc[j].astype(BF16)
                    else:
                        send_up(j).wait_recv()
                        if at < nz - 1:
                            pout[j] = (sloc[j] + pre_ref[j].astype(F32)).astype(BF16)
                    if at < nz - 1:
                        send_up(j).start()

    def attend(b, h):
        narrow = lanes(h, LANES)
        wide = lanes(h, WIDE)
        for i in range(2):
            span = (i + 1) * tile
            at = pl.ds(b * block + i * tile, tile)
            until = pl.ds(b * block, span)
            rows = qk_ref[at]
            s = dot(head_of(rows, h), kq_ref[until], NT)
            w = 1.0 + s * (1.0 / math.sqrt(F))
            w = 0.5 * (w * w) + 0.5
            row = lax.broadcasted_iota(jnp.int32, w.shape, 0) + i * tile
            col = lax.broadcasted_iota(jnp.int32, w.shape, 1)
            w = jnp.where(col <= row, w, 0.0).astype(BF16)
            num = dot(w, v_ref[until, narrow])
            phi = features(rows, e1_ref[:, wide], e2_ref[:, wide], table, True)
            num = num + dot(phi[:, :FEATS].astype(BF16), pre_ref[b * heads + h])
            recip = 1.0 / num[:, value : value + 1]
            lane = lax.broadcasted_iota(jnp.int32, num.shape, 1)
            yx_ref[at, narrow] = jnp.where(lane == value, recip, num * recip)

    def gather(b):
        flat = pl.ds(b * block, block)
        return Gather(
            y_ref.at[flat],
            lambda s: yall_ref.at[s, flat],
            gsems.at[b],
            lambda ref, i: ref.at[pl.ds(i * tile, tile)],
        )

    def pack(b):
        for i in range(2):
            at = pl.ds(b * block + i * tile, tile)
            y_ref[at] = dot(yx_ref[at].astype(BF16), spread_ref[...], NT).astype(BF16)

    def put(src, dst, i):
        return pltpu.make_async_copy(src, dst, osems.at[i])

    def hidden_outs(i):
        at = pl.ds(i * tile, tile)
        return [
            put(gh_ref.at[at], gh_hbm.at[at], 2 * i),
            put(gmt_ref.at[:, at], gmt_hbm.at[:, at], 2 * i + 1),
        ]

    first_out = 4 * seqs
    outs = [
        put(v_ref, v_hbm, first_out),
        put(yx_ref, yx_hbm, first_out + 1),
        put(y_ref, y_hbm, first_out + 2),
    ]

    def hidden_grads(i):
        b, local = i // 2, i % 2
        at = z * block + local * tile + lax.broadcasted_iota(jnp.int32, (tile, 1), 0)
        mask = (at < len_ref[b]).astype(F32)
        gm = (cot_ref[b, pl.ds(local * tile, tile)].astype(F32) * mask).astype(BF16)
        gmt_ref[:, pl.ds(i * tile, tile)] = gm.T
        gh_ref[pl.ds(i * tile, tile)] = dot(gm, wd_ref[...], NT).astype(BF16)
        for c in hidden_outs(i):
            c.start()

    gathers = [gather(b) for b in range(seqs)]
    mid = list(range(1, nz - 1))
    for c in joins:
        c.wait()
    for b in range(seqs + 1):
        if b < seqs:
            for i in range(2):
                project(b, i)
                if b > 0 and i == 0:
                    chain(b - 1, mid[:1])
            if b > 0:
                chain(b - 1, mid[1:])
                wo.forward()
                for s in range(2):
                    share(s, 0).start()
            states(b)
            chain(b, [0])
        if b > 0:
            chain(b - 1, [nz - 1])
            if b == seqs:
                for s in range(2):
                    share(s, 1).start()
            for h in range(heads):
                attend(b - 1, h)
                if b == seqs - 1:
                    chain(b, mid[h : h + 1] if h < heads - 1 else mid[h:])
            pack(b - 1)
            gathers[b - 1].start()
    for c in outs:
        c.start()
    wo.arrive()
    share(2, 0).start()
    share(2, 1).start()
    for c in late:
        c.wait()
    hidden_grads(0)
    gathers[0].forward()
    for i in range(1, 2 * seqs):
        hidden_grads(i)
    for g in gathers[1:]:
        g.forward()
    for s in range(2):
        share(s, 1).wait_recv()
        share(s, 2).start()
    share(2, 1).wait_recv()
    share(2, 2).start()
    for c in outs:
        c.wait()
    for i in range(2 * seqs):
        for c in hidden_outs(i):
            c.wait()
    wo.leave()
    for g in gathers:
        g.finish()
    for s in range(3):
        share(s, 0).wait()
        share(s, 1).wait_send()
        share(s, 2).wait()

    @pl.when(z < nz - 1)
    def _():
        for j in range(seqs * heads):
            send_up(j).wait_send()


def run_attention_forward(x, gain, wq, wk, wv, wo, cot, wd, lengths, tables):
    seqs, block, width = x.shape
    heads = wq.shape[0] // F
    value = wv.shape[0] // heads
    rows = seqs * block
    spread, e1, e2, table = tables
    shape = jax.ShapeDtypeStruct
    wide, ff = heads * LANES, wd.shape[0]
    shapes = [
        shape((rows, 2 * heads * F), BF16),
        shape((rows, 2 * heads * F), BF16),
        shape((seqs * heads, FEATS, LANES), BF16),
        shape((rows, wide), BF16),
        shape((rows, wide), F32),
        shape((rows, heads * value), BF16),
        shape((rows, ff), BF16),
        shape((width, rows), BF16),
        shape((3, rows, heads * value), BF16),
        shape((3,) + wo.shape, BF16),
    ]
    vm, dma = pltpu.VMEM, pltpu.SemaphoreType.DMA
    smem = pl.BlockSpec(memory_space=pltpu.SMEM)
    return pl.pallas_call(
        functools.partial(attention_forward, lax.axis_size("seq")),
        out_shape=shapes,
        in_specs=[ANY_SPEC, VMEM_SPEC] + [ANY_SPEC] * 2 + [VMEM_SPEC] + [ANY_SPEC] * 3 + [smem] + [VMEM_SPEC] * 4,
        out_specs=[VMEM_SPEC] * 3 + [ANY_SPEC] * 7,
        scratch_shapes=[
            vm((2 * heads * F, width), BF16),
            vm(x.shape, BF16),
            vm(x.shape, BF16),
            vm(wd.shape, BF16),
            vm((rows, wide), BF16),
            vm((rows, wide), F32),
            vm((rows, heads * value), BF16),
            vm((rows, ff), BF16),
            vm((width, rows), BF16),
            vm((seqs * heads, FEATS, LANES), F32),
            vm((seqs * heads, FEATS, LANES), BF16),
            dma((seqs, 2, 4)),
            dma((2, 4)),
            dma((2, 9)),
            dma((2, seqs * heads)),
            dma((2 * seqs + 4,)),
            dma((4 * seqs + 3,)),
        ],
        compiler_params=pltpu.CompilerParams(
            collective_id=0, has_side_effects=True, vmem_limit_bytes=VMEM_LIMIT
        ),
        cost_estimate=pl.CostEstimate(
            flops=2 * rows * width * heads * (2 * F + value), bytes_accessed=20 << 20, transcendentals=0
        ),
        name="attention_forward",
    )(x, gain, wq, wk, wv, wo, cot, wd, lengths, spread, e1, e2, table)


class Exchange:
    def __init__(self, sems):
        me = lax.axis_index("tensor")
        self.x, self.y = {"tensor": me ^ 1}, {"tensor": me ^ 2}
        self.sems = sems

    def copy(self, src, dst, i, to):
        return pltpu.make_async_remote_copy(
            src, dst, self.sems.at[0, i], self.sems.at[1, i], device_id=to, device_id_type=MESH
        )


class ReduceScatter(Exchange):
    def __init__(self, part, near, far, sems):
        super().__init__(sems)
        me = lax.axis_index("tensor")
        self.part, self.near, self.far = part, near, far
        self.q = q = near[0].shape[0] * 2
        self.half = q // 2
        self.at = [me * q, (me ^ 1) * q, (me ^ 2) * q, (me ^ 3) * q]
        over = self.at[3]
        self.first = [
            self.copy(part.at[rows_at(over, self.half)], near[0], 0, self.x),
            self.copy(part.at[rows_at(over + self.half, self.half)], near[1], 1, self.y),
        ]
        self.second = [
            self.copy(part.at[rows_at(self.at[2], q)], far[1], 2, self.y),
            self.copy(part.at[rows_at(self.at[1], q)], far[0], 3, self.x),
        ]

    def start(self):
        for c in self.first:
            c.start()

    def forward(self):
        for i, start in ((0, self.at[2]), (1, self.at[1] + self.half)):
            self.first[i].wait_recv()
            rows = rows_at(start, self.half)
            self.part[rows] = (self.part[rows].astype(F32) + self.near[i][...].astype(F32)).astype(BF16)
            self.second[i].start()

    def total(self):
        for c in self.second:
            c.wait_recv()
        mine = self.part[rows_at(self.at[0], self.q)].astype(F32)
        return mine + self.far[0][...].astype(F32) + self.far[1][...].astype(F32)

    def drain(self):
        for c in self.first + self.second:
            c.wait_send()


class RowGather(Exchange):
    def __init__(self, source, piece, half, sems):
        super().__init__(sems)
        me = lax.axis_index("tensor")
        self.first = [
            self.copy(source, piece(me), 0, self.x),
            self.copy(source, piece(me), 1, self.y),
        ]
        self.second = [
            self.copy(half(me ^ 1, 0), half(me ^ 1, 0), 2, self.y),
            self.copy(half(me ^ 2, 1), half(me ^ 2, 1), 3, self.x),
        ]

    start = Gather.start
    forward = Gather.forward
    arrive = Gather.arrive
    leave = Gather.leave
    finish = Gather.finish


def norm_backward(rows, grad, gain):
    norm = lax.rsqrt(jnp.mean(rows * rows, axis=-1, keepdims=True) + 1e-06)
    unit = rows * norm
    gain_grad = jnp.sum(grad * unit, axis=0, keepdims=True)
    scaled = grad * gain
    mean = jnp.mean(scaled * unit, axis=-1, keepdims=True)
    return norm * (scaled - unit * mean), gain_grad


def own_rows(value, t, count):
    parts = [value[i * count : (i + 1) * count] for i in range(4)]
    low = jnp.where(t == 0, parts[0], parts[1])
    return jnp.where(t < 2, low, jnp.where(t == 2, parts[2], parts[3]))


def mlp_kernel(
    nz,
    x_hbm,
    y_hbm,
    yall_hbm,
    wo_hbm,
    woall_hbm,
    wg_hbm,
    wu_hbm,
    wd_hbm,
    gh_hbm,
    gmt_hbm,
    cot_hbm,
    gain_ref,
    len_ref,
    gain_grad_ref,
    down_ref,
    block_hbm,
    gr_hbm,
    gattn_hbm,
    gsum_hbm,
    land_hbm,
    zland_hbm,
    wo4,
    wg,
    wu,
    wd,
    xt,
    yt,
    ght,
    h2t,
    gmt,
    gg,
    gu,
    hid,
    part,
    near,
    far,
    ga,
    r_ref,
    grs,
    stage,
    back,
    keep,
    lsems,
    rsems,
    asems,
    msems,
    bsems,
    dsems,
    osems,
    psems,
    free_sem,
):
    seqs, block, width = x_hbm.shape
    tile = xt.shape[0]
    per = block // tile
    quarter = tile // 4
    tiles = seqs * per
    z = lax.axis_index("seq")
    t = lax.axis_index("tensor")
    core = lax.axis_index("dp")
    side = lax.rem(core, 2)
    mate = {"dp": core + 1 - 2 * side}
    near_z, far_z = {"seq": z ^ 1}, {"seq": z ^ 2}
    greet([{"tensor": t ^ 1}, {"tensor": t ^ 2}, mate, near_z, far_z])
    gain = gain_ref[...].reshape(1, width)

    def load(src, dst, i):
        return pltpu.make_async_copy(src, dst, lsems.at[i])

    weights = [
        load(wo_hbm, wo4.at[0], 0),
        *[load(woall_hbm.at[s], wo4.at[s + 1], 1 + s) for s in range(3)],
        load(wg_hbm, wg, 4),
        load(wu_hbm, wu, 5),
    ]
    late = [load(gmt_hbm, gmt, 6), load(wd_hbm, wd, 7)]

    def xy_loads(i):
        b, at = i // per, lax.rem(i, per) * tile
        flat = rows_at(i * tile, tile)
        return [
            load(x_hbm.at[b, rows_at(at, tile)], xt, 8),
            load(y_hbm.at[flat], yt.at[0], 9),
            *[load(yall_hbm.at[s, flat], yt.at[s + 1], 10 + s) for s in range(3)],
        ]

    def g_load(i):
        return load(gh_hbm.at[rows_at(i * tile, tile)], ght, 13)

    def c_load(i):
        b, at = i // per, lax.rem(i, per) * tile + t * quarter
        return load(cot_hbm.at[b, rows_at(at, quarter)], ga.at[i], 14 + i)

    for c in xy_loads(0) + weights + [g_load(0)] + [c_load(i) for i in range(tiles)] + late:
        c.start()

    def scatter(i):
        return ReduceScatter(
            part.at[rows_at(i * tile, tile)],
            [near.at[i, k] for k in range(2)],
            [far.at[i, k] for k in range(2)],
            rsems.at[i],
        )

    def mlp_scatter(i):
        source = wo4.at[i, pl.ds(0, tile)]
        near_ref = [wo4.at[i, pl.ds(tile + k * (quarter // 2), quarter // 2)] for k in range(2)]
        far_ref = [wo4.at[i, pl.ds(tile + (k + 1) * quarter, quarter)] for k in range(2)]
        return ReduceScatter(source, near_ref, far_ref, psems.at[i])

    def gather(i):
        def piece(k):
            return gattn_hbm.at[rows_at(i * tile + k * quarter, quarter)]

        def half(k, h):
            start = i * tile + k * quarter + h * (quarter // 2)
            return gattn_hbm.at[rows_at(start, quarter // 2)]

        return RowGather(ga.at[i], piece, half, asems.at[i])

    def place(i):
        at = rows_at(i * tile + t * quarter, quarter)
        return [
            pltpu.make_async_copy(ga.at[i], gattn_hbm.at[at], osems.at[0, i]),
            pltpu.make_async_copy(grs, gr_hbm.at[i], osems.at[1, i]),
        ]

    def tile_step(i, first):
        flat = rows_at(i * tile, tile)
        for c in xy_loads(i):
            c.wait()
        if first:
            for c in weights[:4]:
                c.wait()
        r = xt[...].astype(F32)
        for s in range(4):
            r = r + dot(yt[s], wo4[s])

        @pl.when(i + 1 < tiles)
        def _():
            for c in xy_loads(i + 1):
                c.start()

        r_ref[i] = own_rows(r, t, quarter)
        h2 = r * lax.rsqrt(jnp.mean(r * r, axis=-1, keepdims=True) + 1e-06) * gain
        h2 = h2.astype(BF16)
        h2t[:, pl.ds(pl.multiple_of(i * tile, LANES), tile)] = h2.T
        if first:
            for c in weights[4:6]:
                c.wait()
        gate = dot(h2, wg[...], NT)
        up = dot(h2, wu[...], NT)
        if not first:
            scatter(i - 1).forward()
        g_load(i).wait()
        gh = ght[...].astype(F32)
        sig = 1.0 / (1.0 + jnp.exp(-gate))
        silu = gate * sig
        hid[flat] = (silu * up).astype(BF16)
        gg[flat] = (gh * up * (sig * (1.0 + gate * (1.0 - sig)))).astype(BF16)
        gu[flat] = (gh * silu).astype(BF16)

        @pl.when(i + 1 < tiles)
        def _():
            g_load(i + 1).start()

        part[flat] = (dot(gg[flat], wg[...]) + dot(gu[flat], wu[...])).astype(BF16)
        scatter(i).start()

    def mixed(i, first):
        b = i // per
        grad = scatter(i).total()
        c_load(i).wait()
        at = z * block + lax.rem(i, per) * tile + t * quarter
        at = at + lax.broadcasted_iota(jnp.int32, (quarter, 1), 0)
        out = ga[i].astype(F32) * (at < len_ref[b]).astype(F32)
        gr, gain_grad = norm_backward(r_ref[i], grad, gain)
        gr = gr + out
        if first:
            gain_grad_ref[...] = gain_grad
        else:
            gain_grad_ref[...] += gain_grad
            place(i - 1)[1].wait()
        grs[...] = gr
        ga[i] = gr.astype(BF16)
        gather(i).start()
        for c in place(i):
            c.start()

    tile_step(0, True)

    def rest(i, carry):
        tile_step(i, False)
        return carry

    lax.fori_loop(1, tiles - 1, rest, 0)
    mixed(0, True)
    tile_step(tiles - 1, False)

    lefts = (gmt, h2t, h2t)
    rights = (hid, gg, gu)
    half_rows = width // 2
    chunk = back.shape[0]
    last = tiles - 1

    def product(n, base, m):
        return dot(lefts[n][rows_at(base + m * chunk, chunk)], rights[n][...])

    def to_mate(n, m, slot):
        return pltpu.make_async_remote_copy(
            stage.at[slot],
            land_hbm.at[n, m],
            msems.at[0, slot],
            msems.at[1, n * nz + m],
            device_id=mate,
            device_id_type=MESH,
        )

    def from_mate(n, m):
        return pltpu.make_async_copy(land_hbm.at[n, m], back, bsems.at[0])

    def to_sum(n, m, slot):
        return pltpu.make_async_copy(stage.at[slot], gsum_hbm.at[n, m], bsems.at[slot - 1])

    across = [
        pltpu.make_async_remote_copy(
            gsum_hbm.at[n, k],
            zland_hbm.at[n, k],
            dsems.at[0, 2 * n + k],
            dsems.at[1, 2 * n + k],
            device_id=near_z,
            device_id_type=MESH,
        )
        for n in range(2)
        for k in range(2)
    ]
    beyond = pltpu.make_async_remote_copy(
        keep, zland_hbm.at[0, 2], dsems.at[0, 4], dsems.at[1, 4], device_id=far_z, device_id_type=MESH
    )

    def landed(k):
        c = pltpu.make_async_copy(zland_hbm.at[0, k], back, bsems.at[0])
        c.start()
        c.wait()
        return back[...].astype(F32)

    def pass_on():
        across[0].wait_recv()
        keep[...] = (keep[...].astype(F32) + landed(0)).astype(BF16)
        beyond.start()

    def step_mlp(i):
        flat = rows_at(i * tile, tile)
        wo4[i, :tile] = dot(hid[flat], wd[...]).astype(BF16)
        mlp_scatter(i).start()

    def block_out(i):
        return pltpu.make_async_copy(ga.at[i], block_hbm.at[i], osems.at[0, i])

    def block_rows(i):
        b = i // per
        at = z * block + lax.rem(i, per) * tile + t * quarter
        at = at + lax.broadcasted_iota(jnp.int32, (quarter, 1), 0)
        mask = (at < len_ref[b]).astype(F32)
        ga[i] = (mask * (r_ref[i] + mlp_scatter(i).total())).astype(BF16)
        block_out(i).start()

    for to in ({"tensor": t ^ 1}, {"tensor": t ^ 2}):
        pl.semaphore_signal(free_sem, inc=1, device_id=to, device_id_type=MESH)
    late[0].wait()
    late[1].wait()
    steps = {
        2: lambda: (gather(0).forward(), mixed(1, False)),
        3: lambda: scatter(last).forward(),
        4: lambda: (mixed(last - 1, False), pl.semaphore_wait(free_sem, 2)),
        5: lambda: step_mlp(0),
        6: lambda: step_mlp(1),
        7: lambda: step_mlp(2),
        8: lambda: step_mlp(3),
        9: lambda: gather(1).forward(),
        11: lambda: mixed(last, False),
        13: lambda: gather(last - 1).forward(),
        16: lambda: mlp_scatter(0).forward(),
        17: lambda: (gather(last).forward(), mlp_scatter(1).forward()),
        18: lambda: mlp_scatter(2).forward(),
        19: lambda: mlp_scatter(3).forward(),
    }
    count = 0

    def step():
        nonlocal count
        steps.get(count, lambda: None)()
        count += 1

    order = [z ^ 3, z ^ 1, z ^ 2, z]
    for n in range(3):

        def for_mate(k):
            if k >= 2:
                to_mate(n, order[k - 2], k % 2).wait_send()
            stage[k % 2] = product(n, (1 - side) * half_rows, order[k]).astype(BF16)
            to_mate(n, order[k], k % 2).start()
            step()

        def for_own(k):
            m = order[k]
            to_mate(n, m, 0).wait_recv()
            from_mate(n, m).start()
            out = product(n, side * half_rows, m)
            from_mate(n, m).wait()
            out = out + back[...].astype(F32)
            if n == 0 and k == 2:
                keep[...] = out.astype(BF16)
            elif n == 0 and k == 3:
                down_ref[...] = out
            else:
                if k > 0 and (n == 2 or k == 3):
                    to_sum(n, k - 1, 2).wait()
                stage[2] = out.astype(BF16)
                to_sum(n, k, 2).start()
            if n < 2 and k < 2:
                to_sum(n, k, 2).wait()
                across[2 * n + k].start()
            step()

        for_mate(0)
        for_mate(1)
        for_own(0)
        for_mate(2)
        for_own(1)
        for_mate(3)
        for_own(2)
        for_own(3)
        for k in range(nz - 2, nz):
            to_mate(n, order[k], k % 2).wait_send()
        if n > 0:
            to_sum(n, nz - 1, 2).wait()
        if n == 1:
            pass_on()
    across[1].wait_recv()
    down_ref[...] += landed(1)
    place(last)[1].wait()
    for i in range(tiles):
        place(i)[0].wait()
        gather(i).finish()
        scatter(i).drain()
    for c in across:
        c.wait_send()
    for i in range(tiles):
        block_rows(i)
        mlp_scatter(i).drain()
    for i in range(tiles):
        block_out(i).wait()
    for c in across[2:]:
        c.wait_recv()
    beyond.wait_recv()
    down_ref[...] += landed(2)
    beyond.wait_send()


def run_mlp(x, y, yall, wo, woall, wg, wu, wd, gh, gmt, cot, gain, lengths):
    seqs, block, width = x.shape
    rows = seqs * block
    nz = lax.axis_size("seq")
    value, ff = wo.shape[0], wd.shape[0]
    tile = block // 2
    tiles, quarter = rows // tile, tile // 4
    chunk = width // 2 // nz
    shape = jax.ShapeDtypeStruct
    shapes = [
        shape((1, width), F32),
        shape((chunk, ff), F32),
        shape((tiles, quarter, width), BF16),
        shape((tiles, quarter, width), F32),
        shape((rows, width), BF16),
        shape((3, 4, chunk, ff), BF16),
        shape((3, nz, chunk, ff), BF16),
        shape((2, 3, chunk, ff), BF16),
    ]
    vm, dma = pltpu.VMEM, pltpu.SemaphoreType.DMA
    scratch = [
        vm((4, value, width), BF16),
        vm((ff, width), BF16),
        vm((ff, width), BF16),
        vm((ff, width), BF16),
        vm((tile, width), BF16),
        vm((4, tile, value), BF16),
        vm((tile, ff), BF16),
        vm((width, rows), BF16),
        vm((width, rows), BF16),
        vm((rows, ff), BF16),
        vm((rows, ff), BF16),
        vm((rows, ff), BF16),
        vm((rows, width), BF16),
        vm((tiles, 2, quarter // 2, width), BF16),
        vm((tiles, 2, quarter, width), BF16),
        vm((tiles, quarter, width), BF16),
        vm((tiles, quarter, width), F32),
        vm((quarter, width), F32),
        vm((3, chunk, ff), BF16),
        vm((chunk, ff), BF16),
        vm((chunk, ff), BF16),
        dma((14 + tiles,)),
        dma((tiles, 2, 4)),
        dma((tiles, 2, 4)),
        dma((2, 3 * nz)),
        dma((3,)),
        dma((2, 5)),
        dma((2, tiles)),
        dma((tiles, 2, 4)),
        pltpu.SemaphoreType.REGULAR,
    ]
    return pl.pallas_call(
        functools.partial(mlp_kernel, nz),
        out_shape=shapes,
        in_specs=[ANY_SPEC] * 11 + [VMEM_SPEC, pl.BlockSpec(memory_space=pltpu.SMEM)],
        out_specs=[VMEM_SPEC] * 2 + [ANY_SPEC] * 6,
        scratch_shapes=scratch,
        compiler_params=pltpu.CompilerParams(
            collective_id=1, has_side_effects=True, vmem_limit_bytes=VMEM_LIMIT
        ),
        cost_estimate=pl.CostEstimate(
            flops=2 * rows * width * (4 * value + 8 * ff), bytes_accessed=60 << 20, transcendentals=0
        ),
        name="mlp_forward_backward",
    )(x, y, yall, wo, woall, wg.T, wu.T, wd, gh, gmt, cot, gain, lengths)


def attention_backward(
    nz,
    x_hbm,
    gain_ref,
    qk_ref,
    kq_ref,
    v_ref,
    yx_ref,
    pre_ref,
    gattn_ref,
    wo_ref,
    wq_hbm,
    wk_hbm,
    wv_hbm,
    gr_hbm,
    gains_ref,
    block_hbm,
    gsum_hbm,
    gland_hbm,
    spread_ref,
    e1_ref,
    e2_ref,
    f1_ref,
    f2_ref,
    table_ref,
    grads_ref,
    gains_out,
    gate_ref,
    up_ref,
    gt_hbm,
    bo_hbm,
    wqk_ref,
    wv_ref,
    gr_ref,
    gn,
    gv,
    gvb,
    gqk,
    gqkb,
    yb,
    gat,
    h1t,
    sloc,
    sout,
    suf,
    xt,
    xq,
    part,
    near,
    far,
    gq,
    stage,
    land,
    total,
    zland,
    zsum,
    gsend,
    gland,
    gload,
    gfar,
    uload,
    uland,
    ufar,
    lsems,
    zsems,
    rsems,
    asems,
    msems,
    dsems,
    ksems,
    asems2,
    osems,
    hsems,
    fsems,
    usems,
):
    seqs, block, width = x_hbm.shape
    heads = wq_hbm.shape[0] // F
    value = wv_hbm.shape[0] // heads
    tile = block // 2
    quarter = tile // 4
    rows = seqs * block
    tiles = rows // tile
    z = lax.axis_index("seq")
    t = lax.axis_index("tensor")
    core = lax.axis_index("dp")
    side = lax.rem(core, 2)
    mate = {"dp": core + 1 - 2 * side}
    others = [{"seq": lax.rem(z + k, nz)} for k in range(1, nz)]
    greet([{"tensor": t ^ k} for k in (1, 2, 3)] + [mate] + others)
    down = others[-1]
    near_z, far_z = {"seq": z ^ 1}, {"seq": z ^ 2}
    gain = gain_ref[...].reshape(1, width)
    table = table_ref[...]
    scale = table[2:3, :FEATS]

    def lanes(h, n):
        return pl.ds(h * n, n)

    def x_load(i):
        b, at = i // 2, (i % 2) * tile
        return pltpu.make_async_copy(x_hbm.at[b, pl.ds(at, tile)], xt.at[i % 2], lsems.at[i % 2])

    quarters = [
        pltpu.make_async_copy(
            x_hbm.at[u // 2, rows_at((u % 2) * tile + t * quarter, quarter)], xq.at[u], lsems.at[2 + u]
        )
        for u in range(tiles)
    ]
    x_load(0).start()
    x_load(1).start()
    weights = [
        pltpu.make_async_copy(src, dst, lsems.at[2 + tiles + i])
        for i, (src, dst) in enumerate(
            (
                (wq_hbm, wqk_ref.at[pl.ds(0, heads * F)]),
                (wk_hbm, wqk_ref.at[pl.ds(heads * F, heads * F)]),
                (wv_hbm, wv_ref),
                (gr_hbm, gr_ref),
            )
        )
    ]
    for c in quarters + weights:
        c.start()

    def value_grads(i):
        at = pl.ds(i * tile, tile)
        ga = gattn_ref[at]
        gy = dot(dot(ga, wo_ref[...], NT).astype(BF16), spread_ref[...])
        gat[:, pl.ds(i * tile, tile)] = ga.T
        yb[at] = yx_ref[at].astype(BF16)
        for h in range(heads):
            narrow = lanes(h, LANES)
            g, y = gy[:, h * LANES : (h + 1) * LANES], yx_ref[at, narrow]
            recip = y[:, value : value + 1]
            den = -jnp.sum(g * y, axis=-1, keepdims=True)
            lane = lax.broadcasted_iota(jnp.int32, g.shape, 1)
            gn[at, narrow] = (jnp.where(lane == value, den, g) * recip).astype(BF16)

    def expand(ref, at, h):
        a = dot(ref[at], e1_ref[:, h * WIDE : h * WIDE + FEATS]) + table[0:1, :FEATS]
        b = dot(ref[at], e2_ref[:, h * WIDE : h * WIDE + FEATS]) + table[1:2, :FEATS]
        return a, b

    def states(b):
        flat = pl.ds(b * block, block)
        for h in range(heads):
            a, c = expand(qk_ref, flat, h)
            phi = (a * c * scale).astype(BF16)
            sloc[b * heads + h] = dot(phi, gn[flat, lanes(h, LANES)], TN)

    def send_down(j):
        return pltpu.make_async_remote_copy(
            sout.at[j], suf.at[j], zsems.at[0, j], zsems.at[1, j], device_id=down, device_id_type=MESH
        )

    def chain(b, who):
        for at in who:

            @pl.when(z == nz - 1 - at)
            def _():
                for h in range(heads):
                    j = b * heads + h
                    if at == 0:
                        suf[j] = jnp.zeros((FEATS, LANES), BF16)
                        sout[j] = sloc[j].astype(BF16)
                    else:
                        send_down(j).wait_recv()
                        if at < nz - 1:
                            sout[j] = (sloc[j] + suf[j].astype(F32)).astype(BF16)
                    if at < nz - 1:
                        send_down(j).start()

    def contract(a, c, grad, h, first, second):
        wide = slice(h * WIDE, h * WIDE + FEATS)
        return dot((grad * c).astype(BF16), first[:, wide], NT) + dot(
            (grad * a).astype(BF16), second[:, wide], NT
        )

    def local(b, h):
        narrow = lanes(h, LANES)
        for i in range(2):
            span = (i + 1) * tile
            at = pl.ds(b * block + i * tile, tile)
            until = pl.ds(b * block, span)
            s = dot(head_of(qk_ref[at], h), kq_ref[until], NT)
            w = 1.0 + s * (1.0 / math.sqrt(F))
            row = lax.broadcasted_iota(jnp.int32, w.shape, 0) + i * tile
            col = lax.broadcasted_iota(jnp.int32, w.shape, 1)
            seen = col <= row
            kernel = jnp.where(seen, 0.5 * (w * w) + 0.5, 0.0).astype(BF16)
            grad = gn[at, narrow]
            gs = dot(grad, v_ref[until, narrow], NT) * (w * (1.0 / math.sqrt(F)))
            gs = jnp.where(seen, gs, 0.0).astype(BF16)
            gv[until, narrow] += dot(kernel, grad, TN)
            gqk[until] += dot(gs, head_of(kq_ref[at], heads + h), TN)
            a, c = expand(qk_ref, at, h)
            gphi = dot(grad, pre_ref[b * heads + h], NT) * scale
            gqk[at] += dot(gs, head_of(kq_ref[until], h)) + contract(a, c, gphi, h, e1_ref, e2_ref)

    def state_grads(b, h):
        narrow = lanes(h, LANES)
        flat = pl.ds(b * block, block)
        later = suf[b * heads + h]
        a, c = expand(kq_ref, flat, h)
        gphi = dot(v_ref[flat, narrow], later, NT)
        gqk[flat] += contract(a, c, gphi, h, f1_ref, f2_ref)
        gv[flat, narrow] += dot((a * c).astype(BF16), later)

    def norm_grads(b):
        for i in range(2):
            at = pl.ds(b * block + i * tile, tile)
            gvb[at] = gv[at].astype(BF16)
            gqkb[at] = gqk[at].astype(BF16)
            packed = dot(gvb[at], spread_ref[...], NT).astype(BF16)
            part[at] = (dot(gqkb[at], wqk_ref[...]) + dot(packed, wv_ref[...])).astype(BF16)

    def normed_rows(i):
        x_load(i).wait()
        r = xt[i % 2].astype(F32)
        h1 = r * lax.rsqrt(jnp.mean(r * r, axis=-1, keepdims=True) + 1e-06) * gain
        h1t[:, pl.ds(i * tile, tile)] = h1.astype(BF16).T
        if i + 2 < 2 * seqs:
            x_load(i + 2).start()

    def scatter_of(source, near_ref, far_ref, sems, u):
        return ReduceScatter(
            source.at[pl.ds(u * tile, tile)],
            [near_ref.at[u, k] for k in range(2)],
            [far_ref.at[u, k] for k in range(2)],
            sems.at[u],
        )

    scatters = [scatter_of(part, near, far, rsems, u) for u in range(tiles)]

    def gather_of(source, place, sems, u):
        def piece(k):
            return place.at[u // 2, rows_at((u % 2) * tile + k * quarter, quarter)]

        def half(k, h):
            start = (u % 2) * tile + k * quarter + h * (quarter // 2)
            return place.at[u // 2, rows_at(start, quarter // 2)]

        return RowGather(source.at[u], piece, half, sems.at[u]), piece(t)

    def own_copy(source, place, i, u):
        return pltpu.make_async_copy(source.at[u], place, osems.at[i, u])

    pairs = [gather_of(gq, gt_hbm, asems, u) for u in range(tiles)]
    gathers = [g for g, _ in pairs]
    own_rows = [own_copy(gq, p, 0, u) for u, (_, p) in enumerate(pairs)]
    pairs = [gather_of(block_hbm, bo_hbm, asems2, u) for u in range(tiles)]
    out_gathers = [g for g, _ in pairs]
    own_rows += [own_copy(block_hbm, p, 1, u) for u, (_, p) in enumerate(pairs)]

    gate_loads = [
        pltpu.make_async_copy(src, gload.at[i], hsems.at[i])
        for i, src in enumerate(
            (gsum_hbm.at[1, 2], gland_hbm.at[1, 0], gsum_hbm.at[1, 3], gland_hbm.at[1, 1])
        )
    ]
    gate_out = pltpu.make_async_remote_copy(
        gload.at[0], gfar, fsems.at[0], fsems.at[1], device_id=far_z, device_id_type=MESH
    )
    up_loads = [
        pltpu.make_async_copy(gsum_hbm.at[2, 2 + i], uload.at[i], hsems.at[4 + i]) for i in range(2)
    ]
    up_near = [
        pltpu.make_async_remote_copy(
            gsum_hbm.at[2, k], uland.at[k], usems.at[0, k], usems.at[1, k], device_id=near_z, device_id_type=MESH
        )
        for k in range(2)
    ]
    up_out = pltpu.make_async_remote_copy(
        uload.at[0], ufar, usems.at[0, 2], usems.at[1, 2], device_id=far_z, device_id_type=MESH
    )
    for c in gate_loads + up_loads:
        c.start()

    def pass_up():
        up_near[0].wait_recv()
        up_loads[0].wait()
        uload[0] = (uload[0].astype(F32) + uland[0].astype(F32)).astype(BF16)
        up_out.start()


    half_rows = width // 2
    chunk = half_rows // nz
    spans = [pl.ds(0, heads * LANES), pl.ds(heads * LANES, 2 * heads * F + heads * LANES)]

    def product(p, base):
        at = rows_at(base, half_rows)
        if p == 0:
            return dot(gat[at], yb[...])
        return jnp.concatenate([dot(h1t[at], gqkb[...]), dot(h1t[at], gvb[...])], axis=1)

    def to_mate(p):
        return pltpu.make_async_remote_copy(
            stage.at[:, spans[p]],
            land.at[:, spans[p]],
            msems.at[0, p],
            msems.at[1, p],
            device_id=mate,
            device_id_type=MESH,
        )

    def to_near(p, k):
        return pltpu.make_async_remote_copy(
            total.at[rows_at((z ^ (3, 1)[k]) * chunk, chunk), spans[p]],
            zland.at[k, :, spans[p]],
            dsems.at[0, p, k],
            dsems.at[1, p, k],
            device_id=near_z,
            device_id_type=MESH,
        )

    def to_far(p):
        return pltpu.make_async_remote_copy(
            zsum.at[:, spans[p]],
            zland.at[2, :, spans[p]],
            dsems.at[0, p, 2],
            dsems.at[1, p, 2],
            device_id=far_z,
            device_id_type=MESH,
        )

    def pass_on(p):
        to_near(p, 0).wait_recv()
        mine = total[rows_at((z ^ 2) * chunk, chunk), spans[p]].astype(F32)
        zsum[:, spans[p]] = (mine + zland[0, :, spans[p]].astype(F32)).astype(BF16)
        to_far(p).start()

    def conclude(p):
        to_near(p, 1).wait_recv()
        to_far(p).wait_recv()
        out = total[rows_at(z * chunk, chunk), spans[p]].astype(F32)
        grads_ref[:, spans[p]] = (
            out + zland[1, :, spans[p]].astype(F32) + zland[2, :, spans[p]].astype(F32)
        )
        for k in range(2):
            to_near(p, k).wait_send()
        to_far(p).wait_send()
        to_mate(p).wait_send()

    def send_half(p):
        stage[:, spans[p]] = product(p, (1 - side) * half_rows).astype(BF16)
        to_mate(p).start()

    def sum_half(p):
        out = product(p, side * half_rows)
        to_mate(p).wait_recv()
        total[:, spans[p]] = (out + land[:, spans[p]].astype(F32)).astype(BF16)
        for k in range(2):
            to_near(p, k).start()

    def tokens(b):
        quarters[b].wait()
        grad, gain_grad = norm_backward(xq[b].astype(F32), scatters[b].total(), gain)
        gq[b] = (grad + gr_ref[b]).astype(BF16)
        gathers[b].start()
        own_rows[b].start()
        if b == 0:
            gsend[0] = jnp.concatenate(
                [gain_grad, gains_ref[...], jnp.zeros((6, width), F32)], axis=0
            )
        else:
            gsend[0, 0:1] += gain_grad

    gv[...] = jnp.zeros_like(gv)
    gqk[...] = jnp.zeros_like(gqk)
    mid = list(range(1, nz - 1))
    for g, c in zip(out_gathers, own_rows[tiles:]):
        g.start()
        c.start()

    def send_up_near(here):
        @pl.when(here)
        def _():
            for c in up_near:
                c.start()

    send_up_near(lax.rem(z, 2) == 0)
    value_grads(0)
    value_grads(1)
    states(0)
    chain(0, [0])
    local(0, 0)
    chain(0, mid[:1])
    local(0, 1)
    local(0, 2)
    chain(0, mid[1:])
    local(0, 3)
    for h in range(4, heads):
        local(0, h)
    value_grads(2)
    value_grads(3)
    states(1)
    chain(1, [0])
    send_up_near(z == nz - 1)
    for c in weights + gate_loads:
        c.wait()
    gload[0] = (gload[0].astype(F32) + gload[1].astype(F32)).astype(BF16)
    chain(0, [nz - 1])
    for h in range(heads):
        state_grads(0, h)
    norm_grads(0)
    scatters[0].start()
    scatters[1].start()
    chain(1, mid[:1])
    out_gathers[0].forward()
    out_gathers[1].forward()
    for h in range(heads):
        local(1, h)
        if h == heads // 2 - 1:
            chain(1, mid[1:])
            send_up_near((lax.rem(z, 2) == 1) & (z < nz - 1))
    scatters[0].forward()
    scatters[1].forward()
    chain(1, [nz - 1])
    gate_out.start()
    for h in range(heads):
        state_grads(1, h)
    norm_grads(1)
    scatters[2].start()
    scatters[3].start()
    send_half(0)
    out_gathers[2].forward()
    out_gathers[3].forward()
    pass_up()
    normed_rows(0)
    sum_half(0)
    for i in range(1, 2 * seqs):
        normed_rows(i)
    send_half(1)
    scatters[2].forward()
    scatters[3].forward()
    sum_half(1)
    tokens(0)
    tokens(1)
    tokens(2)
    gathers[0].forward()
    gathers[1].forward()
    tokens(3)

    def gain_copy(i, slot, to):
        return pltpu.make_async_remote_copy(
            gsend.at[i], gland.at[slot], ksems.at[0, slot], ksems.at[1, slot], device_id=to, device_id_type=MESH
        )

    hops = [
        [gain_copy(0, k, {"tensor": t ^ (k + 1)}) for k in range(3)],
        [gain_copy(1, 3, mate)],
        [gain_copy(2, 4 + k, others[k]) for k in range(nz - 1)],
    ]

    def gather_gains(i, first):
        out = gsend[i]
        for k, c in enumerate(hops[i]):
            c.wait()
            out = out + gland[first + k]
        if i < 2:
            gsend[i + 1] = out
            for c in hops[i + 1]:
                c.start()
        else:
            gains_out[...] = out

    for c in hops[0]:
        c.start()
    pass_on(0)
    gathers[2].forward()
    gathers[3].forward()
    gather_gains(0, 0)
    pass_on(1)
    gather_gains(1, 3)
    gate_out.wait()
    gate_ref[...] = gload[2].astype(F32) + gload[3].astype(F32) + gfar[...].astype(F32)
    up_near[1].wait_recv()
    up_out.wait()
    up_loads[1].wait()
    up_ref[...] = uload[1].astype(F32) + uland[1].astype(F32) + ufar[...].astype(F32)
    for c in up_near:
        c.wait_send()
    for p in range(2):
        conclude(p)
    gather_gains(2, 4)
    for c in own_rows:
        c.wait()
    for g in out_gathers + gathers:
        g.finish()
    for c in scatters:
        c.drain()

    @pl.when(z > 0)
    def _():
        for j in range(seqs * heads):
            send_down(j).wait_send()


def run_attention_backward(
    x, gain, qk, kq, v_ext, yx, pre, gattn, wo, wq, wk, wv, gr, gains, block_rows, gsum, gland, tables
):
    seqs, block, width = x.shape
    rows = seqs * block
    heads = wq.shape[0] // F
    tile = block // 2
    tiles, quarter = rows // tile, tile // 4
    nz = lax.axis_size("seq")
    spread, e1, e2, table = tables
    half = heads * F
    f1, f2 = jnp.roll(e1, half, 0), jnp.roll(e2, half, 0)
    chunk = width // 2 // nz
    cols = 2 * heads * LANES + 2 * heads * F
    shapes = [
        jax.ShapeDtypeStruct((chunk, cols), F32),
        jax.ShapeDtypeStruct((8, width), F32),
        jax.ShapeDtypeStruct(gsum.shape[2:], F32),
        jax.ShapeDtypeStruct(gsum.shape[2:], F32),
        jax.ShapeDtypeStruct(x.shape, BF16),
        jax.ShapeDtypeStruct(x.shape, BF16),
    ]
    vm, dma = pltpu.VMEM, pltpu.SemaphoreType.DMA
    wide = heads * LANES
    scratch = [
        vm((2 * half, width), BF16),
        vm(wv.shape, BF16),
        vm((tiles, quarter, width), F32),
        vm((rows, wide), BF16),
        vm((rows, wide), F32),
        vm((rows, wide), BF16),
        vm((rows, 2 * half), F32),
        vm((rows, 2 * half), BF16),
        vm((rows, wide), BF16),
        vm((width, rows), BF16),
        vm((width, rows), BF16),
        vm((seqs * heads, FEATS, LANES), F32),
        vm((seqs * heads, FEATS, LANES), BF16),
        vm((seqs * heads, FEATS, LANES), BF16),
        vm((2, tile, width), BF16),
        vm((tiles, quarter, width), BF16),
        vm((rows, width), BF16),
        vm((tiles, 2, quarter // 2, width), BF16),
        vm((tiles, 2, quarter, width), BF16),
        vm((tiles, quarter, width), BF16),
        vm((width // 2, cols), BF16),
        vm((width // 2, cols), BF16),
        vm((width // 2, cols), BF16),
        vm((3, chunk, cols), BF16),
        vm((chunk, cols), BF16),
        vm((4, 8, width), F32),
        vm((4 + nz - 1, 8, width), F32),
        vm((4,) + gsum.shape[2:], BF16),
        vm(gsum.shape[2:], BF16),
        vm((2,) + gsum.shape[2:], BF16),
        vm((2,) + gsum.shape[2:], BF16),
        vm(gsum.shape[2:], BF16),
        dma((6 + tiles,)),
        dma((2, seqs * heads)),
        dma((tiles, 2, 4)),
        dma((tiles, 2, 4)),
        dma((2, 2)),
        dma((2, 2, 3)),
        dma((2, 4 + nz - 1)),
        dma((tiles, 2, 4)),
        dma((2, tiles)),
        dma((6,)),
        dma((2,)),
        dma((2, 3)),
    ]
    return pl.pallas_call(
        functools.partial(attention_backward, nz),
        out_shape=shapes,
        in_specs=[ANY_SPEC] + [VMEM_SPEC] * 8 + [ANY_SPEC] * 4 + [VMEM_SPEC] + [ANY_SPEC] * 3 + [VMEM_SPEC] * 6,
        out_specs=[VMEM_SPEC] * 4 + [ANY_SPEC] * 2,
        scratch_shapes=scratch,
        compiler_params=pltpu.CompilerParams(
            collective_id=2, has_side_effects=True, vmem_limit_bytes=VMEM_LIMIT
        ),
        cost_estimate=pl.CostEstimate(
            flops=8 * rows * width * wide, bytes_accessed=30 << 20, transcendentals=0
        ),
        name="attention_backward",
    )(
        x,
        gain,
        qk,
        kq,
        v_ext,
        yx,
        pre,
        gattn,
        wo,
        wq,
        wk,
        wv,
        gr,
        gains,
        block_rows,
        gsum,
        gland,
        spread,
        e1,
        e2,
        f1,
        f2,
        table,
    )


def finish_kernel(gt_ref, bo_ref, *refs):
    count = len(refs) // 2 - 1
    gt_out, bo_out = refs[count : count + 2]
    gt_out[...] = gt_ref[...].astype(F32)
    bo_out[...] = bo_ref[...]
    for src, dst in zip(refs[:count], refs[count + 2 :]):
        dst[...] = src[...]


def finish(gt, bo, *grads):
    seqs, block, width = gt.shape
    steps = 8
    step = seqs * block // steps
    share, ff = grads[0].shape
    piece = next(p for p in range(8, share + 1, 8) if share % p == 0 and share // p <= steps)
    last = share // piece - 1
    rows = pl.BlockSpec((step, width), lambda i: (i, 0))
    small = pl.BlockSpec((piece, ff), lambda i: (jnp.minimum(i, last), 0))
    shape = jax.ShapeDtypeStruct
    gt, bo, *grads = pl.pallas_call(
        finish_kernel,
        grid=(steps,),
        out_shape=[shape((seqs * block, width), F32), shape((seqs * block, width), BF16)]
        + [shape(g.shape, F32) for g in grads],
        in_specs=[rows] * 2 + [small] * len(grads),
        out_specs=[rows] * 2 + [small] * len(grads),
        cost_estimate=pl.CostEstimate(flops=0, bytes_accessed=25 << 20, transcendentals=0),
        name="finish",
    )(gt.reshape(-1, width), bo.reshape(-1, width), *grads)
    return gt.reshape(seqs, block, width), bo.reshape(seqs, block, width), *grads


def shards(
    tokens,
    lengths,
    attn_gain,
    w_query,
    w_key,
    w_value,
    w_output,
    mlp_gain,
    w_gate,
    w_up,
    w_down,
    cotangent,
):
    seqs, block, width = tokens.shape
    heads = w_query.shape[1] // F
    value = w_value.shape[1] // heads
    chips = lax.axis_size("dp") // 2
    tables = (spread_table(heads, value),) + feature_tables(heads)
    wq, wk, wv = w_query.T, w_key.T, w_value.T
    qk, kq, pre, v_ext, yx, y, gh, gmt, yall, woall = run_attention_forward(
        tokens, attn_gain, wq, wk, wv, w_output, cotangent, w_down, lengths, tables
    )
    mlp_gain_grad, down_grads, block_rows, gr, gattn, gsum, _, gland = run_mlp(
        tokens, y, yall, w_output, woall, w_gate, w_up, w_down, gh, gmt, cotangent, mlp_gain, lengths
    )
    attn_grads, gains, gate_grads, up_grads, grad_tokens, block_out = run_attention_backward(
        tokens,
        attn_gain,
        qk,
        kq,
        v_ext,
        yx,
        pre,
        gattn,
        w_output,
        wq,
        wk,
        wv,
        gr,
        mlp_gain_grad,
        block_rows,
        gsum,
        gland,
        tables,
    )
    if chips > 1:
        nz = lax.axis_size("seq")
        pairs = [[2 * i, 2 * i + 1] for i in range(chips)]

        def respread(a):
            a = lax.all_gather(a.astype(BF16), "seq", axis=0, tiled=True)
            a = lax.all_gather(a, "dp", axis=0, tiled=True, axis_index_groups=pairs)
            a = (a.astype(F32) * (0.5 / nz)).astype(BF16)
            return lax.psum_scatter(a, ("dp", "seq"), scatter_dimension=0, tiled=True).astype(F32)

        attn_grads, down_grads, gate_grads, up_grads = [
            respread(a) for a in (attn_grads, down_grads, gate_grads, up_grads)
        ]
        gains = lax.psum(gains, "dp") * 0.5
    grad_tokens, block_out, gate_grads, up_grads, down_grads = finish(
        grad_tokens, block_out, gate_grads, up_grads, down_grads
    )
    share = width // (lax.axis_size("dp") * lax.axis_size("seq"))
    place = (lax.axis_index("dp") * lax.axis_size("seq") + lax.axis_index("seq")) * share
    gains = lax.dynamic_slice_in_dim(gains, place, share, 1)

    def unspread(a):
        return a.reshape(share, heads, LANES)[:, :, :value].reshape(share, heads * value)

    edge, half = heads * LANES, heads * F
    return (
        block_out,
        grad_tokens,
        gains[0],
        attn_grads[:, edge : edge + half],
        attn_grads[:, edge + half : edge + 2 * half],
        unspread(attn_grads[:, edge + 2 * half :]),
        unspread(attn_grads[:, :edge]).T,
        gains[1],
        gate_grads,
        up_grads,
        down_grads.T,
    )


def solution(mesh):
    in_specs = (
        P("dp", "seq", None),
        P("dp"),
        P(),
        P(None, "tensor"),
        P(None, "tensor"),
        P(None, "tensor"),
        P("tensor", None),
        P(),
        P(None, "tensor"),
        P(None, "tensor"),
        P("tensor", None),
        P("dp", "seq", None),
    )
    out_specs = (
        P("dp", "seq", None),
        P("dp", "seq", None),
        P(("dp", "seq")),
        P(("dp", "seq"), "tensor"),
        P(("dp", "seq"), "tensor"),
        P(("dp", "seq"), "tensor"),
        P("tensor", ("dp", "seq")),
        P(("dp", "seq")),
        P(("dp", "seq"), "tensor"),
        P(("dp", "seq"), "tensor"),
        P("tensor", ("dp", "seq")),
    )
    return jax.shard_map(shards, mesh=mesh, in_specs=in_specs, out_specs=out_specs, check_vma=False)
```

```python
import functools
import math

import jax
import jax.numpy as jnp
import numpy as np
from jax import lax
from jax.experimental import pallas as pl
from jax.experimental.pallas import tpu as pltpu
from jax.sharding import PartitionSpec as P

F = 16
FEATS = 160
LANES = 128
WIDE = 256
VMEM_LIMIT = 62 << 20
MESH = pl.DeviceIdType.MESH
BF16 = jnp.bfloat16
F32 = jnp.float32
VMEM_SPEC = pl.BlockSpec(memory_space=pltpu.VMEM)
ANY_SPEC = pl.BlockSpec(memory_space=pl.ANY)
NN = (((1,), (0,)), ((), ()))
NT = (((1,), (1,)), ((), ()))
TN = (((0,), (0,)), ((), ()))


def dot(a, b, dims=NN):
    return lax.dot_general(a, b, dims, preferred_element_type=F32)


def feature_tables(heads):
    upper_i, upper_j = np.triu_indices(F)
    pairs = len(upper_i)
    first = np.zeros((2 * heads * F, heads * WIDE), np.float32)
    second = np.zeros_like(first)
    rows = np.zeros((8, WIDE), np.float32)
    cols = np.arange(pairs)
    for h in range(heads):
        first[h * F + upper_i, h * WIDE + cols] = 1.0
        second[h * F + upper_j, h * WIDE + cols] = 1.0
        first[h * F + np.arange(F), h * WIDE + pairs + np.arange(F)] = 1.0
    rows[0, pairs + F] = 1.0
    rows[1, pairs : pairs + F + 1] = 1.0
    rows[2, :pairs] = np.where(upper_i == upper_j, 1.0 / (2 * F), 1.0 / F)
    rows[2, pairs : pairs + F] = 1.0 / math.sqrt(F)
    rows[2, pairs + F] = 1.0
    return tuple(jnp.asarray(a, BF16) for a in (first, second)) + (jnp.asarray(rows),)


def spread_table(heads, width):
    table = np.zeros((heads * width, heads * LANES), np.float32)
    for h in range(heads):
        table[h * width + np.arange(width), h * LANES + np.arange(width)] = 1.0
    return jnp.asarray(table, BF16)


def rows_at(start, count):
    return pl.ds(pl.multiple_of(start, 16), count)


class Gather:
    def __init__(self, source, slots, sems, half):
        me = lax.axis_index("tensor")
        self.x, self.y = {"tensor": me ^ 1}, {"tensor": me ^ 2}
        self.source, self.slots, self.sems, self.half = source, slots, sems, half
        self.first = [
            self.copy(source, slots(0), 0, self.x),
            self.copy(source, slots(1), 1, self.y),
        ]
        self.second = [
            self.copy(half(slots(0), 0), half(slots(2), 0), 2, self.y),
            self.copy(half(slots(1), 1), half(slots(2), 1), 3, self.x),
        ]

    def copy(self, src, dst, i, to):
        return pltpu.make_async_remote_copy(
            src, dst, self.sems.at[0, i], self.sems.at[1, i], device_id=to, device_id_type=MESH
        )

    def start(self):
        for c in self.first:
            c.start()

    def forward(self):
        for c, d in zip(self.first, self.second):
            c.wait_recv()
            d.start()

    def arrive(self):
        for d in self.second:
            d.wait_recv()

    def leave(self):
        for c in self.first + self.second:
            c.wait_send()

    def finish(self):
        self.arrive()
        self.leave()


def greet(devices):
    barrier = pltpu.get_barrier_semaphore()
    for d in devices:
        pl.semaphore_signal(barrier, inc=1, device_id=d, device_id_type=MESH)
    pl.semaphore_wait(barrier, len(devices))


def features(rows, first, second, table, scaled):
    a = dot(rows, first) + table[0:1]
    b = dot(rows, second) + table[1:2]
    out = a * b
    return out * table[2:3] if scaled else out


def head_of(rows, h):
    lane = lax.broadcasted_iota(jnp.int32, rows.shape, 1)
    return jnp.where(lane // F == h, rows, jnp.zeros_like(rows))


def attention_forward(
    nz,
    x_hbm,
    gain_ref,
    wq_hbm,
    wk_hbm,
    wv_ref,
    wo_ref,
    cot_hbm,
    wd_hbm,
    len_ref,
    spread_ref,
    e1_ref,
    e2_ref,
    table_ref,
    qk_ref,
    kq_ref,
    pre_ref,
    v_hbm,
    yx_hbm,
    y_hbm,
    gh_hbm,
    gmt_hbm,
    yall_ref,
    woall_ref,
    wqk_ref,
    x_ref,
    cot_ref,
    wd_ref,
    v_ref,
    yx_ref,
    y_ref,
    gh_ref,
    gmt_ref,
    sloc,
    pout,
    gsems,
    wsems,
    csems,
    zsems,
    lsems,
    osems,
):
    seqs, block, width = x_hbm.shape
    heads = wq_hbm.shape[0] // F
    value = wv_ref.shape[0] // heads
    z = lax.axis_index("seq")
    t = lax.axis_index("tensor")
    core = lax.axis_index("dp")
    side = lax.rem(core, 2)
    mate = {"dp": core + 1 - 2 * side}
    up, down = {"seq": lax.rem(z + 1, nz)}, {"seq": lax.rem(z + nz - 1, nz)}

    tile = block // 2
    x_loads = [
        pltpu.make_async_copy(
            x_hbm.at[i // 2, pl.ds((i % 2) * tile, tile)],
            x_ref.at[i // 2, pl.ds((i % 2) * tile, tile)],
            lsems.at[i],
        )
        for i in range(2 * seqs)
    ]
    late = [
        pltpu.make_async_copy(cot_hbm, cot_ref, lsems.at[2 * seqs]),
        pltpu.make_async_copy(wd_hbm, wd_ref, lsems.at[2 * seqs + 1]),
    ]
    half = heads * F
    joins = [
        pltpu.make_async_copy(w, wqk_ref.at[pl.ds(i * half, half)], lsems.at[2 * seqs + 2 + i])
        for i, w in enumerate((wq_hbm, wk_hbm))
    ]
    for c in joins + x_loads + late:
        c.start()
    greet([{"tensor": t ^ 1}, {"tensor": t ^ 2}, mate, up, down])

    wrows = wo_ref.shape[0] // 4
    cut = wrows // 32 * 16 + 16
    zbit = lax.rem(z, 2)

    def part(s, zb):
        return woall_ref.at[s, rows_at((2 * side + zb) * wrows, wrows)]

    wo = Gather(
        wo_ref.at[rows_at((2 * side + zbit) * wrows, wrows)],
        lambda s: part(s, zbit),
        wsems,
        lambda ref, i: ref.at[pl.ds(0, cut)] if i == 0 else ref.at[pl.ds(cut, wrows - cut)],
    )
    wo.start()

    def share(s, i):
        ref = part(s, zbit if i < 2 else 1 - zbit)
        to = {"seq": z ^ 1} if i == 1 else mate
        return pltpu.make_async_remote_copy(
            ref, ref, csems.at[0, 3 * i + s], csems.at[1, 3 * i + s], device_id=to, device_id_type=MESH
        )

    gain = gain_ref[...].reshape(1, width)
    def share_near(here):
        @pl.when(here)
        def _():
            for s in range(2):
                share(s, 1).start()

    table = table_ref[...]
    ones = jnp.where(
        lax.rem(lax.broadcasted_iota(jnp.int32, (1, heads * LANES), 1), LANES) == value, 1.0, 0.0
    )
    def project(b, i):
        at = pl.ds(i * tile, tile)
        flat = pl.ds(b * block + i * tile, tile)
        x_loads[2 * b + i].wait()
        rows = x_ref[b, at].astype(F32)
        normed = rows * lax.rsqrt(jnp.mean(rows * rows, axis=-1, keepdims=True) + 1e-06)
        normed = (normed * gain).astype(BF16)
        qk = dot(normed, wqk_ref[...], NT)
        qk_ref[flat] = qk.astype(BF16)
        kq_ref[flat] = pltpu.roll(qk, heads * F, 1).astype(BF16)
        values = dot(normed, wv_ref[...], NT).astype(BF16)
        v_ref[flat] = (dot(values, spread_ref[...]) + ones).astype(BF16)

    def lanes(h, n):
        return pl.ds(h * n, n)

    def states(b):
        flat = pl.ds(b * block, block)
        for h in range(heads):
            wide = lanes(h, WIDE)
            phi = features(kq_ref[flat], e1_ref[:, wide], e2_ref[:, wide], table, False)
            s = dot(phi.astype(BF16), v_ref[flat, lanes(h, LANES)], TN)
            sloc[b * heads + h] = s[:FEATS]

    def send_up(j):
        return pltpu.make_async_remote_copy(
            pout.at[j],
            pre_ref.at[j],
            zsems.at[0, j],
            zsems.at[1, j],
            device_id=up,
            device_id_type=MESH,
        )

    def chain(b, who):
        for at in who:

            @pl.when(z == at)
            def _():
                for h in range(heads):
                    j = b * heads + h
                    if at == 0:
                        pre_ref[j] = jnp.zeros((FEATS, LANES), BF16)
                        pout[j] = sloc[j].astype(BF16)
                    else:
                        send_up(j).wait_recv()
                        if at < nz - 1:
                            pout[j] = (sloc[j] + pre_ref[j].astype(F32)).astype(BF16)
                    if at < nz - 1:
                        send_up(j).start()

    def attend(b, h):
        narrow = lanes(h, LANES)
        wide = lanes(h, WIDE)
        for i in range(2):
            span = (i + 1) * tile
            at = pl.ds(b * block + i * tile, tile)
            until = pl.ds(b * block, span)
            rows = qk_ref[at]
            s = dot(head_of(rows, h), kq_ref[until], NT)
            w = 1.0 + s * (1.0 / math.sqrt(F))
            w = 0.5 * (w * w) + 0.5
            row = lax.broadcasted_iota(jnp.int32, w.shape, 0) + i * tile
            col = lax.broadcasted_iota(jnp.int32, w.shape, 1)
            w = jnp.where(col <= row, w, 0.0).astype(BF16)
            num = dot(w, v_ref[until, narrow])
            phi = features(rows, e1_ref[:, wide], e2_ref[:, wide], table, True)
            num = num + dot(phi[:, :FEATS].astype(BF16), pre_ref[b * heads + h])
            recip = 1.0 / num[:, value : value + 1]
            lane = lax.broadcasted_iota(jnp.int32, num.shape, 1)
            yx_ref[at, narrow] = jnp.where(lane == value, recip, num * recip)

    def gather(b):
        flat = pl.ds(b * block, block)
        return Gather(
            y_ref.at[flat],
            lambda s: yall_ref.at[s, flat],
            gsems.at[b],
            lambda ref, i: ref.at[pl.ds(i * tile, tile)],
        )

    def pack(b):
        for i in range(2):
            at = pl.ds(b * block + i * tile, tile)
            y_ref[at] = dot(yx_ref[at].astype(BF16), spread_ref[...], NT).astype(BF16)

    def put(src, dst, i):
        return pltpu.make_async_copy(src, dst, osems.at[i])

    def hidden_outs(i):
        at = pl.ds(i * tile, tile)
        return [
            put(gh_ref.at[at], gh_hbm.at[at], 2 * i),
            put(gmt_ref.at[:, at], gmt_hbm.at[:, at], 2 * i + 1),
        ]

    first_out = 4 * seqs
    outs = [
        put(v_ref, v_hbm, first_out),
        put(yx_ref, yx_hbm, first_out + 1),
        put(y_ref, y_hbm, first_out + 2),
    ]

    def hidden_grads(i):
        b, local = i // 2, i % 2
        at = z * block + local * tile + lax.broadcasted_iota(jnp.int32, (tile, 1), 0)
        mask = (at < len_ref[b]).astype(F32)
        gm = (cot_ref[b, pl.ds(local * tile, tile)].astype(F32) * mask).astype(BF16)
        gmt_ref[:, pl.ds(i * tile, tile)] = gm.T
        gh_ref[pl.ds(i * tile, tile)] = dot(gm, wd_ref[...], NT).astype(BF16)
        for c in hidden_outs(i):
            c.start()

    gathers = [gather(b) for b in range(seqs)]
    mid = list(range(1, nz - 1))
    for c in joins:
        c.wait()
    for b in range(seqs + 1):
        if b < seqs:
            for i in range(2):
                project(b, i)
                if b > 0 and i == 0:
                    chain(b - 1, mid[:1])
            if b > 0:
                chain(b - 1, mid[1:])
                wo.forward()
                for s in range(2):
                    share(s, 0).start()
                share_near(zbit == 1)
            states(b)
            chain(b, [0])
        if b > 0:
            chain(b - 1, [nz - 1])
            for h in range(heads):
                attend(b - 1, h)
                if b == seqs - 1:
                    chain(b, mid[h : h + 1] if h < heads - 1 else mid[h:])
                    if h == min(len(mid), heads) - 1:
                        share_near(zbit == 0)
            pack(b - 1)
            gathers[b - 1].start()
    for c in outs:
        c.start()
    wo.arrive()
    share(2, 0).start()
    share(2, 1).start()
    for c in late:
        c.wait()
    hidden_grads(0)
    gathers[0].forward()
    for i in range(1, 2 * seqs):
        hidden_grads(i)
    for g in gathers[1:]:
        g.forward()
    for s in range(2):
        share(s, 1).wait_recv()
        share(s, 2).start()
    share(2, 1).wait_recv()
    share(2, 2).start()
    for c in outs:
        c.wait()
    for i in range(2 * seqs):
        for c in hidden_outs(i):
            c.wait()
    wo.leave()
    for g in gathers:
        g.finish()
    for s in range(3):
        share(s, 0).wait()
        share(s, 1).wait_send()
        share(s, 2).wait()

    @pl.when(z < nz - 1)
    def _():
        for j in range(seqs * heads):
            send_up(j).wait_send()


def run_attention_forward(x, gain, wq, wk, wv, wo, cot, wd, lengths, tables):
    seqs, block, width = x.shape
    heads = wq.shape[0] // F
    value = wv.shape[0] // heads
    rows = seqs * block
    spread, e1, e2, table = tables
    shape = jax.ShapeDtypeStruct
    wide, ff = heads * LANES, wd.shape[0]
    shapes = [
        shape((rows, 2 * heads * F), BF16),
        shape((rows, 2 * heads * F), BF16),
        shape((seqs * heads, FEATS, LANES), BF16),
        shape((rows, wide), BF16),
        shape((rows, wide), F32),
        shape((rows, heads * value), BF16),
        shape((rows, ff), BF16),
        shape((width, rows), BF16),
        shape((3, rows, heads * value), BF16),
        shape((3,) + wo.shape, BF16),
    ]
    vm, dma = pltpu.VMEM, pltpu.SemaphoreType.DMA
    smem = pl.BlockSpec(memory_space=pltpu.SMEM)
    return pl.pallas_call(
        functools.partial(attention_forward, lax.axis_size("seq")),
        out_shape=shapes,
        in_specs=[ANY_SPEC, VMEM_SPEC] + [ANY_SPEC] * 2 + [VMEM_SPEC] + [ANY_SPEC] * 3 + [smem] + [VMEM_SPEC] * 4,
        out_specs=[VMEM_SPEC] * 3 + [ANY_SPEC] * 7,
        scratch_shapes=[
            vm((2 * heads * F, width), BF16),
            vm(x.shape, BF16),
            vm(x.shape, BF16),
            vm(wd.shape, BF16),
            vm((rows, wide), BF16),
            vm((rows, wide), F32),
            vm((rows, heads * value), BF16),
            vm((rows, ff), BF16),
            vm((width, rows), BF16),
            vm((seqs * heads, FEATS, LANES), F32),
            vm((seqs * heads, FEATS, LANES), BF16),
            dma((seqs, 2, 4)),
            dma((2, 4)),
            dma((2, 9)),
            dma((2, seqs * heads)),
            dma((2 * seqs + 4,)),
            dma((4 * seqs + 3,)),
        ],
        compiler_params=pltpu.CompilerParams(
            collective_id=0, has_side_effects=True, vmem_limit_bytes=VMEM_LIMIT
        ),
        cost_estimate=pl.CostEstimate(
            flops=2 * rows * width * heads * (2 * F + value), bytes_accessed=20 << 20, transcendentals=0
        ),
        name="attention_forward",
    )(x, gain, wq, wk, wv, wo, cot, wd, lengths, spread, e1, e2, table)


class Exchange:
    def __init__(self, sems):
        me = lax.axis_index("tensor")
        self.x, self.y = {"tensor": me ^ 1}, {"tensor": me ^ 2}
        self.sems = sems

    def copy(self, src, dst, i, to):
        return pltpu.make_async_remote_copy(
            src, dst, self.sems.at[0, i], self.sems.at[1, i], device_id=to, device_id_type=MESH
        )


class ReduceScatter(Exchange):
    def __init__(self, part, near, far, sems):
        super().__init__(sems)
        me = lax.axis_index("tensor")
        self.part, self.near, self.far = part, near, far
        self.q = q = near[0].shape[0] * 2
        self.half = q // 2
        self.at = [me * q, (me ^ 1) * q, (me ^ 2) * q, (me ^ 3) * q]
        over = self.at[3]
        self.first = [
            self.copy(part.at[rows_at(over, self.half)], near[0], 0, self.x),
            self.copy(part.at[rows_at(over + self.half, self.half)], near[1], 1, self.y),
        ]
        self.second = [
            self.copy(part.at[rows_at(self.at[2], q)], far[1], 2, self.y),
            self.copy(part.at[rows_at(self.at[1], q)], far[0], 3, self.x),
        ]

    def start(self):
        for c in self.first:
            c.start()

    def forward(self):
        for i, start in ((0, self.at[2]), (1, self.at[1] + self.half)):
            self.first[i].wait_recv()
            rows = rows_at(start, self.half)
            self.part[rows] = (self.part[rows].astype(F32) + self.near[i][...].astype(F32)).astype(BF16)
            self.second[i].start()

    def total(self):
        for c in self.second:
            c.wait_recv()
        mine = self.part[rows_at(self.at[0], self.q)].astype(F32)
        return mine + self.far[0][...].astype(F32) + self.far[1][...].astype(F32)

    def drain(self):
        for c in self.first + self.second:
            c.wait_send()


class RowGather(Exchange):
    def __init__(self, source, piece, half, sems):
        super().__init__(sems)
        me = lax.axis_index("tensor")
        self.first = [
            self.copy(source, piece(me), 0, self.x),
            self.copy(source, piece(me), 1, self.y),
        ]
        self.second = [
            self.copy(half(me ^ 1, 0), half(me ^ 1, 0), 2, self.y),
            self.copy(half(me ^ 2, 1), half(me ^ 2, 1), 3, self.x),
        ]

    start = Gather.start
    forward = Gather.forward
    arrive = Gather.arrive
    leave = Gather.leave
    finish = Gather.finish


def norm_backward(rows, grad, gain):
    norm = lax.rsqrt(jnp.mean(rows * rows, axis=-1, keepdims=True) + 1e-06)
    unit = rows * norm
    gain_grad = jnp.sum(grad * unit, axis=0, keepdims=True)
    scaled = grad * gain
    mean = jnp.mean(scaled * unit, axis=-1, keepdims=True)
    return norm * (scaled - unit * mean), gain_grad


def own_rows(value, t, count):
    parts = [value[i * count : (i + 1) * count] for i in range(4)]
    low = jnp.where(t == 0, parts[0], parts[1])
    return jnp.where(t < 2, low, jnp.where(t == 2, parts[2], parts[3]))


def mlp_kernel(
    nz,
    x_hbm,
    y_hbm,
    yall_hbm,
    wo_hbm,
    woall_hbm,
    wg_hbm,
    wu_hbm,
    wd_hbm,
    gh_hbm,
    gmt_hbm,
    cot_hbm,
    gain_ref,
    len_ref,
    gain_grad_ref,
    down_ref,
    block_hbm,
    gr_hbm,
    gattn_hbm,
    gsum_hbm,
    land_hbm,
    zland_hbm,
    wo4,
    wg,
    wu,
    wd,
    xt,
    yt,
    ght,
    h2t,
    gmt,
    gg,
    gu,
    hid,
    part,
    near,
    far,
    ga,
    r_ref,
    grs,
    stage,
    back,
    keep,
    lsems,
    rsems,
    asems,
    msems,
    bsems,
    dsems,
    osems,
    psems,
    free_sem,
):
    seqs, block, width = x_hbm.shape
    tile = xt.shape[0]
    per = block // tile
    quarter = tile // 4
    tiles = seqs * per
    z = lax.axis_index("seq")
    t = lax.axis_index("tensor")
    core = lax.axis_index("dp")
    side = lax.rem(core, 2)
    mate = {"dp": core + 1 - 2 * side}
    near_z, far_z = {"seq": z ^ 1}, {"seq": z ^ 2}
    gain = gain_ref[...].reshape(1, width)

    def load(src, dst, i):
        return pltpu.make_async_copy(src, dst, lsems.at[i])

    weights = [
        load(wo_hbm, wo4.at[0], 0),
        *[load(woall_hbm.at[s], wo4.at[s + 1], 1 + s) for s in range(3)],
        load(wg_hbm, wg, 4),
        load(wu_hbm, wu, 5),
    ]
    late = [load(gmt_hbm, gmt, 6), load(wd_hbm, wd, 7)]

    def xy_loads(i):
        b, at = i // per, lax.rem(i, per) * tile
        flat = rows_at(i * tile, tile)
        return [
            load(x_hbm.at[b, rows_at(at, tile)], xt, 8),
            load(y_hbm.at[flat], yt.at[0], 9),
            *[load(yall_hbm.at[s, flat], yt.at[s + 1], 10 + s) for s in range(3)],
        ]

    def g_load(i):
        return load(gh_hbm.at[rows_at(i * tile, tile)], ght, 13)

    def c_load(i):
        b, at = i // per, lax.rem(i, per) * tile + t * quarter
        return load(cot_hbm.at[b, rows_at(at, quarter)], ga.at[i], 14 + i)

    for c in xy_loads(0) + weights + [g_load(0)] + [c_load(i) for i in range(tiles)] + late:
        c.start()
    greet([{"tensor": t ^ 1}, {"tensor": t ^ 2}, mate, near_z, far_z])

    def scatter(i):
        return ReduceScatter(
            part.at[rows_at(i * tile, tile)],
            [near.at[i, k] for k in range(2)],
            [far.at[i, k] for k in range(2)],
            rsems.at[i],
        )

    def mlp_scatter(i):
        source = wo4.at[i, pl.ds(0, tile)]
        near_ref = [wo4.at[i, pl.ds(tile + k * (quarter // 2), quarter // 2)] for k in range(2)]
        far_ref = [wo4.at[i, pl.ds(tile + (k + 1) * quarter, quarter)] for k in range(2)]
        return ReduceScatter(source, near_ref, far_ref, psems.at[i])

    def gather(i):
        def piece(k):
            return gattn_hbm.at[rows_at(i * tile + k * quarter, quarter)]

        def half(k, h):
            start = i * tile + k * quarter + h * (quarter // 2)
            return gattn_hbm.at[rows_at(start, quarter // 2)]

        return RowGather(ga.at[i], piece, half, asems.at[i])

    def place(i):
        at = rows_at(i * tile + t * quarter, quarter)
        return [
            pltpu.make_async_copy(ga.at[i], gattn_hbm.at[at], osems.at[0, i]),
            pltpu.make_async_copy(grs, gr_hbm.at[i], osems.at[1, i]),
        ]

    def tile_step(i, first):
        flat = rows_at(i * tile, tile)
        for c in xy_loads(i):
            c.wait()
        if first:
            for c in weights[:4]:
                c.wait()
        r = xt[...].astype(F32)
        for s in range(4):
            r = r + dot(yt[s], wo4[s])

        @pl.when(i + 1 < tiles)
        def _():
            for c in xy_loads(i + 1):
                c.start()

        r_ref[i] = own_rows(r, t, quarter)
        h2 = r * lax.rsqrt(jnp.mean(r * r, axis=-1, keepdims=True) + 1e-06) * gain
        h2 = h2.astype(BF16)
        h2t[:, pl.ds(pl.multiple_of(i * tile, LANES), tile)] = h2.T
        if first:
            for c in weights[4:6]:
                c.wait()
        gate = dot(h2, wg[...], NT)
        up = dot(h2, wu[...], NT)
        if not first:
            scatter(i - 1).forward()
        g_load(i).wait()
        gh = ght[...].astype(F32)
        sig = 1.0 / (1.0 + jnp.exp(-gate))
        silu = gate * sig
        hid[flat] = (silu * up).astype(BF16)
        gg[flat] = (gh * up * (sig * (1.0 + gate * (1.0 - sig)))).astype(BF16)
        gu[flat] = (gh * silu).astype(BF16)

        @pl.when(i + 1 < tiles)
        def _():
            g_load(i + 1).start()

        part[flat] = (dot(gg[flat], wg[...]) + dot(gu[flat], wu[...])).astype(BF16)
        scatter(i).start()

    def mixed(i, first):
        b = i // per
        grad = scatter(i).total()
        c_load(i).wait()
        at = z * block + lax.rem(i, per) * tile + t * quarter
        at = at + lax.broadcasted_iota(jnp.int32, (quarter, 1), 0)
        out = ga[i].astype(F32) * (at < len_ref[b]).astype(F32)
        gr, gain_grad = norm_backward(r_ref[i], grad, gain)
        gr = gr + out
        if first:
            gain_grad_ref[...] = gain_grad
        else:
            gain_grad_ref[...] += gain_grad
            place(i - 1)[1].wait()
        grs[...] = gr
        ga[i] = gr.astype(BF16)
        gather(i).start()
        for c in place(i):
            c.start()

    tile_step(0, True)

    def rest(i, carry):
        tile_step(i, False)
        return carry

    lax.fori_loop(1, tiles - 1, rest, 0)
    mixed(0, True)
    tile_step(tiles - 1, False)

    lefts = (gmt, h2t, h2t)
    rights = (hid, gg, gu)
    half_rows = width // 2
    chunk = back.shape[0]
    last = tiles - 1

    def product(n, base, m):
        return dot(lefts[n][rows_at(base + m * chunk, chunk)], rights[n][...])

    def to_mate(n, m, slot):
        return pltpu.make_async_remote_copy(
            stage.at[slot],
            land_hbm.at[n, m],
            msems.at[0, slot],
            msems.at[1, n * nz + m],
            device_id=mate,
            device_id_type=MESH,
        )

    def from_mate(n, m):
        return pltpu.make_async_copy(land_hbm.at[n, m], back, bsems.at[0])

    def to_sum(n, m, slot):
        return pltpu.make_async_copy(stage.at[slot], gsum_hbm.at[n, m], bsems.at[slot - 1])

    across = [
        pltpu.make_async_remote_copy(
            gsum_hbm.at[n, k],
            zland_hbm.at[n, k],
            dsems.at[0, 2 * n + k],
            dsems.at[1, 2 * n + k],
            device_id=near_z,
            device_id_type=MESH,
        )
        for n in range(2)
        for k in range(2)
    ]
    beyond = pltpu.make_async_remote_copy(
        keep, zland_hbm.at[0, 2], dsems.at[0, 4], dsems.at[1, 4], device_id=far_z, device_id_type=MESH
    )

    def landed(k):
        c = pltpu.make_async_copy(zland_hbm.at[0, k], back, bsems.at[0])
        c.start()
        c.wait()
        return back[...].astype(F32)

    def pass_on():
        across[0].wait_recv()
        keep[...] = (keep[...].astype(F32) + landed(0)).astype(BF16)
        beyond.start()

    def step_mlp(i):
        flat = rows_at(i * tile, tile)
        wo4[i, :tile] = dot(hid[flat], wd[...]).astype(BF16)
        mlp_scatter(i).start()

    def block_out(i):
        return pltpu.make_async_copy(ga.at[i], block_hbm.at[i], osems.at[0, i])

    def block_rows(i):
        b = i // per
        at = z * block + lax.rem(i, per) * tile + t * quarter
        at = at + lax.broadcasted_iota(jnp.int32, (quarter, 1), 0)
        mask = (at < len_ref[b]).astype(F32)
        ga[i] = (mask * (r_ref[i] + mlp_scatter(i).total())).astype(BF16)
        block_out(i).start()

    for to in ({"tensor": t ^ 1}, {"tensor": t ^ 2}):
        pl.semaphore_signal(free_sem, inc=1, device_id=to, device_id_type=MESH)
    late[0].wait()
    late[1].wait()
    steps = {
        2: lambda: (gather(0).forward(), mixed(1, False)),
        3: lambda: scatter(last).forward(),
        4: lambda: (mixed(last - 1, False), pl.semaphore_wait(free_sem, 2)),
        5: lambda: step_mlp(0),
        6: lambda: step_mlp(1),
        7: lambda: step_mlp(2),
        8: lambda: step_mlp(3),
        9: lambda: gather(1).forward(),
        11: lambda: mixed(last, False),
        13: lambda: gather(last - 1).forward(),
        16: lambda: mlp_scatter(0).forward(),
        17: lambda: (gather(last).forward(), mlp_scatter(1).forward()),
        18: lambda: mlp_scatter(2).forward(),
        19: lambda: mlp_scatter(3).forward(),
    }
    count = 0

    def step():
        nonlocal count
        steps.get(count, lambda: None)()
        count += 1

    order = [z ^ 3, z ^ 1, z ^ 2, z]
    for n in range(3):

        def for_mate(k):
            if k >= 2:
                to_mate(n, order[k - 2], k % 2).wait_send()
            stage[k % 2] = product(n, (1 - side) * half_rows, order[k]).astype(BF16)
            to_mate(n, order[k], k % 2).start()
            step()

        def for_own(k):
            m = order[k]
            to_mate(n, m, 0).wait_recv()
            from_mate(n, m).start()
            out = product(n, side * half_rows, m)
            from_mate(n, m).wait()
            out = out + back[...].astype(F32)
            if n == 0 and k == 2:
                keep[...] = out.astype(BF16)
            elif n == 0 and k == 3:
                down_ref[...] = out
            else:
                if k > 0 and (n == 2 or k == 3):
                    to_sum(n, k - 1, 2).wait()
                stage[2] = out.astype(BF16)
                to_sum(n, k, 2).start()
            if n < 2 and k < 2:
                to_sum(n, k, 2).wait()
                across[2 * n + k].start()
            step()

        for_mate(0)
        for_mate(1)
        for_own(0)
        for_mate(2)
        for_own(1)
        for_mate(3)
        for_own(2)
        for_own(3)
        for k in range(nz - 2, nz):
            to_mate(n, order[k], k % 2).wait_send()
        if n > 0:
            to_sum(n, nz - 1, 2).wait()
        if n == 1:
            pass_on()
    across[1].wait_recv()
    down_ref[...] += landed(1)
    place(last)[1].wait()
    for i in range(tiles):
        place(i)[0].wait()
        gather(i).finish()
        scatter(i).drain()
    for c in across:
        c.wait_send()
    for i in range(tiles):
        block_rows(i)
        mlp_scatter(i).drain()
    for i in range(tiles):
        block_out(i).wait()
    for c in across[2:]:
        c.wait_recv()
    beyond.wait_recv()
    down_ref[...] += landed(2)
    beyond.wait_send()


def run_mlp(x, y, yall, wo, woall, wg, wu, wd, gh, gmt, cot, gain, lengths):
    seqs, block, width = x.shape
    rows = seqs * block
    nz = lax.axis_size("seq")
    value, ff = wo.shape[0], wd.shape[0]
    tile = block // 2
    tiles, quarter = rows // tile, tile // 4
    chunk = width // 2 // nz
    shape = jax.ShapeDtypeStruct
    shapes = [
        shape((1, width), F32),
        shape((chunk, ff), F32),
        shape((tiles, quarter, width), BF16),
        shape((tiles, quarter, width), F32),
        shape((rows, width), BF16),
        shape((3, 4, chunk, ff), BF16),
        shape((3, nz, chunk, ff), BF16),
        shape((2, 3, chunk, ff), BF16),
    ]
    vm, dma = pltpu.VMEM, pltpu.SemaphoreType.DMA
    scratch = [
        vm((4, value, width), BF16),
        vm((ff, width), BF16),
        vm((ff, width), BF16),
        vm((ff, width), BF16),
        vm((tile, width), BF16),
        vm((4, tile, value), BF16),
        vm((tile, ff), BF16),
        vm((width, rows), BF16),
        vm((width, rows), BF16),
        vm((rows, ff), BF16),
        vm((rows, ff), BF16),
        vm((rows, ff), BF16),
        vm((rows, width), BF16),
        vm((tiles, 2, quarter // 2, width), BF16),
        vm((tiles, 2, quarter, width), BF16),
        vm((tiles, quarter, width), BF16),
        vm((tiles, quarter, width), F32),
        vm((quarter, width), F32),
        vm((3, chunk, ff), BF16),
        vm((chunk, ff), BF16),
        vm((chunk, ff), BF16),
        dma((14 + tiles,)),
        dma((tiles, 2, 4)),
        dma((tiles, 2, 4)),
        dma((2, 3 * nz)),
        dma((3,)),
        dma((2, 5)),
        dma((2, tiles)),
        dma((tiles, 2, 4)),
        pltpu.SemaphoreType.REGULAR,
    ]
    return pl.pallas_call(
        functools.partial(mlp_kernel, nz),
        out_shape=shapes,
        in_specs=[ANY_SPEC] * 11 + [VMEM_SPEC, pl.BlockSpec(memory_space=pltpu.SMEM)],
        out_specs=[VMEM_SPEC] * 2 + [ANY_SPEC] * 6,
        scratch_shapes=scratch,
        compiler_params=pltpu.CompilerParams(
            collective_id=1, has_side_effects=True, vmem_limit_bytes=VMEM_LIMIT
        ),
        cost_estimate=pl.CostEstimate(
            flops=2 * rows * width * (4 * value + 8 * ff), bytes_accessed=60 << 20, transcendentals=0
        ),
        name="mlp_forward_backward",
    )(x, y, yall, wo, woall, wg.T, wu.T, wd, gh, gmt, cot, gain, lengths)


def attention_backward(
    nz,
    x_hbm,
    gain_ref,
    qk_ref,
    kq_ref,
    v_ref,
    yx_hbm,
    pre_ref,
    gattn_hbm,
    wo_ref,
    wq_hbm,
    wk_hbm,
    wv_hbm,
    gr_hbm,
    gains_ref,
    block_hbm,
    gsum_hbm,
    gland_hbm,
    spread_ref,
    e1_ref,
    e2_ref,
    f1_ref,
    f2_ref,
    table_ref,
    grads_ref,
    gains_out,
    gate_ref,
    up_ref,
    gt_hbm,
    bo_hbm,
    wqk_ref,
    wv_ref,
    gr_ref,
    gattn_ref,
    yx_ref,
    gn,
    gv,
    gvb,
    gqk,
    gqkb,
    yb,
    gat,
    h1t,
    sloc,
    sout,
    suf,
    xt,
    xq,
    part,
    near,
    far,
    gq,
    stage,
    land,
    total,
    zland,
    zsum,
    gsend,
    gland,
    gload,
    gfar,
    uload,
    uland,
    ufar,
    lsems,
    zsems,
    rsems,
    asems,
    msems,
    dsems,
    ksems,
    asems2,
    osems,
    hsems,
    fsems,
    usems,
    tsems,
):
    seqs, block, width = x_hbm.shape
    heads = wq_hbm.shape[0] // F
    value = wv_hbm.shape[0] // heads
    tile = block // 2
    quarter = tile // 4
    rows = seqs * block
    tiles = rows // tile
    z = lax.axis_index("seq")
    t = lax.axis_index("tensor")
    core = lax.axis_index("dp")
    side = lax.rem(core, 2)
    mate = {"dp": core + 1 - 2 * side}
    others = [{"seq": lax.rem(z + k, nz)} for k in range(1, nz)]
    down = others[-1]
    near_z, far_z = {"seq": z ^ 1}, {"seq": z ^ 2}
    gain = gain_ref[...].reshape(1, width)
    table = table_ref[...]
    scale = table[2:3, :FEATS]

    def lanes(h, n):
        return pl.ds(h * n, n)

    def x_load(i):
        b, at = i // 2, (i % 2) * tile
        return pltpu.make_async_copy(x_hbm.at[b, pl.ds(at, tile)], xt.at[i % 2], lsems.at[i % 2])

    quarters = [
        pltpu.make_async_copy(
            x_hbm.at[u // 2, rows_at((u % 2) * tile + t * quarter, quarter)], xq.at[u], lsems.at[2 + u]
        )
        for u in range(tiles)
    ]
    tile_loads = []
    for i in range(tiles):
        at = pl.ds(i * tile, tile)
        pair = ((gattn_hbm, gattn_ref), (yx_hbm, yx_ref))
        tile_loads.append(
            [pltpu.make_async_copy(a.at[at], b.at[at], tsems.at[k, i]) for k, (a, b) in enumerate(pair)]
        )
        for c in tile_loads[i]:
            c.start()
    x_load(0).start()
    x_load(1).start()
    weights = [
        pltpu.make_async_copy(src, dst, lsems.at[2 + tiles + i])
        for i, (src, dst) in enumerate(
            (
                (wq_hbm, wqk_ref.at[pl.ds(0, heads * F)]),
                (wk_hbm, wqk_ref.at[pl.ds(heads * F, heads * F)]),
                (wv_hbm, wv_ref),
                (gr_hbm, gr_ref),
            )
        )
    ]
    for c in quarters + weights:
        c.start()
    greet([{"tensor": t ^ k} for k in (1, 2, 3)] + [mate] + others)

    def value_grads(i):
        at = pl.ds(i * tile, tile)
        for c in tile_loads[i]:
            c.wait()
        ga = gattn_ref[at]
        gy = dot(dot(ga, wo_ref[...], NT).astype(BF16), spread_ref[...])
        gat[:, pl.ds(i * tile, tile)] = ga.T
        yb[at] = yx_ref[at].astype(BF16)
        for h in range(heads):
            narrow = lanes(h, LANES)
            g, y = gy[:, h * LANES : (h + 1) * LANES], yx_ref[at, narrow]
            recip = y[:, value : value + 1]
            den = -jnp.sum(g * y, axis=-1, keepdims=True)
            lane = lax.broadcasted_iota(jnp.int32, g.shape, 1)
            gn[at, narrow] = (jnp.where(lane == value, den, g) * recip).astype(BF16)

    def expand(ref, at, h):
        a = dot(ref[at], e1_ref[:, h * WIDE : h * WIDE + FEATS]) + table[0:1, :FEATS]
        b = dot(ref[at], e2_ref[:, h * WIDE : h * WIDE + FEATS]) + table[1:2, :FEATS]
        return a, b

    def states(b):
        flat = pl.ds(b * block, block)
        for h in range(heads):
            a, c = expand(qk_ref, flat, h)
            phi = (a * c * scale).astype(BF16)
            sloc[b * heads + h] = dot(phi, gn[flat, lanes(h, LANES)], TN)

    def send_down(j):
        return pltpu.make_async_remote_copy(
            sout.at[j], suf.at[j], zsems.at[0, j], zsems.at[1, j], device_id=down, device_id_type=MESH
        )

    def chain(b, who):
        for at in who:

            @pl.when(z == nz - 1 - at)
            def _():
                for h in range(heads):
                    j = b * heads + h
                    if at == 0:
                        suf[j] = jnp.zeros((FEATS, LANES), BF16)
                        sout[j] = sloc[j].astype(BF16)
                    else:
                        send_down(j).wait_recv()
                        if at < nz - 1:
                            sout[j] = (sloc[j] + suf[j].astype(F32)).astype(BF16)
                    if at < nz - 1:
                        send_down(j).start()

    def contract(a, c, grad, h, first, second):
        wide = slice(h * WIDE, h * WIDE + FEATS)
        return dot((grad * c).astype(BF16), first[:, wide], NT) + dot(
            (grad * a).astype(BF16), second[:, wide], NT
        )

    def local(b, h):
        narrow = lanes(h, LANES)
        for i in range(2):
            span = (i + 1) * tile
            at = pl.ds(b * block + i * tile, tile)
            until = pl.ds(b * block, span)
            s = dot(head_of(qk_ref[at], h), kq_ref[until], NT)
            w = 1.0 + s * (1.0 / math.sqrt(F))
            row = lax.broadcasted_iota(jnp.int32, w.shape, 0) + i * tile
            col = lax.broadcasted_iota(jnp.int32, w.shape, 1)
            seen = col <= row
            kernel = jnp.where(seen, 0.5 * (w * w) + 0.5, 0.0).astype(BF16)
            grad = gn[at, narrow]
            gs = dot(grad, v_ref[until, narrow], NT) * (w * (1.0 / math.sqrt(F)))
            gs = jnp.where(seen, gs, 0.0).astype(BF16)
            gv[until, narrow] += dot(kernel, grad, TN)
            gqk[until] += dot(gs, head_of(kq_ref[at], heads + h), TN)
            a, c = expand(qk_ref, at, h)
            gphi = dot(grad, pre_ref[b * heads + h], NT) * scale
            gqk[at] += dot(gs, head_of(kq_ref[until], h)) + contract(a, c, gphi, h, e1_ref, e2_ref)

    def state_grads(b, h):
        narrow = lanes(h, LANES)
        flat = pl.ds(b * block, block)
        later = suf[b * heads + h]
        a, c = expand(kq_ref, flat, h)
        gphi = dot(v_ref[flat, narrow], later, NT)
        gqk[flat] += contract(a, c, gphi, h, f1_ref, f2_ref)
        gv[flat, narrow] += dot((a * c).astype(BF16), later)

    def norm_grads(b):
        for i in range(2):
            at = pl.ds(b * block + i * tile, tile)
            gvb[at] = gv[at].astype(BF16)
            gqkb[at] = gqk[at].astype(BF16)
            packed = dot(gvb[at], spread_ref[...], NT).astype(BF16)
            part[at] = (dot(gqkb[at], wqk_ref[...]) + dot(packed, wv_ref[...])).astype(BF16)

    def normed_rows(i):
        x_load(i).wait()
        r = xt[i % 2].astype(F32)
        h1 = r * lax.rsqrt(jnp.mean(r * r, axis=-1, keepdims=True) + 1e-06) * gain
        h1t[:, pl.ds(i * tile, tile)] = h1.astype(BF16).T
        if i + 2 < 2 * seqs:
            x_load(i + 2).start()

    def scatter_of(source, near_ref, far_ref, sems, u):
        return ReduceScatter(
            source.at[pl.ds(u * tile, tile)],
            [near_ref.at[u, k] for k in range(2)],
            [far_ref.at[u, k] for k in range(2)],
            sems.at[u],
        )

    scatters = [scatter_of(part, near, far, rsems, u) for u in range(tiles)]

    def gather_of(source, place, sems, u):
        def piece(k):
            return place.at[u // 2, rows_at((u % 2) * tile + k * quarter, quarter)]

        def half(k, h):
            start = (u % 2) * tile + k * quarter + h * (quarter // 2)
            return place.at[u // 2, rows_at(start, quarter // 2)]

        return RowGather(source.at[u], piece, half, sems.at[u]), piece(t)

    def own_copy(source, place, i, u):
        return pltpu.make_async_copy(source.at[u], place, osems.at[i, u])

    pairs = [gather_of(gq, gt_hbm, asems, u) for u in range(tiles)]
    gathers = [g for g, _ in pairs]
    own_rows = [own_copy(gq, p, 0, u) for u, (_, p) in enumerate(pairs)]
    pairs = [gather_of(block_hbm, bo_hbm, asems2, u) for u in range(tiles)]
    out_gathers = [g for g, _ in pairs]
    own_rows += [own_copy(block_hbm, p, 1, u) for u, (_, p) in enumerate(pairs)]

    gate_loads = [
        pltpu.make_async_copy(src, gload.at[i], hsems.at[i])
        for i, src in enumerate(
            (gsum_hbm.at[1, 2], gland_hbm.at[1, 0], gsum_hbm.at[1, 3], gland_hbm.at[1, 1])
        )
    ]
    gate_out = pltpu.make_async_remote_copy(
        gload.at[0], gfar, fsems.at[0], fsems.at[1], device_id=far_z, device_id_type=MESH
    )
    up_loads = [
        pltpu.make_async_copy(gsum_hbm.at[2, 2 + i], uload.at[i], hsems.at[4 + i]) for i in range(2)
    ]
    up_near = [
        pltpu.make_async_remote_copy(
            gsum_hbm.at[2, k], uland.at[k], usems.at[0, k], usems.at[1, k], device_id=near_z, device_id_type=MESH
        )
        for k in range(2)
    ]
    up_out = pltpu.make_async_remote_copy(
        uload.at[0], ufar, usems.at[0, 2], usems.at[1, 2], device_id=far_z, device_id_type=MESH
    )
    for c in gate_loads + up_loads:
        c.start()

    def pass_up():
        up_near[0].wait_recv()
        up_loads[0].wait()
        uload[0] = (uload[0].astype(F32) + uland[0].astype(F32)).astype(BF16)
        up_out.start()


    half_rows = width // 2
    chunk = half_rows // nz
    spans = [pl.ds(0, heads * LANES), pl.ds(heads * LANES, 2 * heads * F + heads * LANES)]

    def product(p, base):
        at = rows_at(base, half_rows)
        if p == 0:
            return dot(gat[at], yb[...])
        return jnp.concatenate([dot(h1t[at], gqkb[...]), dot(h1t[at], gvb[...])], axis=1)

    def to_mate(p):
        return pltpu.make_async_remote_copy(
            stage.at[:, spans[p]],
            land.at[:, spans[p]],
            msems.at[0, p],
            msems.at[1, p],
            device_id=mate,
            device_id_type=MESH,
        )

    def to_near(p, k):
        return pltpu.make_async_remote_copy(
            total.at[rows_at((z ^ (3, 1)[k]) * chunk, chunk), spans[p]],
            zland.at[k, :, spans[p]],
            dsems.at[0, p, k],
            dsems.at[1, p, k],
            device_id=near_z,
            device_id_type=MESH,
        )

    def to_far(p):
        return pltpu.make_async_remote_copy(
            zsum.at[:, spans[p]],
            zland.at[2, :, spans[p]],
            dsems.at[0, p, 2],
            dsems.at[1, p, 2],
            device_id=far_z,
            device_id_type=MESH,
        )

    def pass_on(p):
        to_near(p, 0).wait_recv()
        mine = total[rows_at((z ^ 2) * chunk, chunk), spans[p]].astype(F32)
        zsum[:, spans[p]] = (mine + zland[0, :, spans[p]].astype(F32)).astype(BF16)
        to_far(p).start()

    def conclude(p):
        to_near(p, 1).wait_recv()
        to_far(p).wait_recv()
        out = total[rows_at(z * chunk, chunk), spans[p]].astype(F32)
        grads_ref[:, spans[p]] = (
            out + zland[1, :, spans[p]].astype(F32) + zland[2, :, spans[p]].astype(F32)
        )
        for k in range(2):
            to_near(p, k).wait_send()
        to_far(p).wait_send()
        to_mate(p).wait_send()

    def send_half(p):
        stage[:, spans[p]] = product(p, (1 - side) * half_rows).astype(BF16)
        to_mate(p).start()

    def sum_half(p):
        out = product(p, side * half_rows)
        to_mate(p).wait_recv()
        total[:, spans[p]] = (out + land[:, spans[p]].astype(F32)).astype(BF16)
        for k in range(2):
            to_near(p, k).start()

    def tokens(b):
        quarters[b].wait()
        grad, gain_grad = norm_backward(xq[b].astype(F32), scatters[b].total(), gain)
        gq[b] = (grad + gr_ref[b]).astype(BF16)
        gathers[b].start()
        own_rows[b].start()
        if b == 0:
            gsend[0] = jnp.concatenate(
                [gain_grad, gains_ref[...], jnp.zeros((6, width), F32)], axis=0
            )
        else:
            gsend[0, 0:1] += gain_grad

    gv[...] = jnp.zeros_like(gv)
    gqk[...] = jnp.zeros_like(gqk)
    mid = list(range(1, nz - 1))
    for g, c in zip(out_gathers, own_rows[tiles:]):
        g.start()
        c.start()

    def send_up_near(here):
        @pl.when(here)
        def _():
            for c in up_near:
                c.start()

    send_up_near(lax.rem(z, 2) == 0)
    value_grads(0)
    value_grads(1)
    states(0)
    chain(0, [0])
    local(0, 0)
    chain(0, mid[:1])
    local(0, 1)
    local(0, 2)
    chain(0, mid[1:])
    local(0, 3)
    for h in range(4, heads):
        local(0, h)
    value_grads(2)
    value_grads(3)
    states(1)
    chain(1, [0])
    send_up_near(z == nz - 1)
    for c in weights + gate_loads:
        c.wait()
    gload[0] = (gload[0].astype(F32) + gload[1].astype(F32)).astype(BF16)
    chain(0, [nz - 1])
    for h in range(heads):
        state_grads(0, h)
    norm_grads(0)
    scatters[0].start()
    scatters[1].start()
    chain(1, mid[:1])
    out_gathers[0].forward()
    out_gathers[1].forward()
    for h in range(heads):
        local(1, h)
        if h == heads // 2 - 1:
            chain(1, mid[1:])
            send_up_near((lax.rem(z, 2) == 1) & (z < nz - 1))
    scatters[0].forward()
    scatters[1].forward()
    chain(1, [nz - 1])
    gate_out.start()
    for h in range(heads):
        state_grads(1, h)
    norm_grads(1)
    scatters[2].start()
    scatters[3].start()
    send_half(0)
    out_gathers[2].forward()
    out_gathers[3].forward()
    pass_up()
    normed_rows(0)
    sum_half(0)
    for i in range(1, 2 * seqs):
        normed_rows(i)
    send_half(1)
    scatters[2].forward()
    scatters[3].forward()
    sum_half(1)
    tokens(0)
    tokens(1)
    tokens(2)
    gathers[0].forward()
    gathers[1].forward()
    tokens(3)

    def gain_copy(i, slot, to):
        return pltpu.make_async_remote_copy(
            gsend.at[i], gland.at[slot], ksems.at[0, slot], ksems.at[1, slot], device_id=to, device_id_type=MESH
        )

    hops = [
        [gain_copy(0, k, {"tensor": t ^ (k + 1)}) for k in range(3)],
        [gain_copy(1, 3, mate)],
        [gain_copy(2, 4 + k, others[k]) for k in range(nz - 1)],
    ]

    def gather_gains(i, first):
        out = gsend[i]
        for k, c in enumerate(hops[i]):
            c.wait()
            out = out + gland[first + k]
        if i < 2:
            gsend[i + 1] = out
            for c in hops[i + 1]:
                c.start()
        else:
            gains_out[...] = out

    for c in hops[0]:
        c.start()
    pass_on(0)
    gathers[2].forward()
    gathers[3].forward()
    gather_gains(0, 0)
    pass_on(1)
    gather_gains(1, 3)
    gate_out.wait()
    gate_ref[...] = gload[2].astype(F32) + gload[3].astype(F32) + gfar[...].astype(F32)
    up_near[1].wait_recv()
    up_out.wait()
    up_loads[1].wait()
    up_ref[...] = uload[1].astype(F32) + uland[1].astype(F32) + ufar[...].astype(F32)
    for c in up_near:
        c.wait_send()
    for p in range(2):
        conclude(p)
    gather_gains(2, 4)
    for c in own_rows:
        c.wait()
    for g in out_gathers + gathers:
        g.finish()
    for c in scatters:
        c.drain()

    @pl.when(z > 0)
    def _():
        for j in range(seqs * heads):
            send_down(j).wait_send()


def run_attention_backward(
    x, gain, qk, kq, v_ext, yx, pre, gattn, wo, wq, wk, wv, gr, gains, block_rows, gsum, gland, tables
):
    seqs, block, width = x.shape
    rows = seqs * block
    heads = wq.shape[0] // F
    tile = block // 2
    tiles, quarter = rows // tile, tile // 4
    nz = lax.axis_size("seq")
    spread, e1, e2, table = tables
    half = heads * F
    f1, f2 = jnp.roll(e1, half, 0), jnp.roll(e2, half, 0)
    chunk = width // 2 // nz
    cols = 2 * heads * LANES + 2 * heads * F
    shapes = [
        jax.ShapeDtypeStruct((chunk, cols), F32),
        jax.ShapeDtypeStruct((8, width), F32),
        jax.ShapeDtypeStruct(gsum.shape[2:], F32),
        jax.ShapeDtypeStruct(gsum.shape[2:], F32),
        jax.ShapeDtypeStruct(x.shape, BF16),
        jax.ShapeDtypeStruct(x.shape, BF16),
    ]
    vm, dma = pltpu.VMEM, pltpu.SemaphoreType.DMA
    wide = heads * LANES
    scratch = [
        vm((2 * half, width), BF16),
        vm(wv.shape, BF16),
        vm((tiles, quarter, width), F32),
        vm((rows, width), BF16),
        vm((rows, wide), F32),
        vm((rows, wide), BF16),
        vm((rows, wide), F32),
        vm((rows, wide), BF16),
        vm((rows, 2 * half), F32),
        vm((rows, 2 * half), BF16),
        vm((rows, wide), BF16),
        vm((width, rows), BF16),
        vm((width, rows), BF16),
        vm((seqs * heads, FEATS, LANES), F32),
        vm((seqs * heads, FEATS, LANES), BF16),
        vm((seqs * heads, FEATS, LANES), BF16),
        vm((2, tile, width), BF16),
        vm((tiles, quarter, width), BF16),
        vm((rows, width), BF16),
        vm((tiles, 2, quarter // 2, width), BF16),
        vm((tiles, 2, quarter, width), BF16),
        vm((tiles, quarter, width), BF16),
        vm((width // 2, cols), BF16),
        vm((width // 2, cols), BF16),
        vm((width // 2, cols), BF16),
        vm((3, chunk, cols), BF16),
        vm((chunk, cols), BF16),
        vm((4, 8, width), F32),
        vm((4 + nz - 1, 8, width), F32),
        vm((4,) + gsum.shape[2:], BF16),
        vm(gsum.shape[2:], BF16),
        vm((2,) + gsum.shape[2:], BF16),
        vm((2,) + gsum.shape[2:], BF16),
        vm(gsum.shape[2:], BF16),
        dma((6 + tiles,)),
        dma((2, seqs * heads)),
        dma((tiles, 2, 4)),
        dma((tiles, 2, 4)),
        dma((2, 2)),
        dma((2, 2, 3)),
        dma((2, 4 + nz - 1)),
        dma((tiles, 2, 4)),
        dma((2, tiles)),
        dma((6,)),
        dma((2,)),
        dma((2, 3)),
        dma((2, tiles)),
    ]
    return pl.pallas_call(
        functools.partial(attention_backward, nz),
        out_shape=shapes,
        in_specs=[ANY_SPEC] + [VMEM_SPEC] * 4 + [ANY_SPEC, VMEM_SPEC] * 2 + [ANY_SPEC] * 4 + [VMEM_SPEC] + [ANY_SPEC] * 3 + [VMEM_SPEC] * 6,
        out_specs=[VMEM_SPEC] * 4 + [ANY_SPEC] * 2,
        scratch_shapes=scratch,
        compiler_params=pltpu.CompilerParams(
            collective_id=2, has_side_effects=True, vmem_limit_bytes=VMEM_LIMIT
        ),
        cost_estimate=pl.CostEstimate(
            flops=8 * rows * width * wide, bytes_accessed=30 << 20, transcendentals=0
        ),
        name="attention_backward",
    )(
        x,
        gain,
        qk,
        kq,
        v_ext,
        yx,
        pre,
        gattn,
        wo,
        wq,
        wk,
        wv,
        gr,
        gains,
        block_rows,
        gsum,
        gland,
        spread,
        e1,
        e2,
        f1,
        f2,
        table,
    )


def finish_kernel(gt_ref, bo_ref, *refs):
    count = len(refs) // 2 - 1
    gt_out, bo_out = refs[count : count + 2]
    gt_out[...] = gt_ref[...].astype(F32)
    bo_out[...] = bo_ref[...]
    for src, dst in zip(refs[:count], refs[count + 2 :]):
        dst[...] = src[...]


def finish(gt, bo, *grads):
    seqs, block, width = gt.shape
    steps = 8
    step = seqs * block // steps
    share, ff = grads[0].shape
    piece = next(p for p in range(8, share + 1, 8) if share % p == 0 and share // p <= steps)
    last = share // piece - 1
    rows = pl.BlockSpec((step, width), lambda i: (i, 0))
    small = pl.BlockSpec((piece, ff), lambda i: (jnp.minimum(i, last), 0))
    shape = jax.ShapeDtypeStruct
    gt, bo, *grads = pl.pallas_call(
        finish_kernel,
        grid=(steps,),
        out_shape=[shape((seqs * block, width), F32), shape((seqs * block, width), BF16)]
        + [shape(g.shape, F32) for g in grads],
        in_specs=[rows] * 2 + [small] * len(grads),
        out_specs=[rows] * 2 + [small] * len(grads),
        cost_estimate=pl.CostEstimate(flops=0, bytes_accessed=25 << 20, transcendentals=0),
        name="finish",
    )(gt.reshape(-1, width), bo.reshape(-1, width), *grads)
    return gt.reshape(seqs, block, width), bo.reshape(seqs, block, width), *grads


def shards(
    tokens,
    lengths,
    attn_gain,
    w_query,
    w_key,
    w_value,
    w_output,
    mlp_gain,
    w_gate,
    w_up,
    w_down,
    cotangent,
):
    seqs, block, width = tokens.shape
    heads = w_query.shape[1] // F
    value = w_value.shape[1] // heads
    chips = lax.axis_size("dp") // 2
    tables = (spread_table(heads, value),) + feature_tables(heads)
    wq, wk, wv = w_query.T, w_key.T, w_value.T
    qk, kq, pre, v_ext, yx, y, gh, gmt, yall, woall = run_attention_forward(
        tokens, attn_gain, wq, wk, wv, w_output, cotangent, w_down, lengths, tables
    )
    mlp_gain_grad, down_grads, block_rows, gr, gattn, gsum, _, gland = run_mlp(
        tokens, y, yall, w_output, woall, w_gate, w_up, w_down, gh, gmt, cotangent, mlp_gain, lengths
    )
    attn_grads, gains, gate_grads, up_grads, grad_tokens, block_out = run_attention_backward(
        tokens,
        attn_gain,
        qk,
        kq,
        v_ext,
        yx,
        pre,
        gattn,
        w_output,
        wq,
        wk,
        wv,
        gr,
        mlp_gain_grad,
        block_rows,
        gsum,
        gland,
        tables,
    )
    if chips > 1:
        nz = lax.axis_size("seq")
        pairs = [[2 * i, 2 * i + 1] for i in range(chips)]

        def respread(a):
            a = lax.all_gather(a.astype(BF16), "seq", axis=0, tiled=True)
            a = lax.all_gather(a, "dp", axis=0, tiled=True, axis_index_groups=pairs)
            a = (a.astype(F32) * (0.5 / nz)).astype(BF16)
            return lax.psum_scatter(a, ("dp", "seq"), scatter_dimension=0, tiled=True).astype(F32)

        attn_grads, down_grads, gate_grads, up_grads = [
            respread(a) for a in (attn_grads, down_grads, gate_grads, up_grads)
        ]
        gains = lax.psum(gains, "dp") * 0.5
    grad_tokens, block_out, gate_grads, up_grads, down_grads = finish(
        grad_tokens, block_out, gate_grads, up_grads, down_grads
    )
    share = width // (lax.axis_size("dp") * lax.axis_size("seq"))
    place = (lax.axis_index("dp") * lax.axis_size("seq") + lax.axis_index("seq")) * share
    gains = lax.dynamic_slice_in_dim(gains, place, share, 1)

    def unspread(a):
        return a.reshape(share, heads, LANES)[:, :, :value].reshape(share, heads * value)

    edge, half = heads * LANES, heads * F
    return (
        block_out,
        grad_tokens,
        gains[0],
        attn_grads[:, edge : edge + half],
        attn_grads[:, edge + half : edge + 2 * half],
        unspread(attn_grads[:, edge + 2 * half :]),
        unspread(attn_grads[:, :edge]).T,
        gains[1],
        gate_grads,
        up_grads,
        down_grads.T,
    )


def solution(mesh):
    in_specs = (
        P("dp", "seq", None),
        P("dp"),
        P(),
        P(None, "tensor"),
        P(None, "tensor"),
        P(None, "tensor"),
        P("tensor", None),
        P(),
        P(None, "tensor"),
        P(None, "tensor"),
        P("tensor", None),
        P("dp", "seq", None),
    )
    out_specs = (
        P("dp", "seq", None),
        P("dp", "seq", None),
        P(("dp", "seq")),
        P(("dp", "seq"), "tensor"),
        P(("dp", "seq"), "tensor"),
        P(("dp", "seq"), "tensor"),
        P("tensor", ("dp", "seq")),
        P(("dp", "seq")),
        P(("dp", "seq"), "tensor"),
        P(("dp", "seq"), "tensor"),
        P("tensor", ("dp", "seq")),
    )
    return jax.shard_map(shards, mesh=mesh, in_specs=in_specs, out_specs=out_specs, check_vma=False)
```

```python
import functools
import math

import jax
import jax.numpy as jnp
import numpy as np
from jax import lax
from jax.experimental import pallas as pl
from jax.experimental.pallas import tpu as pltpu
from jax.sharding import PartitionSpec as P

F = 16
FEATS = 160
LANES = 128
WIDE = 256
VMEM_LIMIT = 62 << 20
MESH = pl.DeviceIdType.MESH
BF16 = jnp.bfloat16
F32 = jnp.float32
VMEM_SPEC = pl.BlockSpec(memory_space=pltpu.VMEM)
ANY_SPEC = pl.BlockSpec(memory_space=pl.ANY)
NN = (((1,), (0,)), ((), ()))
NT = (((1,), (1,)), ((), ()))
TN = (((0,), (0,)), ((), ()))


def dot(a, b, dims=NN):
    return lax.dot_general(a, b, dims, preferred_element_type=F32)


def feature_tables(heads):
    upper_i, upper_j = np.triu_indices(F)
    pairs = len(upper_i)
    first = np.zeros((2 * heads * F, heads * WIDE), np.float32)
    second = np.zeros_like(first)
    rows = np.zeros((8, WIDE), np.float32)
    cols = np.arange(pairs)
    for h in range(heads):
        first[h * F + upper_i, h * WIDE + cols] = 1.0
        second[h * F + upper_j, h * WIDE + cols] = 1.0
        first[h * F + np.arange(F), h * WIDE + pairs + np.arange(F)] = 1.0
    rows[0, pairs + F] = 1.0
    rows[1, pairs : pairs + F + 1] = 1.0
    rows[2, :pairs] = np.where(upper_i == upper_j, 1.0 / (2 * F), 1.0 / F)
    rows[2, pairs : pairs + F] = 1.0 / math.sqrt(F)
    rows[2, pairs + F] = 1.0
    return tuple(jnp.asarray(a, BF16) for a in (first, second)) + (jnp.asarray(rows),)


def spread_table(heads, width):
    table = np.zeros((heads * width, heads * LANES), np.float32)
    for h in range(heads):
        table[h * width + np.arange(width), h * LANES + np.arange(width)] = 1.0
    return jnp.asarray(table, BF16)


def rows_at(start, count):
    return pl.ds(pl.multiple_of(start, 16), count)


class Gather:
    def __init__(self, source, slots, sems, half):
        me = lax.axis_index("tensor")
        self.x, self.y = {"tensor": me ^ 1}, {"tensor": me ^ 2}
        self.source, self.slots, self.sems, self.half = source, slots, sems, half
        self.first = [
            self.copy(source, slots(0), 0, self.x),
            self.copy(source, slots(1), 1, self.y),
        ]
        self.second = [
            self.copy(half(slots(0), 0), half(slots(2), 0), 2, self.y),
            self.copy(half(slots(1), 1), half(slots(2), 1), 3, self.x),
        ]

    def copy(self, src, dst, i, to):
        return pltpu.make_async_remote_copy(
            src, dst, self.sems.at[0, i], self.sems.at[1, i], device_id=to, device_id_type=MESH
        )

    def start(self):
        for c in self.first:
            c.start()

    def forward(self):
        for c, d in zip(self.first, self.second):
            c.wait_recv()
            d.start()

    def arrive(self):
        for d in self.second:
            d.wait_recv()

    def leave(self):
        for c in self.first + self.second:
            c.wait_send()

    def finish(self):
        self.arrive()
        self.leave()


def greet(devices):
    barrier = pltpu.get_barrier_semaphore()
    for d in devices:
        pl.semaphore_signal(barrier, inc=1, device_id=d, device_id_type=MESH)
    pl.semaphore_wait(barrier, len(devices))


def features(rows, first, second, table, scaled):
    a = dot(rows, first) + table[0:1]
    b = dot(rows, second) + table[1:2]
    out = a * b
    return out * table[2:3] if scaled else out


def head_of(rows, h):
    lane = lax.broadcasted_iota(jnp.int32, rows.shape, 1)
    return jnp.where(lane // F == h, rows, jnp.zeros_like(rows))


def attention_forward(
    nz,
    x_hbm,
    gain_ref,
    wq_hbm,
    wk_hbm,
    wv_ref,
    wo_ref,
    cot_hbm,
    wd_hbm,
    len_ref,
    spread_ref,
    e1_ref,
    e2_ref,
    table_ref,
    qk_ref,
    kq_ref,
    pre_ref,
    v_hbm,
    yx_hbm,
    y_hbm,
    gh_hbm,
    gmt_hbm,
    yall_ref,
    woall_ref,
    wqk_ref,
    x_ref,
    cot_ref,
    wd_ref,
    v_ref,
    yx_ref,
    y_ref,
    gh_ref,
    gmt_ref,
    sloc,
    pout,
    gsems,
    wsems,
    csems,
    zsems,
    lsems,
    osems,
):
    seqs, block, width = x_hbm.shape
    heads = wq_hbm.shape[0] // F
    value = wv_ref.shape[0] // heads
    z = lax.axis_index("seq")
    t = lax.axis_index("tensor")
    core = lax.axis_index("dp")
    side = lax.rem(core, 2)
    mate = {"dp": core + 1 - 2 * side}
    up, down = {"seq": lax.rem(z + 1, nz)}, {"seq": lax.rem(z + nz - 1, nz)}

    tile = block // 2
    x_loads = [
        pltpu.make_async_copy(
            x_hbm.at[i // 2, pl.ds((i % 2) * tile, tile)],
            x_ref.at[i // 2, pl.ds((i % 2) * tile, tile)],
            lsems.at[i],
        )
        for i in range(2 * seqs)
    ]
    late = [
        pltpu.make_async_copy(cot_hbm, cot_ref, lsems.at[2 * seqs]),
        pltpu.make_async_copy(wd_hbm, wd_ref, lsems.at[2 * seqs + 1]),
    ]
    half = heads * F
    joins = [
        pltpu.make_async_copy(w, wqk_ref.at[pl.ds(i * half, half)], lsems.at[2 * seqs + 2 + i])
        for i, w in enumerate((wq_hbm, wk_hbm))
    ]
    for c in joins + x_loads + late:
        c.start()
    greet([{"tensor": t ^ 1}, {"tensor": t ^ 2}, mate, up, down])

    wrows = wo_ref.shape[0] // 4
    cut = wrows // 32 * 16 + 16
    zbit = lax.rem(z, 2)

    def part(s, zb):
        return woall_ref.at[s, rows_at((2 * side + zb) * wrows, wrows)]

    wo = Gather(
        wo_ref.at[rows_at((2 * side + zbit) * wrows, wrows)],
        lambda s: part(s, zbit),
        wsems,
        lambda ref, i: ref.at[pl.ds(0, cut)] if i == 0 else ref.at[pl.ds(cut, wrows - cut)],
    )
    wo.start()

    def share(s, i):
        ref = part(s, zbit if i < 2 else 1 - zbit)
        to = {"seq": z ^ 1} if i == 1 else mate
        return pltpu.make_async_remote_copy(
            ref, ref, csems.at[0, 3 * i + s], csems.at[1, 3 * i + s], device_id=to, device_id_type=MESH
        )

    gain = gain_ref[...].reshape(1, width)
    def share_near(here):
        @pl.when(here)
        def _():
            for s in range(2):
                share(s, 1).start()

    table = table_ref[...]
    ones = jnp.where(
        lax.rem(lax.broadcasted_iota(jnp.int32, (1, heads * LANES), 1), LANES) == value, 1.0, 0.0
    )
    def project(b, i):
        at = pl.ds(i * tile, tile)
        flat = pl.ds(b * block + i * tile, tile)
        x_loads[2 * b + i].wait()
        rows = x_ref[b, at].astype(F32)
        normed = rows * lax.rsqrt(jnp.mean(rows * rows, axis=-1, keepdims=True) + 1e-06)
        normed = (normed * gain).astype(BF16)
        qk = dot(normed, wqk_ref[...], NT)
        qk_ref[flat] = qk.astype(BF16)
        kq_ref[flat] = pltpu.roll(qk, heads * F, 1).astype(BF16)
        values = dot(normed, wv_ref[...], NT).astype(BF16)
        v_ref[flat] = (dot(values, spread_ref[...]) + ones).astype(BF16)

    def lanes(h, n):
        return pl.ds(h * n, n)

    def states(b):
        flat = pl.ds(b * block, block)
        for h in range(heads):
            wide = lanes(h, WIDE)
            phi = features(kq_ref[flat], e1_ref[:, wide], e2_ref[:, wide], table, False)
            s = dot(phi.astype(BF16), v_ref[flat, lanes(h, LANES)], TN)
            sloc[b * heads + h] = s[:FEATS]

    def send_up(j):
        return pltpu.make_async_remote_copy(
            pout.at[j],
            pre_ref.at[j],
            zsems.at[0, j],
            zsems.at[1, j],
            device_id=up,
            device_id_type=MESH,
        )

    def chain(b, who):
        for at in who:

            @pl.when(z == at)
            def _():
                for h in range(heads):
                    j = b * heads + h
                    if at == 0:
                        pre_ref[j] = jnp.zeros((FEATS, LANES), BF16)
                        pout[j] = sloc[j].astype(BF16)
                    else:
                        send_up(j).wait_recv()
                        if at < nz - 1:
                            pout[j] = (sloc[j] + pre_ref[j].astype(F32)).astype(BF16)
                    if at < nz - 1:
                        send_up(j).start()

    def attend(b, h):
        narrow = lanes(h, LANES)
        wide = lanes(h, WIDE)
        for i in range(2):
            span = (i + 1) * tile
            at = pl.ds(b * block + i * tile, tile)
            until = pl.ds(b * block, span)
            rows = qk_ref[at]
            s = dot(head_of(rows, h), kq_ref[until], NT)
            w = 1.0 + s * (1.0 / math.sqrt(F))
            w = 0.5 * (w * w) + 0.5
            row = lax.broadcasted_iota(jnp.int32, w.shape, 0) + i * tile
            col = lax.broadcasted_iota(jnp.int32, w.shape, 1)
            w = jnp.where(col <= row, w, 0.0).astype(BF16)
            num = dot(w, v_ref[until, narrow])
            phi = features(rows, e1_ref[:, wide], e2_ref[:, wide], table, True)
            num = num + dot(phi[:, :FEATS].astype(BF16), pre_ref[b * heads + h])
            recip = 1.0 / num[:, value : value + 1]
            lane = lax.broadcasted_iota(jnp.int32, num.shape, 1)
            yx_ref[at, narrow] = jnp.where(lane == value, recip, num * recip)

    def gather(b):
        flat = pl.ds(b * block, block)
        return Gather(
            y_ref.at[flat],
            lambda s: yall_ref.at[s, flat],
            gsems.at[b],
            lambda ref, i: ref.at[pl.ds(i * tile, tile)],
        )

    def pack(b):
        for i in range(2):
            at = pl.ds(b * block + i * tile, tile)
            y_ref[at] = dot(yx_ref[at].astype(BF16), spread_ref[...], NT).astype(BF16)

    def put(src, dst, i):
        return pltpu.make_async_copy(src, dst, osems.at[i])

    def hidden_outs(i):
        at = pl.ds(i * tile, tile)
        return [
            put(gh_ref.at[at], gh_hbm.at[at], 2 * i),
            put(gmt_ref.at[:, at], gmt_hbm.at[:, at], 2 * i + 1),
        ]

    first_out = 4 * seqs
    outs = [
        put(v_ref, v_hbm, first_out),
        put(yx_ref, yx_hbm, first_out + 1),
        put(y_ref, y_hbm, first_out + 2),
    ]

    def hidden_grads(i):
        b, local = i // 2, i % 2
        at = z * block + local * tile + lax.broadcasted_iota(jnp.int32, (tile, 1), 0)
        mask = (at < len_ref[b]).astype(F32)
        gm = (cot_ref[b, pl.ds(local * tile, tile)].astype(F32) * mask).astype(BF16)
        gmt_ref[:, pl.ds(i * tile, tile)] = gm.T
        gh_ref[pl.ds(i * tile, tile)] = dot(gm, wd_ref[...], NT).astype(BF16)
        for c in hidden_outs(i):
            c.start()

    gathers = [gather(b) for b in range(seqs)]
    mid = list(range(1, nz - 1))
    for c in joins:
        c.wait()
    for b in range(seqs + 1):
        if b < seqs:
            for i in range(2):
                project(b, i)
                if b > 0 and i == 0:
                    chain(b - 1, mid[:1])
            if b > 0:
                chain(b - 1, mid[1:])
                wo.forward()
                for s in range(2):
                    share(s, 0).start()
                share_near(zbit == 1)
            states(b)
            chain(b, [0])
        if b > 0:
            chain(b - 1, [nz - 1])
            for h in range(heads):
                attend(b - 1, h)
                if b == seqs - 1:
                    chain(b, mid[h : h + 1] if h < heads - 1 else mid[h:])
                    if h == min(len(mid), heads) - 1:
                        share_near(zbit == 0)
            pack(b - 1)
            gathers[b - 1].start()
    for c in outs:
        c.start()
    wo.arrive()
    share(2, 0).start()
    share(2, 1).start()
    for c in late:
        c.wait()
    hidden_grads(0)
    gathers[0].forward()
    for i in range(1, 2 * seqs):
        hidden_grads(i)
    for g in gathers[1:]:
        g.forward()
    for s in range(2):
        share(s, 1).wait_recv()
        share(s, 2).start()
    share(2, 1).wait_recv()
    share(2, 2).start()
    for c in outs:
        c.wait()
    for i in range(2 * seqs):
        for c in hidden_outs(i):
            c.wait()
    wo.leave()
    for g in gathers:
        g.finish()
    for s in range(3):
        share(s, 0).wait()
        share(s, 1).wait_send()
        share(s, 2).wait()

    @pl.when(z < nz - 1)
    def _():
        for j in range(seqs * heads):
            send_up(j).wait_send()


def run_attention_forward(x, gain, wq, wk, wv, wo, cot, wd, lengths, tables):
    seqs, block, width = x.shape
    heads = wq.shape[0] // F
    value = wv.shape[0] // heads
    rows = seqs * block
    spread, e1, e2, table = tables
    shape = jax.ShapeDtypeStruct
    wide, ff = heads * LANES, wd.shape[0]
    shapes = [
        shape((rows, 2 * heads * F), BF16),
        shape((rows, 2 * heads * F), BF16),
        shape((seqs * heads, FEATS, LANES), BF16),
        shape((rows, wide), BF16),
        shape((rows, wide), F32),
        shape((rows, heads * value), BF16),
        shape((rows, ff), BF16),
        shape((width, rows), BF16),
        shape((3, rows, heads * value), BF16),
        shape((3,) + wo.shape, BF16),
    ]
    vm, dma = pltpu.VMEM, pltpu.SemaphoreType.DMA
    smem = pl.BlockSpec(memory_space=pltpu.SMEM)
    return pl.pallas_call(
        functools.partial(attention_forward, lax.axis_size("seq")),
        out_shape=shapes,
        in_specs=[ANY_SPEC, VMEM_SPEC] + [ANY_SPEC] * 2 + [VMEM_SPEC] + [ANY_SPEC] * 3 + [smem] + [VMEM_SPEC] * 4,
        out_specs=[VMEM_SPEC] * 3 + [ANY_SPEC] * 7,
        scratch_shapes=[
            vm((2 * heads * F, width), BF16),
            vm(x.shape, BF16),
            vm(x.shape, BF16),
            vm(wd.shape, BF16),
            vm((rows, wide), BF16),
            vm((rows, wide), F32),
            vm((rows, heads * value), BF16),
            vm((rows, ff), BF16),
            vm((width, rows), BF16),
            vm((seqs * heads, FEATS, LANES), F32),
            vm((seqs * heads, FEATS, LANES), BF16),
            dma((seqs, 2, 4)),
            dma((2, 4)),
            dma((2, 9)),
            dma((2, seqs * heads)),
            dma((2 * seqs + 4,)),
            dma((4 * seqs + 3,)),
        ],
        compiler_params=pltpu.CompilerParams(
            collective_id=0, has_side_effects=True, vmem_limit_bytes=VMEM_LIMIT
        ),
        cost_estimate=pl.CostEstimate(
            flops=2 * rows * width * heads * (2 * F + value), bytes_accessed=20 << 20, transcendentals=0
        ),
        name="attention_forward",
    )(x, gain, wq, wk, wv, wo, cot, wd, lengths, spread, e1, e2, table)


class Exchange:
    def __init__(self, sems):
        me = lax.axis_index("tensor")
        self.x, self.y = {"tensor": me ^ 1}, {"tensor": me ^ 2}
        self.sems = sems

    def copy(self, src, dst, i, to):
        return pltpu.make_async_remote_copy(
            src, dst, self.sems.at[0, i], self.sems.at[1, i], device_id=to, device_id_type=MESH
        )


class ReduceScatter(Exchange):
    def __init__(self, part, near, far, sems):
        super().__init__(sems)
        me = lax.axis_index("tensor")
        self.part, self.near, self.far = part, near, far
        self.q = q = near[0].shape[0] * 2
        self.half = q // 2
        self.at = [me * q, (me ^ 1) * q, (me ^ 2) * q, (me ^ 3) * q]
        over = self.at[3]
        self.first = [
            self.copy(part.at[rows_at(over, self.half)], near[0], 0, self.x),
            self.copy(part.at[rows_at(over + self.half, self.half)], near[1], 1, self.y),
        ]
        self.second = [
            self.copy(part.at[rows_at(self.at[2], q)], far[1], 2, self.y),
            self.copy(part.at[rows_at(self.at[1], q)], far[0], 3, self.x),
        ]

    def start(self):
        for c in self.first:
            c.start()

    def forward(self):
        for i, start in ((0, self.at[2]), (1, self.at[1] + self.half)):
            self.first[i].wait_recv()
            rows = rows_at(start, self.half)
            self.part[rows] = (self.part[rows].astype(F32) + self.near[i][...].astype(F32)).astype(BF16)
            self.second[i].start()

    def total(self):
        for c in self.second:
            c.wait_recv()
        mine = self.part[rows_at(self.at[0], self.q)].astype(F32)
        return mine + self.far[0][...].astype(F32) + self.far[1][...].astype(F32)

    def drain(self):
        for c in self.first + self.second:
            c.wait_send()


class RowGather(Exchange):
    def __init__(self, source, piece, half, sems):
        super().__init__(sems)
        me = lax.axis_index("tensor")
        self.first = [
            self.copy(source, piece(me), 0, self.x),
            self.copy(source, piece(me), 1, self.y),
        ]
        self.second = [
            self.copy(half(me ^ 1, 0), half(me ^ 1, 0), 2, self.y),
            self.copy(half(me ^ 2, 1), half(me ^ 2, 1), 3, self.x),
        ]

    start = Gather.start
    forward = Gather.forward
    arrive = Gather.arrive
    leave = Gather.leave
    finish = Gather.finish


def norm_backward(rows, grad, gain):
    norm = lax.rsqrt(jnp.mean(rows * rows, axis=-1, keepdims=True) + 1e-06)
    unit = rows * norm
    gain_grad = jnp.sum(grad * unit, axis=0, keepdims=True)
    scaled = grad * gain
    mean = jnp.mean(scaled * unit, axis=-1, keepdims=True)
    return norm * (scaled - unit * mean), gain_grad


def own_rows(value, t, count):
    parts = [value[i * count : (i + 1) * count] for i in range(4)]
    low = jnp.where(t == 0, parts[0], parts[1])
    return jnp.where(t < 2, low, jnp.where(t == 2, parts[2], parts[3]))


def mlp_kernel(
    nz,
    x_hbm,
    y_hbm,
    yall_hbm,
    wo_hbm,
    woall_hbm,
    wg_hbm,
    wu_hbm,
    wd_hbm,
    gh_hbm,
    gmt_hbm,
    cot_hbm,
    gain_ref,
    len_ref,
    gain_grad_ref,
    down_ref,
    block_hbm,
    gr_hbm,
    gattn_hbm,
    gsum_hbm,
    land_hbm,
    zland_hbm,
    wo4,
    wg,
    wu,
    wd,
    xt,
    yt,
    ght,
    h2t,
    gmt,
    gg,
    gu,
    hid,
    part,
    near,
    far,
    ga,
    r_ref,
    grs,
    stage,
    back,
    keep,
    lsems,
    rsems,
    asems,
    msems,
    bsems,
    dsems,
    osems,
    psems,
    free_sem,
):
    seqs, block, width = x_hbm.shape
    tile = xt.shape[0]
    per = block // tile
    quarter = tile // 4
    tiles = seqs * per
    z = lax.axis_index("seq")
    t = lax.axis_index("tensor")
    core = lax.axis_index("dp")
    side = lax.rem(core, 2)
    mate = {"dp": core + 1 - 2 * side}
    near_z, far_z = {"seq": z ^ 1}, {"seq": z ^ 2}
    gain = gain_ref[...].reshape(1, width)

    def load(src, dst, i):
        return pltpu.make_async_copy(src, dst, lsems.at[i])

    weights = [
        load(wo_hbm, wo4.at[0], 0),
        *[load(woall_hbm.at[s], wo4.at[s + 1], 1 + s) for s in range(3)],
        load(wg_hbm, wg, 4),
        load(wu_hbm, wu, 5),
    ]
    late = [load(gmt_hbm, gmt, 6), load(wd_hbm, wd, 7)]

    def xy_loads(i):
        b, at = i // per, lax.rem(i, per) * tile
        flat = rows_at(i * tile, tile)
        return [
            load(x_hbm.at[b, rows_at(at, tile)], xt, 8),
            load(y_hbm.at[flat], yt.at[0], 9),
            *[load(yall_hbm.at[s, flat], yt.at[s + 1], 10 + s) for s in range(3)],
        ]

    def g_load(i):
        return load(gh_hbm.at[rows_at(i * tile, tile)], ght, 13)

    def c_load(i):
        b, at = i // per, lax.rem(i, per) * tile + t * quarter
        return load(cot_hbm.at[b, rows_at(at, quarter)], ga.at[i], 14 + i)

    for c in xy_loads(0) + weights + [g_load(0)] + [c_load(i) for i in range(tiles)] + late:
        c.start()
    greet([{"tensor": t ^ 1}, {"tensor": t ^ 2}, mate, near_z, far_z])

    def scatter(i):
        return ReduceScatter(
            part.at[rows_at(i * tile, tile)],
            [near.at[i, k] for k in range(2)],
            [far.at[i, k] for k in range(2)],
            rsems.at[i],
        )

    def mlp_scatter(i):
        source = wo4.at[i, pl.ds(0, tile)]
        near_ref = [wo4.at[i, pl.ds(tile + k * (quarter // 2), quarter // 2)] for k in range(2)]
        far_ref = [wo4.at[i, pl.ds(tile + (k + 1) * quarter, quarter)] for k in range(2)]
        return ReduceScatter(source, near_ref, far_ref, psems.at[i])

    def gather(i):
        def piece(k):
            return gattn_hbm.at[rows_at(i * tile + k * quarter, quarter)]

        def half(k, h):
            start = i * tile + k * quarter + h * (quarter // 2)
            return gattn_hbm.at[rows_at(start, quarter // 2)]

        return RowGather(ga.at[i], piece, half, asems.at[i])

    def place(i):
        at = rows_at(i * tile + t * quarter, quarter)
        return [
            pltpu.make_async_copy(ga.at[i], gattn_hbm.at[at], osems.at[0, i]),
            pltpu.make_async_copy(grs, gr_hbm.at[i], osems.at[1, i]),
        ]

    def tile_step(i, first):
        flat = rows_at(i * tile, tile)
        for c in xy_loads(i):
            c.wait()
        if first:
            for c in weights[:4]:
                c.wait()
        r = xt[...].astype(F32)
        for s in range(4):
            r = r + dot(yt[s], wo4[s])

        @pl.when(i + 1 < tiles)
        def _():
            for c in xy_loads(i + 1):
                c.start()

        r_ref[i] = own_rows(r, t, quarter)
        h2 = r * lax.rsqrt(jnp.mean(r * r, axis=-1, keepdims=True) + 1e-06) * gain
        h2 = h2.astype(BF16)
        h2t[:, pl.ds(pl.multiple_of(i * tile, LANES), tile)] = h2.T
        if first:
            for c in weights[4:6]:
                c.wait()
        gate = dot(h2, wg[...], NT)
        up = dot(h2, wu[...], NT)
        if not first:
            scatter(i - 1).forward()
        g_load(i).wait()
        gh = ght[...].astype(F32)
        sig = 1.0 / (1.0 + jnp.exp(-gate))
        silu = gate * sig
        hid[flat] = (silu * up).astype(BF16)
        gg[flat] = (gh * up * (sig * (1.0 + gate * (1.0 - sig)))).astype(BF16)
        gu[flat] = (gh * silu).astype(BF16)

        @pl.when(i + 1 < tiles)
        def _():
            g_load(i + 1).start()

        part[flat] = (dot(gg[flat], wg[...]) + dot(gu[flat], wu[...])).astype(BF16)
        scatter(i).start()

    def mixed(i, first):
        b = i // per
        grad = scatter(i).total()
        c_load(i).wait()
        at = z * block + lax.rem(i, per) * tile + t * quarter
        at = at + lax.broadcasted_iota(jnp.int32, (quarter, 1), 0)
        out = ga[i].astype(F32) * (at < len_ref[b]).astype(F32)
        gr, gain_grad = norm_backward(r_ref[i], grad, gain)
        gr = gr + out
        if first:
            gain_grad_ref[...] = gain_grad
        else:
            gain_grad_ref[...] += gain_grad
            place(i - 1)[1].wait()
        grs[...] = gr
        ga[i] = gr.astype(BF16)
        gather(i).start()
        for c in place(i):
            c.start()

    tile_step(0, True)

    def rest(i, carry):
        tile_step(i, False)
        return carry

    lax.fori_loop(1, tiles - 1, rest, 0)
    mixed(0, True)
    tile_step(tiles - 1, False)

    lefts = (gmt, h2t, h2t)
    rights = (hid, gg, gu)
    half_rows = width // 2
    chunk = back.shape[0]
    last = tiles - 1

    def product(n, base, m):
        return dot(lefts[n][rows_at(base + m * chunk, chunk)], rights[n][...])

    def to_mate(n, m, slot):
        return pltpu.make_async_remote_copy(
            stage.at[slot],
            land_hbm.at[n, m],
            msems.at[0, slot],
            msems.at[1, n * nz + m],
            device_id=mate,
            device_id_type=MESH,
        )

    def from_mate(n, m):
        return pltpu.make_async_copy(land_hbm.at[n, m], back, bsems.at[0])

    def to_sum(n, m, slot):
        return pltpu.make_async_copy(stage.at[slot], gsum_hbm.at[n, m], bsems.at[slot - 1])

    across = [
        pltpu.make_async_remote_copy(
            gsum_hbm.at[n, k],
            zland_hbm.at[n, k],
            dsems.at[0, 2 * n + k],
            dsems.at[1, 2 * n + k],
            device_id=near_z,
            device_id_type=MESH,
        )
        for n in range(2)
        for k in range(2)
    ]
    beyond = pltpu.make_async_remote_copy(
        keep, zland_hbm.at[0, 2], dsems.at[0, 4], dsems.at[1, 4], device_id=far_z, device_id_type=MESH
    )

    def landed(k):
        c = pltpu.make_async_copy(zland_hbm.at[0, k], back, bsems.at[0])
        c.start()
        c.wait()
        return back[...].astype(F32)

    def pass_on():
        across[0].wait_recv()
        keep[...] = (keep[...].astype(F32) + landed(0)).astype(BF16)
        beyond.start()

    def step_mlp(i):
        flat = rows_at(i * tile, tile)
        wo4[i, :tile] = dot(hid[flat], wd[...]).astype(BF16)
        mlp_scatter(i).start()

    def block_out(i):
        return pltpu.make_async_copy(ga.at[i], block_hbm.at[i], osems.at[0, i])

    def block_rows(i):
        b = i // per
        at = z * block + lax.rem(i, per) * tile + t * quarter
        at = at + lax.broadcasted_iota(jnp.int32, (quarter, 1), 0)
        mask = (at < len_ref[b]).astype(F32)
        ga[i] = (mask * (r_ref[i] + mlp_scatter(i).total())).astype(BF16)
        block_out(i).start()

    for to in ({"tensor": t ^ 1}, {"tensor": t ^ 2}):
        pl.semaphore_signal(free_sem, inc=1, device_id=to, device_id_type=MESH)
    late[0].wait()
    late[1].wait()
    steps = {
        2: lambda: (gather(0).forward(), mixed(1, False)),
        3: lambda: scatter(last).forward(),
        4: lambda: (mixed(last - 1, False), pl.semaphore_wait(free_sem, 2)),
        5: lambda: step_mlp(0),
        6: lambda: step_mlp(1),
        7: lambda: step_mlp(2),
        8: lambda: step_mlp(3),
        9: lambda: gather(1).forward(),
        11: lambda: mixed(last, False),
        13: lambda: gather(last - 1).forward(),
        16: lambda: mlp_scatter(0).forward(),
        17: lambda: (gather(last).forward(), mlp_scatter(1).forward()),
        18: lambda: mlp_scatter(2).forward(),
        19: lambda: mlp_scatter(3).forward(),
    }
    count = 0

    def step():
        nonlocal count
        steps.get(count, lambda: None)()
        count += 1

    order = [z ^ 3, z ^ 1, z ^ 2, z]
    for n in range(3):

        def for_mate(k):
            if k >= 2:
                to_mate(n, order[k - 2], k % 2).wait_send()
            stage[k % 2] = product(n, (1 - side) * half_rows, order[k]).astype(BF16)
            to_mate(n, order[k], k % 2).start()
            step()

        def for_own(k):
            m = order[k]
            to_mate(n, m, 0).wait_recv()
            from_mate(n, m).start()
            out = product(n, side * half_rows, m)
            from_mate(n, m).wait()
            out = out + back[...].astype(F32)
            if n == 0 and k == 2:
                keep[...] = out.astype(BF16)
            elif n == 0 and k == 3:
                down_ref[...] = out
            else:
                if k > 0 and (n == 2 or k == 3):
                    to_sum(n, k - 1, 2).wait()
                stage[2] = out.astype(BF16)
                to_sum(n, k, 2).start()
            if n < 2 and k < 2:
                to_sum(n, k, 2).wait()
                across[2 * n + k].start()
            step()

        for_mate(0)
        for_mate(1)
        for_own(0)
        for_mate(2)
        for_own(1)
        for_mate(3)
        for_own(2)
        for_own(3)
        for k in range(nz - 2, nz):
            to_mate(n, order[k], k % 2).wait_send()
        if n > 0:
            to_sum(n, nz - 1, 2).wait()
        if n == 1:
            pass_on()
    across[1].wait_recv()
    down_ref[...] += landed(1)
    place(last)[1].wait()
    for i in range(tiles):
        place(i)[0].wait()
        gather(i).finish()
        scatter(i).drain()
    for c in across:
        c.wait_send()
    for i in range(tiles):
        block_rows(i)
        mlp_scatter(i).drain()
    for i in range(tiles):
        block_out(i).wait()
    for c in across[2:]:
        c.wait_recv()
    beyond.wait_recv()
    down_ref[...] += landed(2)
    beyond.wait_send()


def run_mlp(x, y, yall, wo, woall, wg, wu, wd, gh, gmt, cot, gain, lengths):
    seqs, block, width = x.shape
    rows = seqs * block
    nz = lax.axis_size("seq")
    value, ff = wo.shape[0], wd.shape[0]
    tile = block // 2
    tiles, quarter = rows // tile, tile // 4
    chunk = width // 2 // nz
    shape = jax.ShapeDtypeStruct
    shapes = [
        shape((1, width), F32),
        shape((chunk, ff), F32),
        shape((tiles, quarter, width), BF16),
        shape((tiles, quarter, width), F32),
        shape((rows, width), BF16),
        shape((3, 4, chunk, ff), BF16),
        shape((3, nz, chunk, ff), BF16),
        shape((2, 3, chunk, ff), BF16),
    ]
    vm, dma = pltpu.VMEM, pltpu.SemaphoreType.DMA
    scratch = [
        vm((4, value, width), BF16),
        vm((ff, width), BF16),
        vm((ff, width), BF16),
        vm((ff, width), BF16),
        vm((tile, width), BF16),
        vm((4, tile, value), BF16),
        vm((tile, ff), BF16),
        vm((width, rows), BF16),
        vm((width, rows), BF16),
        vm((rows, ff), BF16),
        vm((rows, ff), BF16),
        vm((rows, ff), BF16),
        vm((rows, width), BF16),
        vm((tiles, 2, quarter // 2, width), BF16),
        vm((tiles, 2, quarter, width), BF16),
        vm((tiles, quarter, width), BF16),
        vm((tiles, quarter, width), F32),
        vm((quarter, width), F32),
        vm((3, chunk, ff), BF16),
        vm((chunk, ff), BF16),
        vm((chunk, ff), BF16),
        dma((14 + tiles,)),
        dma((tiles, 2, 4)),
        dma((tiles, 2, 4)),
        dma((2, 3 * nz)),
        dma((3,)),
        dma((2, 5)),
        dma((2, tiles)),
        dma((tiles, 2, 4)),
        pltpu.SemaphoreType.REGULAR,
    ]
    return pl.pallas_call(
        functools.partial(mlp_kernel, nz),
        out_shape=shapes,
        in_specs=[ANY_SPEC] * 11 + [VMEM_SPEC, pl.BlockSpec(memory_space=pltpu.SMEM)],
        out_specs=[VMEM_SPEC] * 2 + [ANY_SPEC] * 6,
        scratch_shapes=scratch,
        compiler_params=pltpu.CompilerParams(
            collective_id=1, has_side_effects=True, vmem_limit_bytes=VMEM_LIMIT
        ),
        cost_estimate=pl.CostEstimate(
            flops=2 * rows * width * (4 * value + 8 * ff), bytes_accessed=60 << 20, transcendentals=0
        ),
        name="mlp_forward_backward",
    )(x, y, yall, wo, woall, wg.T, wu.T, wd, gh, gmt, cot, gain, lengths)


def attention_backward(
    nz,
    x_hbm,
    gain_ref,
    qk_ref,
    kq_ref,
    v_ref,
    yx_hbm,
    pre_ref,
    gattn_hbm,
    wo_ref,
    wq_hbm,
    wk_hbm,
    wv_hbm,
    gr_hbm,
    gains_ref,
    block_hbm,
    gsum_hbm,
    gland_hbm,
    spread_ref,
    e1_ref,
    e2_ref,
    f1_ref,
    f2_ref,
    table_ref,
    grads_ref,
    gains_out,
    gate_ref,
    up_ref,
    gt_hbm,
    bo_hbm,
    wqk_ref,
    wv_ref,
    gr_ref,
    gattn_ref,
    yx_ref,
    gn,
    gv,
    gvb,
    gqk,
    gqkb,
    yb,
    gat,
    h1t,
    sloc,
    sout,
    suf,
    xt,
    xq,
    part,
    near,
    far,
    gq,
    stage,
    land,
    total,
    zland,
    zsum,
    gsend,
    gland,
    gload,
    gfar,
    uload,
    uland,
    ufar,
    lsems,
    zsems,
    rsems,
    asems,
    msems,
    dsems,
    ksems,
    asems2,
    osems,
    hsems,
    fsems,
    usems,
    tsems,
):
    seqs, block, width = x_hbm.shape
    heads = wq_hbm.shape[0] // F
    value = wv_hbm.shape[0] // heads
    tile = block // 2
    quarter = tile // 4
    rows = seqs * block
    tiles = rows // tile
    z = lax.axis_index("seq")
    t = lax.axis_index("tensor")
    core = lax.axis_index("dp")
    side = lax.rem(core, 2)
    mate = {"dp": core + 1 - 2 * side}
    others = [{"seq": lax.rem(z + k, nz)} for k in range(1, nz)]
    down = others[-1]
    near_z, far_z = {"seq": z ^ 1}, {"seq": z ^ 2}
    gain = gain_ref[...].reshape(1, width)
    table = table_ref[...]
    scale = table[2:3, :FEATS]

    def lanes(h, n):
        return pl.ds(h * n, n)

    def x_load(i):
        b, at = i // 2, (i % 2) * tile
        return pltpu.make_async_copy(x_hbm.at[b, pl.ds(at, tile)], xt.at[i % 2], lsems.at[i % 2])

    quarters = [
        pltpu.make_async_copy(
            x_hbm.at[u // 2, rows_at((u % 2) * tile + t * quarter, quarter)], xq.at[u], lsems.at[2 + u]
        )
        for u in range(tiles)
    ]
    tile_loads = []
    for i in range(tiles):
        at = pl.ds(i * tile, tile)
        pair = ((gattn_hbm, gattn_ref), (yx_hbm, yx_ref))
        tile_loads.append(
            [pltpu.make_async_copy(a.at[at], b.at[at], tsems.at[k, i]) for k, (a, b) in enumerate(pair)]
        )
        for c in tile_loads[i]:
            c.start()
    x_load(0).start()
    x_load(1).start()
    weights = [
        pltpu.make_async_copy(src, dst, lsems.at[2 + tiles + i])
        for i, (src, dst) in enumerate(
            (
                (wq_hbm, wqk_ref.at[pl.ds(0, heads * F)]),
                (wk_hbm, wqk_ref.at[pl.ds(heads * F, heads * F)]),
                (wv_hbm, wv_ref),
                (gr_hbm, gr_ref),
            )
        )
    ]
    for c in quarters + weights:
        c.start()
    greet([{"tensor": t ^ k} for k in (1, 2, 3)] + [mate] + others)

    def value_grads(i):
        at = pl.ds(i * tile, tile)
        for c in tile_loads[i]:
            c.wait()
        ga = gattn_ref[at]
        gy = dot(dot(ga, wo_ref[...], NT).astype(BF16), spread_ref[...])
        gat[:, pl.ds(i * tile, tile)] = ga.T
        yb[at] = yx_ref[at].astype(BF16)
        for h in range(heads):
            narrow = lanes(h, LANES)
            g, y = gy[:, h * LANES : (h + 1) * LANES], yx_ref[at, narrow]
            recip = y[:, value : value + 1]
            den = -jnp.sum(g * y, axis=-1, keepdims=True)
            lane = lax.broadcasted_iota(jnp.int32, g.shape, 1)
            gn[at, narrow] = (jnp.where(lane == value, den, g) * recip).astype(BF16)

    def expand(ref, at, h):
        a = dot(ref[at], e1_ref[:, h * WIDE : h * WIDE + FEATS]) + table[0:1, :FEATS]
        b = dot(ref[at], e2_ref[:, h * WIDE : h * WIDE + FEATS]) + table[1:2, :FEATS]
        return a, b

    def states(b):
        flat = pl.ds(b * block, block)
        for h in range(heads):
            a, c = expand(qk_ref, flat, h)
            phi = (a * c * scale).astype(BF16)
            sloc[b * heads + h] = dot(phi, gn[flat, lanes(h, LANES)], TN)

    def send_down(j):
        return pltpu.make_async_remote_copy(
            sout.at[j], suf.at[j], zsems.at[0, j], zsems.at[1, j], device_id=down, device_id_type=MESH
        )

    def chain(b, who):
        for at in who:

            @pl.when(z == nz - 1 - at)
            def _():
                for h in range(heads):
                    j = b * heads + h
                    if at == 0:
                        suf[j] = jnp.zeros((FEATS, LANES), BF16)
                        sout[j] = sloc[j].astype(BF16)
                    else:
                        send_down(j).wait_recv()
                        if at < nz - 1:
                            sout[j] = (sloc[j] + suf[j].astype(F32)).astype(BF16)
                    if at < nz - 1:
                        send_down(j).start()

    def contract(a, c, grad, h, first, second):
        wide = slice(h * WIDE, h * WIDE + FEATS)
        return dot((grad * c).astype(BF16), first[:, wide], NT) + dot(
            (grad * a).astype(BF16), second[:, wide], NT
        )

    def local(b, h):
        narrow = lanes(h, LANES)
        for i in range(2):
            span = (i + 1) * tile
            at = pl.ds(b * block + i * tile, tile)
            until = pl.ds(b * block, span)
            s = dot(head_of(qk_ref[at], h), kq_ref[until], NT)
            w = 1.0 + s * (1.0 / math.sqrt(F))
            row = lax.broadcasted_iota(jnp.int32, w.shape, 0) + i * tile
            col = lax.broadcasted_iota(jnp.int32, w.shape, 1)
            seen = col <= row
            kernel = jnp.where(seen, 0.5 * (w * w) + 0.5, 0.0).astype(BF16)
            grad = gn[at, narrow]
            gs = dot(grad, v_ref[until, narrow], NT) * (w * (1.0 / math.sqrt(F)))
            gs = jnp.where(seen, gs, 0.0).astype(BF16)
            gv[until, narrow] += dot(kernel, grad, TN)
            gqk[until] += dot(gs, head_of(kq_ref[at], heads + h), TN)
            a, c = expand(qk_ref, at, h)
            gphi = dot(grad, pre_ref[b * heads + h], NT) * scale
            gqk[at] += dot(gs, head_of(kq_ref[until], h)) + contract(a, c, gphi, h, e1_ref, e2_ref)

    def state_grads(b, h):
        narrow = lanes(h, LANES)
        flat = pl.ds(b * block, block)
        later = suf[b * heads + h]
        a, c = expand(kq_ref, flat, h)
        gphi = dot(v_ref[flat, narrow], later, NT)
        gqk[flat] += contract(a, c, gphi, h, f1_ref, f2_ref)
        gv[flat, narrow] += dot((a * c).astype(BF16), later)

    def norm_grads(b):
        for i in range(2):
            at = pl.ds(b * block + i * tile, tile)
            gvb[at] = gv[at].astype(BF16)
            gqkb[at] = gqk[at].astype(BF16)
            packed = dot(gvb[at], spread_ref[...], NT).astype(BF16)
            part[at] = (dot(gqkb[at], wqk_ref[...]) + dot(packed, wv_ref[...])).astype(BF16)

    def normed_rows(i):
        x_load(i).wait()
        r = xt[i % 2].astype(F32)
        h1 = r * lax.rsqrt(jnp.mean(r * r, axis=-1, keepdims=True) + 1e-06) * gain
        h1t[:, pl.ds(i * tile, tile)] = h1.astype(BF16).T
        if i + 2 < 2 * seqs:
            x_load(i + 2).start()

    def scatter_of(source, near_ref, far_ref, sems, u):
        return ReduceScatter(
            source.at[pl.ds(u * tile, tile)],
            [near_ref.at[u, k] for k in range(2)],
            [far_ref.at[u, k] for k in range(2)],
            sems.at[u],
        )

    scatters = [scatter_of(part, near, far, rsems, u) for u in range(tiles)]

    def gather_of(source, place, sems, u):
        def piece(k):
            return place.at[u // 2, rows_at((u % 2) * tile + k * quarter, quarter)]

        def half(k, h):
            start = (u % 2) * tile + k * quarter + h * (quarter // 2)
            return place.at[u // 2, rows_at(start, quarter // 2)]

        return RowGather(source.at[u], piece, half, sems.at[u]), piece(t)

    def own_copy(source, place, i, u):
        return pltpu.make_async_copy(source.at[u], place, osems.at[i, u])

    pairs = [gather_of(gq, gt_hbm, asems, u) for u in range(tiles)]
    gathers = [g for g, _ in pairs]
    own_rows = [own_copy(gq, p, 0, u) for u, (_, p) in enumerate(pairs)]
    pairs = [gather_of(block_hbm, bo_hbm, asems2, u) for u in range(tiles)]
    out_gathers = [g for g, _ in pairs]
    own_rows += [own_copy(block_hbm, p, 1, u) for u, (_, p) in enumerate(pairs)]

    gate_loads = [
        pltpu.make_async_copy(src, gload.at[i], hsems.at[i])
        for i, src in enumerate(
            (gsum_hbm.at[1, 2], gland_hbm.at[1, 0], gsum_hbm.at[1, 3], gland_hbm.at[1, 1])
        )
    ]
    gate_out = pltpu.make_async_remote_copy(
        gload.at[0], gfar, fsems.at[0], fsems.at[1], device_id=far_z, device_id_type=MESH
    )
    up_loads = [
        pltpu.make_async_copy(gsum_hbm.at[2, 2 + i], uload.at[i], hsems.at[4 + i]) for i in range(2)
    ]
    up_near = [
        pltpu.make_async_remote_copy(
            gsum_hbm.at[2, k], uland.at[k], usems.at[0, k], usems.at[1, k], device_id=near_z, device_id_type=MESH
        )
        for k in range(2)
    ]
    up_out = pltpu.make_async_remote_copy(
        uload.at[0], ufar, usems.at[0, 2], usems.at[1, 2], device_id=far_z, device_id_type=MESH
    )
    for c in gate_loads + up_loads:
        c.start()

    def pass_up():
        up_near[0].wait_recv()
        up_loads[0].wait()
        uload[0] = (uload[0].astype(F32) + uland[0].astype(F32)).astype(BF16)
        up_out.start()


    half_rows = width // 2
    chunk = half_rows // nz
    spans = [pl.ds(0, heads * LANES), pl.ds(heads * LANES, 2 * heads * F + heads * LANES)]

    def product(p, base):
        at = rows_at(base, half_rows)
        if p == 0:
            return dot(gat[at], yb[...])
        return jnp.concatenate([dot(h1t[at], gqkb[...]), dot(h1t[at], gvb[...])], axis=1)

    def to_mate(p):
        return pltpu.make_async_remote_copy(
            stage.at[:, spans[p]],
            land.at[:, spans[p]],
            msems.at[0, p],
            msems.at[1, p],
            device_id=mate,
            device_id_type=MESH,
        )

    def to_near(p, k):
        return pltpu.make_async_remote_copy(
            total.at[rows_at((z ^ (3, 1)[k]) * chunk, chunk), spans[p]],
            zland.at[k, :, spans[p]],
            dsems.at[0, p, k],
            dsems.at[1, p, k],
            device_id=near_z,
            device_id_type=MESH,
        )

    def to_far(p):
        return pltpu.make_async_remote_copy(
            zsum.at[:, spans[p]],
            zland.at[2, :, spans[p]],
            dsems.at[0, p, 2],
            dsems.at[1, p, 2],
            device_id=far_z,
            device_id_type=MESH,
        )

    def pass_on(p):
        to_near(p, 0).wait_recv()
        mine = total[rows_at((z ^ 2) * chunk, chunk), spans[p]].astype(F32)
        zsum[:, spans[p]] = (mine + zland[0, :, spans[p]].astype(F32)).astype(BF16)
        to_far(p).start()

    def conclude(p):
        to_near(p, 1).wait_recv()
        to_far(p).wait_recv()
        out = total[rows_at(z * chunk, chunk), spans[p]].astype(F32)
        grads_ref[:, spans[p]] = (
            out + zland[1, :, spans[p]].astype(F32) + zland[2, :, spans[p]].astype(F32)
        )
        for k in range(2):
            to_near(p, k).wait_send()
        to_far(p).wait_send()
        to_mate(p).wait_send()

    def send_half(p):
        stage[:, spans[p]] = product(p, (1 - side) * half_rows).astype(BF16)
        to_mate(p).start()

    def sum_half(p):
        out = product(p, side * half_rows)
        to_mate(p).wait_recv()
        total[:, spans[p]] = (out + land[:, spans[p]].astype(F32)).astype(BF16)
        for k in range(2):
            to_near(p, k).start()

    def tokens(b):
        quarters[b].wait()
        grad, gain_grad = norm_backward(xq[b].astype(F32), scatters[b].total(), gain)
        gq[b] = (grad + gr_ref[b]).astype(BF16)
        gathers[b].start()
        own_rows[b].start()
        if b == 0:
            gsend[0] = jnp.concatenate(
                [gain_grad, gains_ref[...], jnp.zeros((6, width), F32)], axis=0
            )
        else:
            gsend[0, 0:1] += gain_grad

    gv[...] = jnp.zeros_like(gv)
    gqk[...] = jnp.zeros_like(gqk)
    mid = list(range(1, nz - 1))
    for g, c in zip(out_gathers, own_rows[tiles:]):
        g.start()
        c.start()

    def send_up_near(here):
        @pl.when(here)
        def _():
            for c in up_near:
                c.start()

    send_up_near(lax.rem(z, 2) == 0)
    value_grads(0)
    value_grads(1)
    states(0)
    chain(0, [0])
    local(0, 0)
    chain(0, mid[:1])
    local(0, 1)
    local(0, 2)
    chain(0, mid[1:])
    local(0, 3)
    for h in range(4, heads):
        local(0, h)
    value_grads(2)
    value_grads(3)
    states(1)
    chain(1, [0])
    send_up_near(z == nz - 1)
    for c in weights + gate_loads:
        c.wait()
    gload[0] = (gload[0].astype(F32) + gload[1].astype(F32)).astype(BF16)
    chain(0, [nz - 1])
    for h in range(heads):
        state_grads(0, h)
    norm_grads(0)
    scatters[0].start()
    scatters[1].start()
    chain(1, mid[:1])
    out_gathers[0].forward()
    out_gathers[1].forward()
    for h in range(heads):
        local(1, h)
        if h == heads // 2 - 1:
            chain(1, mid[1:])
            send_up_near((lax.rem(z, 2) == 1) & (z < nz - 1))
    scatters[0].forward()
    scatters[1].forward()
    chain(1, [nz - 1])
    gate_out.start()
    for h in range(heads):
        state_grads(1, h)
    norm_grads(1)
    scatters[2].start()
    scatters[3].start()
    send_half(0)
    out_gathers[2].forward()
    out_gathers[3].forward()
    pass_up()
    normed_rows(0)
    sum_half(0)
    for i in range(1, 2 * seqs):
        normed_rows(i)
    send_half(1)
    scatters[2].forward()
    scatters[3].forward()
    sum_half(1)
    tokens(0)
    tokens(1)
    tokens(2)
    gathers[0].forward()
    gathers[1].forward()
    tokens(3)

    def gain_copy(i, slot, to):
        return pltpu.make_async_remote_copy(
            gsend.at[i], gland.at[slot], ksems.at[0, slot], ksems.at[1, slot], device_id=to, device_id_type=MESH
        )

    hops = [
        [gain_copy(0, k, {"tensor": t ^ (k + 1)}) for k in range(3)],
        [gain_copy(1, 3, mate)],
        [gain_copy(2, 4 + k, others[k]) for k in range(nz - 1)],
    ]

    def gather_gains(i, first):
        out = gsend[i]
        for k, c in enumerate(hops[i]):
            c.wait()
            out = out + gland[first + k]
        if i < 2:
            gsend[i + 1] = out
            for c in hops[i + 1]:
                c.start()
        else:
            gains_out[...] = out

    for c in hops[0]:
        c.start()
    pass_on(0)
    gathers[2].forward()
    gathers[3].forward()
    gather_gains(0, 0)
    pass_on(1)
    gather_gains(1, 3)
    gate_out.wait()
    gate_ref[...] = gload[2].astype(F32) + gload[3].astype(F32) + gfar[...].astype(F32)
    up_near[1].wait_recv()
    up_out.wait()
    up_loads[1].wait()
    up_ref[...] = uload[1].astype(F32) + uland[1].astype(F32) + ufar[...].astype(F32)
    for c in up_near:
        c.wait_send()
    for p in range(2):
        conclude(p)
    gather_gains(2, 4)
    for c in own_rows:
        c.wait()
    for g in out_gathers + gathers:
        g.finish()
    for c in scatters:
        c.drain()

    @pl.when(z > 0)
    def _():
        for j in range(seqs * heads):
            send_down(j).wait_send()


def run_attention_backward(
    x, gain, qk, kq, v_ext, yx, pre, gattn, wo, wq, wk, wv, gr, gains, block_rows, gsum, gland, tables
):
    seqs, block, width = x.shape
    rows = seqs * block
    heads = wq.shape[0] // F
    tile = block // 2
    tiles, quarter = rows // tile, tile // 4
    nz = lax.axis_size("seq")
    spread, e1, e2, table = tables
    half = heads * F
    f1, f2 = jnp.roll(e1, half, 0), jnp.roll(e2, half, 0)
    chunk = width // 2 // nz
    cols = 2 * heads * LANES + 2 * heads * F
    shapes = [
        jax.ShapeDtypeStruct((chunk, cols), F32),
        jax.ShapeDtypeStruct((8, width), F32),
        jax.ShapeDtypeStruct(gsum.shape[2:], F32),
        jax.ShapeDtypeStruct(gsum.shape[2:], F32),
        jax.ShapeDtypeStruct(x.shape, BF16),
        jax.ShapeDtypeStruct(x.shape, BF16),
    ]
    vm, dma = pltpu.VMEM, pltpu.SemaphoreType.DMA
    wide = heads * LANES
    scratch = [
        vm((2 * half, width), BF16),
        vm(wv.shape, BF16),
        vm((tiles, quarter, width), F32),
        vm((rows, width), BF16),
        vm((rows, wide), F32),
        vm((rows, wide), BF16),
        vm((rows, wide), F32),
        vm((rows, wide), BF16),
        vm((rows, 2 * half), F32),
        vm((rows, 2 * half), BF16),
        vm((rows, wide), BF16),
        vm((width, rows), BF16),
        vm((width, rows), BF16),
        vm((seqs * heads, FEATS, LANES), F32),
        vm((seqs * heads, FEATS, LANES), BF16),
        vm((seqs * heads, FEATS, LANES), BF16),
        vm((2, tile, width), BF16),
        vm((tiles, quarter, width), BF16),
        vm((rows, width), BF16),
        vm((tiles, 2, quarter // 2, width), BF16),
        vm((tiles, 2, quarter, width), BF16),
        vm((tiles, quarter, width), BF16),
        vm((width // 2, cols), BF16),
        vm((width // 2, cols), BF16),
        vm((width // 2, cols), BF16),
        vm((3, chunk, cols), BF16),
        vm((chunk, cols), BF16),
        vm((4, 8, width), F32),
        vm((4 + nz - 1, 8, width), F32),
        vm((4,) + gsum.shape[2:], BF16),
        vm(gsum.shape[2:], BF16),
        vm((2,) + gsum.shape[2:], BF16),
        vm((2,) + gsum.shape[2:], BF16),
        vm(gsum.shape[2:], BF16),
        dma((6 + tiles,)),
        dma((2, seqs * heads)),
        dma((tiles, 2, 4)),
        dma((tiles, 2, 4)),
        dma((2, 2)),
        dma((2, 2, 3)),
        dma((2, 4 + nz - 1)),
        dma((tiles, 2, 4)),
        dma((2, tiles)),
        dma((6,)),
        dma((2,)),
        dma((2, 3)),
        dma((2, tiles)),
    ]
    return pl.pallas_call(
        functools.partial(attention_backward, nz),
        out_shape=shapes,
        in_specs=[ANY_SPEC] + [VMEM_SPEC] * 4 + [ANY_SPEC, VMEM_SPEC] * 2 + [ANY_SPEC] * 4 + [VMEM_SPEC] + [ANY_SPEC] * 3 + [VMEM_SPEC] * 6,
        out_specs=[VMEM_SPEC] * 4 + [ANY_SPEC] * 2,
        scratch_shapes=scratch,
        compiler_params=pltpu.CompilerParams(
            collective_id=2, has_side_effects=True, vmem_limit_bytes=VMEM_LIMIT
        ),
        cost_estimate=pl.CostEstimate(
            flops=8 * rows * width * wide, bytes_accessed=30 << 20, transcendentals=0
        ),
        name="attention_backward",
    )(
        x,
        gain,
        qk,
        kq,
        v_ext,
        yx,
        pre,
        gattn,
        wo,
        wq,
        wk,
        wv,
        gr,
        gains,
        block_rows,
        gsum,
        gland,
        spread,
        e1,
        e2,
        f1,
        f2,
        table,
    )


def finish_kernel(gt_ref, bo_ref, *refs):
    count = len(refs) // 2 - 1
    gt_out, bo_out = refs[count : count + 2]
    gt_out[...] = gt_ref[...].astype(F32)
    bo_out[...] = bo_ref[...]
    for src, dst in zip(refs[:count], refs[count + 2 :]):
        dst[...] = src[...]


def finish(gt, bo, *grads):
    seqs, block, width = gt.shape
    steps = 4
    step = seqs * block // steps
    share, ff = grads[0].shape
    piece = next(p for p in range(8, share + 1, 8) if share % p == 0 and share // p <= steps)
    last = share // piece - 1
    rows = pl.BlockSpec((step, width), lambda i: (i, 0))
    small = pl.BlockSpec((piece, ff), lambda i: (jnp.minimum(i, last), 0))
    shape = jax.ShapeDtypeStruct
    gt, bo, *grads = pl.pallas_call(
        finish_kernel,
        grid=(steps,),
        out_shape=[shape((seqs * block, width), F32), shape((seqs * block, width), BF16)]
        + [shape(g.shape, F32) for g in grads],
        in_specs=[rows] * 2 + [small] * len(grads),
        out_specs=[rows] * 2 + [small] * len(grads),
        cost_estimate=pl.CostEstimate(flops=0, bytes_accessed=25 << 20, transcendentals=0),
        name="finish",
    )(gt.reshape(-1, width), bo.reshape(-1, width), *grads)
    return gt.reshape(seqs, block, width), bo.reshape(seqs, block, width), *grads


def shards(
    tokens,
    lengths,
    attn_gain,
    w_query,
    w_key,
    w_value,
    w_output,
    mlp_gain,
    w_gate,
    w_up,
    w_down,
    cotangent,
):
    seqs, block, width = tokens.shape
    heads = w_query.shape[1] // F
    value = w_value.shape[1] // heads
    chips = lax.axis_size("dp") // 2
    tables = (spread_table(heads, value),) + feature_tables(heads)
    wq, wk, wv = w_query.T, w_key.T, w_value.T
    qk, kq, pre, v_ext, yx, y, gh, gmt, yall, woall = run_attention_forward(
        tokens, attn_gain, wq, wk, wv, w_output, cotangent, w_down, lengths, tables
    )
    mlp_gain_grad, down_grads, block_rows, gr, gattn, gsum, _, gland = run_mlp(
        tokens, y, yall, w_output, woall, w_gate, w_up, w_down, gh, gmt, cotangent, mlp_gain, lengths
    )
    attn_grads, gains, gate_grads, up_grads, grad_tokens, block_out = run_attention_backward(
        tokens,
        attn_gain,
        qk,
        kq,
        v_ext,
        yx,
        pre,
        gattn,
        w_output,
        wq,
        wk,
        wv,
        gr,
        mlp_gain_grad,
        block_rows,
        gsum,
        gland,
        tables,
    )
    if chips > 1:
        nz = lax.axis_size("seq")
        pairs = [[2 * i, 2 * i + 1] for i in range(chips)]

        def respread(a):
            a = lax.all_gather(a.astype(BF16), "seq", axis=0, tiled=True)
            a = lax.all_gather(a, "dp", axis=0, tiled=True, axis_index_groups=pairs)
            a = (a.astype(F32) * (0.5 / nz)).astype(BF16)
            return lax.psum_scatter(a, ("dp", "seq"), scatter_dimension=0, tiled=True).astype(F32)

        attn_grads, down_grads, gate_grads, up_grads = [
            respread(a) for a in (attn_grads, down_grads, gate_grads, up_grads)
        ]
        gains = lax.psum(gains, "dp") * 0.5
    grad_tokens, block_out, gate_grads, up_grads, down_grads = finish(
        grad_tokens, block_out, gate_grads, up_grads, down_grads
    )
    share = width // (lax.axis_size("dp") * lax.axis_size("seq"))
    place = (lax.axis_index("dp") * lax.axis_size("seq") + lax.axis_index("seq")) * share
    gains = lax.dynamic_slice_in_dim(gains, place, share, 1)

    def unspread(a):
        return a.reshape(share, heads, LANES)[:, :, :value].reshape(share, heads * value)

    edge, half = heads * LANES, heads * F
    return (
        block_out,
        grad_tokens,
        gains[0],
        attn_grads[:, edge : edge + half],
        attn_grads[:, edge + half : edge + 2 * half],
        unspread(attn_grads[:, edge + 2 * half :]),
        unspread(attn_grads[:, :edge]).T,
        gains[1],
        gate_grads,
        up_grads,
        down_grads.T,
    )


def solution(mesh):
    in_specs = (
        P("dp", "seq", None),
        P("dp"),
        P(),
        P(None, "tensor"),
        P(None, "tensor"),
        P(None, "tensor"),
        P("tensor", None),
        P(),
        P(None, "tensor"),
        P(None, "tensor"),
        P("tensor", None),
        P("dp", "seq", None),
    )
    out_specs = (
        P("dp", "seq", None),
        P("dp", "seq", None),
        P(("dp", "seq")),
        P(("dp", "seq"), "tensor"),
        P(("dp", "seq"), "tensor"),
        P(("dp", "seq"), "tensor"),
        P("tensor", ("dp", "seq")),
        P(("dp", "seq")),
        P(("dp", "seq"), "tensor"),
        P(("dp", "seq"), "tensor"),
        P("tensor", ("dp", "seq")),
    )
    return jax.shard_map(shards, mesh=mesh, in_specs=in_specs, out_specs=out_specs, check_vma=False)
```
